32 devices in a mesh: shard: 2 (over y), ctx: 4 (over z), tp: 4 (over x, core).
Axes of the slice: x: 2, y: 2, z: 4, core: 2. Of those that a mesh axis runs over, the one named last changes fastest.
Arguments:
- prompt_x: bfloat16 [4, 1024, 1024], P('shard', 'ctx'), may hold values from -6 to 6
- cont_x: bfloat16 [32, 128, 1024], P(('shard', 'ctx')), may hold values from -6 to 6
- owner: int32 [32], P(('shard', 'ctx')), may hold values from 0 to 3, as said below
- w_query: bfloat16 [1024, 1024], P('shard', 'tp'), may hold values from -0.1875 to 0.1875
- w_key: bfloat16 [1024, 1024], P('shard', 'tp'), may hold values from -0.1875 to 0.1875
- w_value: bfloat16 [1024, 1024], P('shard', 'tp'), may hold values from -0.1875 to 0.1875
- w_out: bfloat16 [1024, 1024], P('tp', 'shard'), may hold values from -0.1875 to 0.1875
- w_up: bfloat16 [1024, 4096], P('shard', 'tp'), may hold values from -0.1875 to 0.1875
- w_down: bfloat16 [4096, 1024], P('tp', 'shard'), may hold values from -0.09375 to 0.09375
- ln_gain: bfloat16 [4, 1024], P(None, 'shard'), may hold values from 0.099609375 to 1.8984375
- ln_bias: bfloat16 [4, 1024], P(None, 'shard'), may hold values from -3 to 3
- prompt_grad: bfloat16 [4, 1024, 1024], P('shard', 'ctx'), may hold values from -6 to 6
- cont_grad: bfloat16 [32, 128, 1024], P(('shard', 'ctx')), may hold values from -6 to 6
Outputs:
- prompt_out: bfloat16 [4, 1024, 1024], P('shard', 'ctx')
- cont_out: bfloat16 [32, 128, 1024], P(('shard', 'ctx'))
- prompt_dx: bfloat16 [4, 1024, 1024], P('shard', 'ctx')
- cont_dx: bfloat16 [32, 128, 1024], P(('shard', 'ctx'))
- grad_query: float32 [1024, 1024], P('shard', 'tp')
- grad_key: float32 [1024, 1024], P('shard', 'tp')
- grad_value: float32 [1024, 1024], P('shard', 'tp')
- grad_out: float32 [1024, 1024], P('tp', 'shard')
- grad_up: float32 [1024, 4096], P('shard', 'tp')
- grad_down: float32 [4096, 1024], P('tp', 'shard')
- grad_gain: float32 [4, 1024], P(None, 'shard')
- grad_bias: float32 [4, 1024], P(None, 'shard')
The draws below stay inside these ranges and needn't reach their ends.
Inputs may be any that keep to these rules, and one draw needn't show every extreme that they name: owner[n] lies on continuation n's index of shard: owner[n] // 2 == n // 16; every group is named by exactly 8 continuations.
All inputs are finite; a program needn't handle non-finite values.
Results may differ from the reference program's by a relative error of at most 0.018.
Values may be sent and summed in bfloat16 or wider, within the bound.
No kernel may reach another device: no remote copies, remote signals or barrier semaphores. Data moves between devices by JAX's collectives and lax.ppermute only.
A program may use at most 192 MiB of HBM per device.

```python
import jax
import jax.numpy as jnp
from jax import lax

D = 1024
HEADS = 16
HEAD_DIM = 64
FF = 4096
PROMPT = 1024
CONT_LEN = 128
K_CONT = 8
G_DEV = 2
GROUPS = 4
CONTS = 32


def draw_owner(key, part):
    key = jax.random.fold_in(key, 3)
    per_block = G_DEV * K_CONT
    blocks = CONTS // per_block
    block_keys = jax.random.split(key, blocks)
    orders = jax.vmap(lambda one_key: jax.random.permutation(one_key, per_block))(block_keys)
    local_group = orders.astype(jnp.int32) // K_CONT
    base_group = jnp.arange(blocks, dtype=jnp.int32)[:, None] * G_DEV
    return (local_group + base_group).reshape(CONTS).astype(jnp.int32)


def steps_of(rng, extent, pieces, least, top_value):
    gain, own = 1.0, jax.random.fold_in(rng, 6)
    for position, parts in pieces:
        steps = jnp.exp(jax.random.uniform(jax.random.fold_in(own, position), (parts,), jnp.float32, least / len(pieces), top_value / len(pieces)))
        gain = gain * jnp.repeat(steps, extent[position] // parts).reshape([-1 if axis == position else 1 for axis in range(len(extent))])
    return gain


def gaussian(rng, extent, deviation, limit, cuts=(), held_as=jnp.bfloat16):
    gain = steps_of(rng, extent, cuts, -0.22, 0.18) if cuts else 1.0
    drawn = jax.random.normal(rng, extent, jnp.float32) * deviation * gain
    return jnp.minimum(jnp.maximum(drawn, -limit), limit).astype(held_as)


def setup_inputs(seed: int = 0) -> dict:
    key_of = jax.random.split(jax.random.key(seed), 14)
    prompt_x = gaussian(key_of[0], (GROUPS, PROMPT, D), 1.0, 6.0, ((0, 2), (1, 4)))
    cont_x = gaussian(key_of[1], (CONTS, CONT_LEN, D), 1.0, 6.0, ((0, 8),))
    owner = draw_owner(jax.random.fold_in(key_of[13], 71), 0)
    w_query = gaussian(key_of[3], (D, D), D ** -0.5, 0.1875, ((0, 2), (1, 4)))
    w_key = gaussian(key_of[4], (D, D), D ** -0.5, 0.1875, ((0, 2), (1, 4)))
    w_value = gaussian(key_of[5], (D, D), D ** -0.5, 0.1875, ((0, 2), (1, 4)))
    w_out = gaussian(key_of[6], (D, D), D ** -0.5, 0.1875, ((0, 4), (1, 2)))
    w_up = gaussian(key_of[7], (D, FF), D ** -0.5, 0.1875, ((0, 2), (1, 4)))
    w_down = gaussian(key_of[8], (FF, D), FF ** -0.5, 0.09375, ((0, 4), (1, 2)))
    ln_gain = jnp.clip(1.0 + 0.18 * jax.random.normal(key_of[9], (4, D), jnp.float32), 0.099609375, 1.8984375).astype(jnp.bfloat16)
    ln_bias = gaussian(key_of[10], (4, D), 0.5, 3.0, ((1, 2),))
    prompt_grad = gaussian(key_of[11], (GROUPS, PROMPT, D), 1.0, 6.0, ((0, 2), (1, 4)))
    cont_grad = gaussian(key_of[12], (CONTS, CONT_LEN, D), 1.0, 6.0, ((0, 8),))
    return {"prompt_x": prompt_x, "cont_x": cont_x, "owner": owner, "w_query": w_query, "w_key": w_key, "w_value": w_value, "w_out": w_out, "w_up": w_up, "w_down": w_down, "ln_gain": ln_gain, "ln_bias": ln_bias, "prompt_grad": prompt_grad, "cont_grad": cont_grad}


EPSILON = 1e-05
ROPE_BASE = 10000.0
GELU_COEF = 0.7978845608028654
MASKED = -1e+30
HIGHEST_PREC = lax.Precision.HIGHEST

@jax.custom_vjp
def low(v):
    return lax.optimization_barrier(v.astype(jnp.bfloat16)).astype(jnp.float32)

@jax.custom_vjp
def low_back(v):
    return v

def low_keep(v):
    return (low(v), None)

def low_pass(kept, grad):
    return (grad,)

def back_keep(v):
    return (v, None)

def back_low(kept, grad):
    return (low(grad),)
low.defvjp(low_keep, low_pass)
low_back.defvjp(back_keep, back_low)

def layer_norm(inputs, norm_gain, norm_bias):
    centre = lax.optimization_barrier(jnp.mean(inputs, axis=-1, keepdims=True))
    centred = inputs - centre
    spread = lax.optimization_barrier(jnp.mean(centred * centred, axis=-1, keepdims=True))
    return centred * lax.rsqrt(spread + EPSILON) * norm_gain + norm_bias

def gelu_tanh(inputs):
    return 0.5 * inputs * (1.0 + jnp.tanh(GELU_COEF * (inputs + 0.044715 * inputs * inputs * inputs)))

def angles(positions, head_width):
    freqs = ROPE_BASE ** (-jnp.arange(head_width // 2, dtype=jnp.float32) * (2.0 / head_width))
    theta = positions.astype(jnp.float32)[:, None] * freqs[None, :]
    return (jnp.cos(theta)[:, None, :], jnp.sin(theta)[:, None, :])

def rotate(table, cosine, sine):
    half_width = table.shape[-1] // 2
    first_half = table[..., :half_width]
    second_half = table[..., half_width:]
    return jnp.concatenate([first_half * cosine - second_half * sine, first_half * sine + second_half * cosine], -1)

def product(left, right):
    return jnp.dot(left, right, precision=HIGHEST_PREC)

def attend(query, key_rows, val_rows, allowed):
    scores = jnp.einsum('qhd,khd->hqk', query, key_rows, precision=HIGHEST_PREC)
    scores = jnp.where(allowed[None], low_back(scores * HEAD_DIM ** (-0.5)), MASKED)
    probs = low(jax.nn.softmax(scores, axis=-1))
    return jnp.einsum('hqk,khd->qhd', probs, val_rows, precision=HIGHEST_PREC)

def block_forward(weights, prompt_rows, cont_rows, which):
    w_query, w_key, w_value, w_out, w_up, w_down, gain_rows, bias_rows = weights
    groups = prompt_rows.shape[0]
    conts = cont_rows.shape[0]
    split = groups * PROMPT
    all_rows = jnp.concatenate([prompt_rows.reshape(split, D), cont_rows.reshape(conts * CONT_LEN, D)], 0)
    positions = jnp.concatenate([jnp.tile(jnp.arange(PROMPT, dtype=jnp.int32), groups), jnp.tile(PROMPT + jnp.arange(CONT_LEN, dtype=jnp.int32), conts)])
    cosine, sine = angles(positions, HEAD_DIM)
    normed_one = low(layer_norm(all_rows, gain_rows[0], bias_rows[0]))

    def turned(weight):
        raw_rows = low_back(product(normed_one, weight)).reshape(-1, HEADS, HEAD_DIM)
        return low(rotate(raw_rows, cosine, sine))
    query = turned(w_query)
    key_rows = turned(w_key)
    val_rows = low(low_back(product(normed_one, w_value))).reshape(-1, HEADS, HEAD_DIM)
    query_prompt = query[:split].reshape(groups, PROMPT, HEADS, HEAD_DIM)
    key_prompt = key_rows[:split].reshape(groups, PROMPT, HEADS, HEAD_DIM)
    val_prompt = val_rows[:split].reshape(groups, PROMPT, HEADS, HEAD_DIM)
    query_cont = query[split:].reshape(conts, CONT_LEN, HEADS, HEAD_DIM)
    key_cont = key_rows[split:].reshape(conts, CONT_LEN, HEADS, HEAD_DIM)
    val_cont = val_rows[split:].reshape(conts, CONT_LEN, HEADS, HEAD_DIM)
    causal = jnp.arange(PROMPT)[None, :] <= jnp.arange(PROMPT)[:, None]
    columns = jnp.arange(PROMPT + CONT_LEN)[None, :]
    seen = (columns < PROMPT) | (columns - PROMPT <= jnp.arange(CONT_LEN)[:, None])

    def prompt_one(inputs):
        return attend(inputs[0], inputs[1], inputs[2], causal)

    def cont_one(inputs):
        query_one, key_one, val_one, owner_one = inputs
        keys_all = jnp.concatenate([key_prompt[owner_one], key_one], 0)
        vals_all = jnp.concatenate([val_prompt[owner_one], val_one], 0)
        return attend(query_one, keys_all, vals_all, seen)
    mixed_prompt = lax.map(jax.checkpoint(prompt_one), (query_prompt, key_prompt, val_prompt))
    mixed_cont = lax.map(jax.checkpoint(cont_one), (query_cont, key_cont, val_cont, which))
    mixed = jnp.concatenate([mixed_prompt.reshape(split, D), mixed_cont.reshape(conts * CONT_LEN, D)], 0)
    mixed = low(low_back(mixed))
    branch_one = low_back(product(mixed, w_out))
    resid_one = all_rows + layer_norm(branch_one, gain_rows[1], bias_rows[1])
    normed_three = low(layer_norm(resid_one, gain_rows[2], bias_rows[2]))
    hidden_pre = low_back(product(normed_three, w_up))
    hidden_act = low(gelu_tanh(hidden_pre))
    branch_two = low_back(product(hidden_act, w_down))
    layer_out = resid_one + layer_norm(branch_two, gain_rows[3], bias_rows[3])
    return (layer_out[:split].reshape(groups, PROMPT, D), layer_out[split:].reshape(conts, CONT_LEN, D))

def reference(prompt_x, cont_x, owner, w_query, w_key, w_value, w_out, w_up, w_down, ln_gain, ln_bias, prompt_grad, cont_grad):
    weights = tuple((w.astype(jnp.float32) for w in (w_query, w_key, w_value, w_out, w_up, w_down, ln_gain, ln_bias)))
    per_block = G_DEV * K_CONT
    blocks = CONTS // per_block
    prompt_blocks = prompt_x.astype(jnp.float32).reshape(blocks, G_DEV, PROMPT, D)
    cont_blocks = cont_x.astype(jnp.float32).reshape(blocks, per_block, CONT_LEN, D)
    pgrad_blocks = prompt_grad.astype(jnp.float32).reshape(blocks, G_DEV, PROMPT, D)
    cgrad_blocks = cont_grad.astype(jnp.float32).reshape(blocks, per_block, CONT_LEN, D)
    which = (owner.reshape(blocks, per_block) - (jnp.arange(blocks, dtype=jnp.int32) * G_DEV)[:, None]).astype(jnp.int32)

    def scan_step(totals, inputs):
        block_prompt, block_cont, block_which, grad_prompt, grad_cont = inputs

        def forward(weight_set, rows_prompt, rows_cont):
            return block_forward(weight_set, rows_prompt, rows_cont, block_which)
        outputs, pull = jax.vjp(forward, weights, block_prompt, block_cont)
        grad_weights, grad_rows_p, grad_rows_c = pull((grad_prompt, grad_cont))
        totals = tuple((left + right for left, right in zip(totals, grad_weights)))
        return (totals, (outputs[0].astype(jnp.bfloat16), outputs[1].astype(jnp.bfloat16), grad_rows_p.astype(jnp.bfloat16), grad_rows_c.astype(jnp.bfloat16)))
    start = tuple((jnp.zeros_like(w) for w in weights))
    totals, results = lax.scan(scan_step, start, (prompt_blocks, cont_blocks, which, pgrad_blocks, cgrad_blocks))
    out_prompt, out_cont, dx_prompt, dx_cont = results
    return (out_prompt.reshape(GROUPS, PROMPT, D), out_cont.reshape(CONTS, CONT_LEN, D), dx_prompt.reshape(GROUPS, PROMPT, D), dx_cont.reshape(CONTS, CONT_LEN, D), totals[0], totals[1], totals[2], totals[3], totals[4], totals[5], totals[6], totals[7])
```

```python
import functools

import jax
import jax.numpy as jnp
import numpy as np
from jax import lax
from jax.experimental import pallas as pl
from jax.experimental.pallas import tpu as pltpu
from jax.sharding import PartitionSpec as P

F32 = jnp.float32
BF16 = jnp.bfloat16
HEAD = 64
EPSILON = 1e-05
ROPE_BASE = 10000.0
GELU_COEF = 0.7978845608028654
MASKED = -1e30
MIB = 1024 * 1024


def nn(left, right):
    return jnp.dot(left, right, preferred_element_type=F32)


def nt(left, right):
    return lax.dot_general(left, right, (((1,), (1,)), ((), ())), preferred_element_type=F32)


def tn(left, right):
    return lax.dot_general(left, right, (((0,), (0,)), ((), ())), preferred_element_type=F32)


def mean(value):
    return jnp.mean(value, axis=-1, keepdims=True)


def norm(value):
    centred = value - mean(value)
    inverse = lax.rsqrt(mean(centred * centred) + EPSILON)
    return centred * inverse, inverse


def norm_back(normed, inverse, cotangent, gain):
    scaled = cotangent * gain
    return (scaled - mean(scaled) - normed * mean(scaled * normed)) * inverse


def tiles(count, size, body):
    @pl.loop(0, count // size)
    def _(step):
        body(pl.multiple_of(step * size, size))


def at(start, size):
    return pl.ds(pl.multiple_of(start, size), size)


def turn(value, start, tables, sign):
    rows, width = value.shape
    cosine, minus, plus = (
        jnp.concatenate([table[at(start, rows), :]] * (width // 128), axis=1) for table in tables
    )
    left = pltpu.roll(value, width - HEAD // 2, 1)
    right = pltpu.roll(value, HEAD // 2, 1)
    return value * cosine + sign * (left * minus + right * plus)


def head_rows(value, head, count=1):
    which = lax.broadcasted_iota(jnp.int32, value.shape, 0) // (HEAD * count)
    return jnp.where(which == head, value, jnp.zeros_like(value))


def head_lanes(value, head):
    which = lax.broadcasted_iota(jnp.int32, value.shape, 1) // HEAD
    return jnp.where(which == head, value, jnp.zeros_like(value))


def normed_dots(n1, raw, half, weight):
    rows, width = n1.shape
    part = width // 2
    own, other = weight
    for start in range(0, rows, 256):
        raw[start : start + 256, :] = nn(n1[start : start + 256, at(half * part, part)], own[...]) + nn(
            n1[start : start + 256, at((1 - half) * part, part)], other[...]
        )


def qkv_kernel(prompt, idx, x, gain, bias, wqa, wqb, wka, wkb, wva, wvb, cos, sa, sb, n1, q, k, v, raw):
    core, half, ctx = idx[0], idx[1], idx[2]
    rows = x.shape[0]
    own = rows // 2
    for side in range(2):
        first = (core if side == 0 else 1 - core) * own

        def one(start, first=first, side=side):
            normed, _ = norm(x[at(first + start, 32), :].astype(F32))
            n1[at(side * own + start, 32), :] = (normed * gain[...] + bias[...]).astype(BF16)

        tiles(own, 32, one)
    tables = (cos, sa, sb)

    def place(start):
        if prompt:
            return ctx * own + start % own
        return cos.shape[0] - 128

    for out, weight, scale in ((k, (wka, wkb), 1.0), (q, (wqa, wqb), HEAD**-0.5)):
        normed_dots(n1, raw, half, weight)
        for start in range(0, rows, 128):
            turned = turn(raw[start : start + 128, :], place(start), tables, 1.0)
            out[start : start + 128, :] = turned.astype(BF16) * BF16(scale)
    normed_dots(n1, raw, half, (wva, wvb))
    v[...] = raw[...].astype(BF16)


def kv_kernel(block, idx, xo, xt, gain, bias, wka, wkb, wva, wvb, cos, sa, sb, k, v, n1, raw):
    half, ctx = idx[1], idx[2]
    own = xo.shape[0]
    for side, x in enumerate((xo, xt)):

        def one(start, side=side, x=x):
            normed, _ = norm(x[at(start, 32), :].astype(F32))
            n1[at(side * own + start, 32), :] = (normed * gain[...] + bias[...]).astype(BF16)

        tiles(own, 32, one)
    normed_dots(n1, raw, half, (wka, wkb))
    for start in range(0, 2 * own, 128):
        turned = turn(raw[start : start + 128, :], (ctx ^ block) * own + start % own, (cos, sa, sb), 1.0)
        k[start : start + 128, :] = turned.astype(BF16)
    normed_dots(n1, raw, half, (wva, wvb))
    v[...] = raw[...].astype(BF16)


def prompt_kernel(idx, q, k0, k1, k2, k3, v0, v1, v2, v3, o_own, o_oth, p, vt, ot):
    ctx = idx[2]
    ks, vs = (k0, k1, k2, k3), (v0, v1, v2, v3)
    own = o_own.shape[0]
    width = q.shape[1]
    key = lax.broadcasted_iota(jnp.int32, (own, own), 0)
    row = lax.broadcasted_iota(jnp.int32, (own, own), 1)
    seen = key <= row
    for side, out in enumerate((o_own, o_oth)):
        rows = slice(side * own, (side + 1) * own)
        qt = q[rows, :].T
        for j in range(4):
            vt[:, j * own : (j + 1) * own] = vs[j][rows, :].T
        for head in range(width // HEAD):
            feats = slice(head * HEAD, (head + 1) * HEAD)
            qh = head_rows(qt, head)
            scores = []
            for j in range(4):
                part = nn(ks[j][rows, :], qh)
                if j == 0:
                    part = jnp.where(seen, part, MASKED)
                else:
                    part = part + jnp.where((ctx ^ j) < ctx, 0.0, MASKED).astype(F32)
                scores.append(part)
            top = functools.reduce(jnp.maximum, [jnp.max(s, axis=0, keepdims=True) for s in scores])
            scores = [jnp.exp(s - top) for s in scores]
            total = sum(jnp.sum(s, axis=0, keepdims=True) for s in scores)
            inverse = 1.0 / total
            for j in range(4):
                p[side, head, j * own : (j + 1) * own, :] = (scores[j] * inverse).astype(BF16)
            ot[feats, :] = nn(vt[feats, :], p[side, head])
        out[...] = ot[...].T.astype(BF16)


def cont_kernel(idx, q, k, v, k0, k1, k2, k3, v0, v1, v2, v3, o_own, o_oth, p, ps, vt, vst, ot):
    ks, vs = (k0, k1, k2, k3), (v0, v1, v2, v3)
    own = o_own.shape[0]
    width = q.shape[1]
    length = 128
    key = lax.broadcasted_iota(jnp.int32, (length, 2 * length), 0)
    row = lax.broadcasted_iota(jnp.int32, (length, 2 * length), 1) % length
    seen = key <= row
    for c in range(2 * own // length):
        group = idx[3 + c]
        mine = slice(c * length, (c + 1) * length)
        theirs = at(group * own, own)
        qt = q[mine, :].T
        for j in range(4):
            vt[:, j * own : (j + 1) * own] = vs[j][theirs, :].T
        vst[...] = v[mine, :].T
        for pair in range(width // HEAD // 2):
            feats = slice(pair * 2 * HEAD, (pair + 1) * 2 * HEAD)
            q2 = jnp.concatenate([head_rows(qt, 2 * pair), head_rows(qt, 2 * pair + 1)], axis=1)
            scores = [nn(ks[j][theirs, :], q2) for j in range(4)]
            scores.append(jnp.where(seen, nn(k[mine, :], q2), MASKED))
            top = functools.reduce(jnp.maximum, [jnp.max(s, axis=0, keepdims=True) for s in scores])
            scores = [jnp.exp(s - top) for s in scores]
            total = sum(jnp.sum(s, axis=0, keepdims=True) for s in scores)
            inverse = 1.0 / total
            for j in range(4):
                p[c, pair, j * own : (j + 1) * own, :] = (scores[j] * inverse).astype(BF16)
            ps[c, pair] = (scores[4] * inverse).astype(BF16)
            both = nn(vt[feats, :], p[c, pair]) + nn(vst[feats, :], ps[c, pair])
            first = pair * 2 * HEAD
            ot[first : first + HEAD, :] = both[:HEAD, :length]
            ot[first + HEAD : first + 2 * HEAD, :] = both[HEAD:, length:]
        out = o_own if c < own // length else o_oth
        place = c * length % own
        out[place : place + length, :] = ot[...].T.astype(BF16)


def after_kernel(idx, x, o0, o1, o2, o3, w0, w1, w2, w3, gain1, bias1, gain2, bias2, z, x1, n3):
    core, half = idx[0], idx[1]
    own = z.shape[0]
    part = z.shape[1] // 2
    for side in range(2):
        cols = at((half if side == 0 else 1 - half) * part, part)
        z[:, cols] = sum(nn(o[...], w[side]) for o, w in ((o0, w0), (o1, w1), (o2, w2), (o3, w3)))

    def one(start):
        rows = at(start, 32)
        normed, _ = norm(z[rows, :])
        after = x[at(core * own + start, 32), :].astype(F32) + (normed * gain1[...] + bias1[...])
        x1[rows, :] = after
        normed, _ = norm(after)
        n3[rows, :] = (normed * gain2[...] + bias2[...]).astype(BF16)

    tiles(own, 32, one)


def up_down_kernel(idx, n3o, n3t, wua, wub, wda, wdb, act, slope, keep, send):
    half = idx[1]
    own = n3o.shape[0]
    part = n3o.shape[1] // 2
    for start in range(0, act.shape[1], 256):
        cols = slice(start, start + 256)
        for side, n3 in enumerate((n3o, n3t)):
            rows = slice(side * own, (side + 1) * own)
            pre = nn(n3[:, at(half * part, part)], wua[:, cols]) + nn(
                n3[:, at((1 - half) * part, part)], wub[:, cols]
            )
            square = pre * pre
            tanh = jnp.tanh(GELU_COEF * (pre + 0.044715 * pre * square))
            up = 0.5 * (1.0 + tanh)
            act[rows, cols] = (pre * up).astype(BF16)
            inner = GELU_COEF * (1.0 + (3.0 * 0.044715) * square)
            slope[rows, cols] = (up + 0.5 * pre * (1.0 - tanh * tanh) * inner).astype(BF16)
    for side, w in enumerate((wda, wdb)):
        cols = at((half if side == 0 else 1 - half) * part, part)
        send[:, cols] = nn(act[own:, :], w[...]).astype(BF16)
        keep[:, cols] = nn(act[:own, :], w[...])


def last_kernel(idx, mine, theirs, x1, cotangent, gain, bias, y, dm, dgain, dbias):
    own = mine.shape[0]
    core = idx[0]
    dgain[...] = jnp.zeros_like(dgain)
    dbias[...] = jnp.zeros_like(dbias)

    def one(start):
        rows = at(start, 32)
        total = mine[rows, :].astype(F32) + theirs[rows, :].astype(F32)
        normed, inverse = norm(total)
        y[rows, :] = (x1[rows, :] + (normed * gain[...] + bias[...])).astype(BF16)
        dy = cotangent[at(core * own + start, 32), :].astype(F32)
        dm[rows, :] = norm_back(normed, inverse, dy, gain[...]).astype(BF16)
        dgain[...] += jnp.sum(dy * normed, axis=0, keepdims=True)
        dbias[...] += jnp.sum(dy, axis=0, keepdims=True)

    tiles(own, 32, one)


def down_up_kernel(idx, dmo, dmt, wua, wub, wda, wdb, slope, du, keep, send):
    half = idx[1]
    own = dmo.shape[0]
    part = dmo.shape[1] // 2
    for start in range(0, slope.shape[1], 256):
        cols = slice(start, start + 256)
        for side, dm in enumerate((dmo, dmt)):
            rows = slice(side * own, (side + 1) * own)
            back = nt(dm[:, at(half * part, part)], wda[cols, :]) + nt(
                dm[:, at((1 - half) * part, part)], wdb[cols, :]
            )
            du[rows, cols] = (back * slope[rows, cols].astype(F32)).astype(BF16)
    for side, w in enumerate((wua, wub)):
        cols = at((half if side == 0 else 1 - half) * part, part)
        send[:, cols] = nt(du[own:, :], w[...]).astype(BF16)
        keep[:, cols] = nt(du[:own, :], w[...])


def middle_kernel(
    idx, mine, theirs, x1, z, cotangent, gain1, gain2, dx1, dz, dgain1, dbias1, dgain2, dbias2
):
    own = mine.shape[0]
    core = idx[0]
    for total in (dgain1, dbias1, dgain2, dbias2):
        total[...] = jnp.zeros_like(total)

    def one(start):
        rows = at(start, 32)
        back = mine[rows, :].astype(F32) + theirs[rows, :].astype(F32)
        normed, inverse = norm(x1[rows, :])
        dgain2[...] += jnp.sum(back * normed, axis=0, keepdims=True)
        dbias2[...] += jnp.sum(back, axis=0, keepdims=True)
        after = cotangent[at(core * own + start, 32), :].astype(F32) + norm_back(
            normed, inverse, back, gain2[...]
        )
        dx1[rows, :] = after
        normed, inverse = norm(z[rows, :])
        dgain1[...] += jnp.sum(after * normed, axis=0, keepdims=True)
        dbias1[...] += jnp.sum(after, axis=0, keepdims=True)
        dz[rows, :] = norm_back(normed, inverse, after, gain1[...]).astype(BF16)

    tiles(own, 32, one)


def spread_out(half, dzo, dzt, woa, wob, do):
    own = dzo.shape[0]
    part = dzo.shape[1] // 2
    for side, dz in enumerate((dzo, dzt)):
        do[side * own : (side + 1) * own, :] = (
            nt(dz[:, at(half * part, part)], woa[...]) + nt(dz[:, at((1 - half) * part, part)], wob[...])
        ).astype(BF16)


def prompt_back_kernel(*refs):
    idx, dzo, dzt, woa, wob, p, q = refs[:7]
    ks, vs = refs[7:11], refs[11:15]
    cos, sa, sb, dq = refs[15:19]
    dks, dvs = refs[19:23], refs[23:27]
    do, kt, dqt, dst = refs[27:]
    half, ctx = idx[1], idx[2]
    spread_out(half, dzo, dzt, woa, wob, do)
    own = dzo.shape[0]
    width = q.shape[1]
    heads = width // HEAD
    for side in range(2):
        rows = slice(side * own, (side + 1) * own)
        dot = do[rows, :].T
        for j in range(4):
            kt[:, j * own : (j + 1) * own] = ks[j][rows, :].T
        for head in range(heads):
            feats = slice(head * HEAD, (head + 1) * HEAD)
            doh = head_rows(dot, head)
            probs = [p[side, head, j * own : (j + 1) * own, :].astype(F32) for j in range(4)]
            terms = [probs[j] * nn(vs[j][rows, :], doh) for j in range(4)]
            centre = sum(jnp.sum(t, axis=0, keepdims=True) for t in terms)
            for j in range(4):
                dst[head, j * own : (j + 1) * own, :] = (terms[j] - probs[j] * centre).astype(BF16)
            dqt[feats, :] = nn(kt[feats, :], dst[head]) * (HEAD**-0.5)
        for j in range(4):
            keys = slice(j * own, (j + 1) * own)
            dks[j][rows, :] = sum(
                nn(dst[head, keys, :], head_lanes(q[rows, :], head)) for head in range(heads)
            )
            dvs[j][rows, :] = sum(
                nn(p[side, head, keys, :], head_lanes(do[rows, :], head)) for head in range(heads)
            )
        dqf = dqt[...].T
        for start in range(0, own, 128):
            dq[side * own + start : side * own + start + 128, :] = turn(
                dqf[start : start + 128, :], ctx * own + start, (cos, sa, sb), -1.0
            ).astype(BF16)


def cont_back_kernel(*refs):
    idx, dzo, dzt, woa, wob, p, ps, q, k, v = refs[:10]
    ks, vs = refs[10:14], refs[14:18]
    adds = refs[18:26]
    cos, sa, sb, dq, dk, dv = refs[26:32]
    outs = refs[32:40]
    do, kt, kst, dqt, dst, dsst, total = refs[40:]
    half = idx[1]
    spread_out(half, dzo, dzt, woa, wob, do)
    own = dzo.shape[0]
    width = q.shape[1]
    pairs = width // HEAD // 2
    length = 128
    tables = (cos, sa, sb)
    last = cos.shape[0] - length
    for j in range(8):
        total[j] = adds[j][...]
    for c in range(2 * own // length):
        group = idx[3 + c]
        mine = slice(c * length, (c + 1) * length)
        theirs = at(group * own, own)
        dot = do[mine, :].T
        for j in range(4):
            kt[:, j * own : (j + 1) * own] = ks[j][theirs, :].T
        kst[...] = k[mine, :].T
        for pair in range(pairs):
            feats = slice(pair * 2 * HEAD, (pair + 1) * 2 * HEAD)
            do2 = jnp.concatenate([head_rows(dot, 2 * pair), head_rows(dot, 2 * pair + 1)], axis=1)
            probs = [p[c, pair, j * own : (j + 1) * own, :].astype(F32) for j in range(4)]
            probs.append(ps[c, pair].astype(F32))
            terms = [probs[j] * nn(vs[j][theirs, :], do2) for j in range(4)]
            terms.append(probs[4] * nn(v[mine, :], do2))
            centre = sum(jnp.sum(t, axis=0, keepdims=True) for t in terms)
            for j in range(4):
                dst[pair, j * own : (j + 1) * own, :] = (terms[j] - probs[j] * centre).astype(BF16)
            dsst[pair] = (terms[4] - probs[4] * centre).astype(BF16)
            both = (nn(kt[feats, :], dst[pair]) + nn(kst[feats, :], dsst[pair])) * (HEAD**-0.5)
            first = pair * 2 * HEAD
            dqt[first : first + HEAD, :] = both[:HEAD, :length]
            dqt[first + HEAD : first + 2 * HEAD, :] = both[HEAD:, length:]
        q2 = [
            jnp.concatenate([head_lanes(q[mine, :], 2 * r), head_lanes(q[mine, :], 2 * r + 1)], axis=0)
            for r in range(pairs)
        ]
        do2 = [
            jnp.concatenate([head_lanes(do[mine, :], 2 * r), head_lanes(do[mine, :], 2 * r + 1)], axis=0)
            for r in range(pairs)
        ]
        for j in range(4):
            keys = slice(j * own, (j + 1) * own)
            total[j, theirs, :] += sum(nn(dst[r, keys, :], q2[r]) for r in range(pairs))
            total[4 + j, theirs, :] += sum(nn(p[c, r, keys, :], do2[r]) for r in range(pairs))
        dkf = sum(nn(dsst[r], q2[r]) for r in range(pairs))
        dv[mine, :] = sum(nn(ps[c, r], do2[r]) for r in range(pairs)).astype(BF16)
        dk[mine, :] = turn(dkf, last, tables, -1.0).astype(BF16)
        dq[mine, :] = turn(dqt[...].T, last, tables, -1.0).astype(BF16)
    for j in range(8):
        outs[j][...] = total[j].astype(BF16)


def input_kernel(turned, idx, dq, dk, dv, wqa, wqb, wka, wkb, wva, wvb, keep, send):
    half = idx[1]
    own = dq.shape[0] // 2
    part = keep.shape[1] // 2
    for side, weights in enumerate(((wqa, wka, wva), (wqb, wkb, wvb))):
        cols = at((half if side == 0 else 1 - half) * part, part)
        for rows, out in ((slice(own, 2 * own), send), (slice(0, own), keep)):
            total = sum(nt(d[rows, :], w[...]) for d, w in zip((dq, dk, dv), weights))
            out[:, cols] = total.astype(out.dtype)


def unturn_kernel(idx, k_own, k1, k2, v_own, v1, v2, cos, sa, sb, dk, dv):
    ctx = idx[2]
    rows = dk.shape[0]
    own = rows // 2
    for start in range(0, rows, 128):
        r = slice(start, start + 128)
        total = k_own[r, :].astype(F32) + k1[r, :].astype(F32) + k2[r, :].astype(F32)
        dk[r, :] = turn(total, ctx * own + start % own, (cos, sa, sb), -1.0).astype(BF16)
    dv[...] = (v_own[...].astype(F32) + v1[...].astype(F32) + v2[...].astype(F32)).astype(BF16)


def first_kernel(idx, mine, theirs, x, dx1, gain, dx, dgain, dbias):
    own = mine.shape[0]
    core = idx[0]
    dgain[...] = jnp.zeros_like(dgain)
    dbias[...] = jnp.zeros_like(dbias)

    def one(start):
        rows = at(start, 32)
        back = mine[rows, :].astype(F32) + theirs[rows, :].astype(F32)
        normed, inverse = norm(x[at(core * own + start, 32), :].astype(F32))
        dgain[...] += jnp.sum(back * normed, axis=0, keepdims=True)
        dbias[...] += jnp.sum(back, axis=0, keepdims=True)
        dx[rows, :] = (dx1[rows, :] + norm_back(normed, inverse, back, gain[...])).astype(BF16)

    tiles(own, 32, one)


def call(kernel, idx, inputs, outputs, scratch=(), flops=0, mib=40, name=None):
    shapes = [jax.ShapeDtypeStruct(shape, dtype) for shape, dtype in outputs]
    moved = sum(int(np.prod(a.shape)) * a.dtype.itemsize for a in [*inputs, *shapes])
    vmem = pl.BlockSpec(memory_space=pltpu.VMEM)
    return pl.pallas_call(
        kernel,
        out_shape=shapes,
        in_specs=[pl.BlockSpec(memory_space=pltpu.SMEM)] + [vmem] * len(inputs),
        out_specs=[vmem] * len(outputs),
        scratch_shapes=list(scratch),
        compiler_params=pltpu.CompilerParams(vmem_limit_bytes=mib * MIB),
        cost_estimate=pl.CostEstimate(flops=int(flops), bytes_accessed=moved, transcendentals=0),
        name=name,
    )(idx, *inputs)


def rope_tables(length):
    freqs = ROPE_BASE ** (-np.arange(HEAD // 2, dtype=np.float32) * np.float32(2.0 / HEAD))
    theta = np.arange(length, dtype=np.float32)[:, None] * freqs.astype(np.float32)[None, :]
    cosine, sine = np.cos(theta), np.sin(theta)
    none = np.zeros_like(sine)
    return tuple(
        jnp.asarray(np.tile(np.concatenate(pair, axis=1), (1, 2)).astype(np.float32))
        for pair in ((cosine, cosine), (-sine, none), (none, sine))
    )


def swap(value, axis, bit):
    size = lax.axis_size(axis)
    return lax.ppermute(value, axis, [(i, i ^ bit) for i in range(size)])


def per_device(
    prompt_x,
    cont_x,
    owner,
    w_query,
    w_key,
    w_value,
    w_out,
    w_up,
    w_down,
    ln_gain,
    ln_bias,
    prompt_grad,
    cont_grad,
):
    shards = lax.axis_size("shard")
    groups, block, width = prompt_x.shape
    conts, cont_len, _ = cont_x.shape
    local = w_query.shape[1]
    hidden = w_up.shape[1]
    rows = groups * block
    own = rows // 2
    prompt_len = block * lax.axis_size("ctx")
    core = lax.axis_index("tp") % 2
    shard = lax.axis_index("shard")
    ctx = lax.axis_index("ctx")

    def both(weight, dim):
        if shards == 2:
            return weight, swap(weight, "shard", 1)
        full = lax.all_gather(weight, "shard", axis=dim, tiled=True)
        return tuple(jnp.split(full, 2, axis=dim))

    half = shard if shards == 2 else jnp.zeros_like(shard)
    which = (owner - shard * groups).reshape(2, conts // 2)
    which = jnp.where(core == 1, which[::-1], which) ^ core
    idx = jnp.concatenate([jnp.stack([core, half, ctx]), which.reshape(conts)]).astype(jnp.int32)

    wk, wv, wq = both(w_key, 0), both(w_value, 0), both(w_query, 0)
    wo = both(w_out, 1)
    wu, wd = both(w_up, 0), both(w_down, 1)
    wo0 = jnp.stack(wo)
    wo1 = swap(wo0, "tp", 1)
    wo2 = swap(wo0, "tp", 2)
    wo3 = swap(wo2, "tp", 1)

    def wide(small):
        full = lax.all_gather(small, "shard", axis=1, tiled=True)
        return [full[r : r + 1].astype(F32) for r in range(4)]

    gains, biases = wide(ln_gain), wide(ln_bias)
    tables = rope_tables(prompt_len + cont_len)

    def mine(value):
        return lax.dynamic_slice_in_dim(value, core * own, own, 0)

    xs = (prompt_x.reshape(rows, width), cont_x.reshape(rows, width))
    dys = (prompt_grad.reshape(rows, width), cont_grad.reshape(rows, width))

    x_own = mine(xs[0])
    far_own = [None] + [swap(x_own, "ctx", j) for j in (1, 2)]
    far_own.append(swap(far_own[2], "ctx", 1))
    far_oth = [None] + [swap(far_own[j], "tp", 1) for j in (1, 2, 3)]

    wide_rows = (rows, local)
    raw = pltpu.VMEM(wide_rows, F32)
    qkv_flops = 2 * rows * width * local
    chunks = []
    for prompt in (True, False):
        chunks.append(
            call(
                functools.partial(qkv_kernel, prompt),
                idx,
                [xs[0 if prompt else 1], gains[0], biases[0], *wq, *wk, *wv, *tables],
                [((rows, width), BF16)] + [(wide_rows, BF16)] * 3,
                [raw],
                flops=3 * qkv_flops,
                name="qkv_prompt" if prompt else "qkv_cont",
            )
        )
    (n1p, qp, kp, vp), (n1c, qc, kc, vc) = chunks
    keys, values = [kp], [vp]
    for j in (1, 2, 3):
        k, v = call(
            functools.partial(kv_kernel, j),
            idx,
            [far_own[j], far_oth[j], gains[0], biases[0], *wk, *wv, *tables],
            [(wide_rows, BF16)] * 2,
            [pltpu.VMEM((rows, width), BF16), raw],
            flops=2 * qkv_flops,
            name=f"kv_{j}",
        )
        keys.append(k)
        values.append(v)

    attention_flops = 2 * rows * prompt_len * local * (local // HEAD)
    half_o = ((own, local), BF16)
    o_own_p, o_oth_p, probs_p = call(
        prompt_kernel,
        idx,
        [qp, *keys, *values],
        [half_o, half_o, ((2, local // HEAD, prompt_len, own), BF16)],
        [pltpu.VMEM((local, prompt_len), BF16), pltpu.VMEM((local, own), F32)],
        flops=2 * attention_flops,
        name="attend_prompt",
    )
    pairs = local // HEAD // 2
    o_own_c, o_oth_c, probs_c, probs_s = call(
        cont_kernel,
        idx,
        [qc, kc, vc, *keys, *values],
        [
            half_o,
            half_o,
            ((conts, pairs, prompt_len, 2 * cont_len), BF16),
            ((conts, pairs, cont_len, 2 * cont_len), BF16),
        ],
        [
            pltpu.VMEM((local, prompt_len), BF16),
            pltpu.VMEM((local, cont_len), BF16),
            pltpu.VMEM((local, cont_len), F32),
        ],
        flops=2 * attention_flops,
        name="attend_cont",
    )

    big = 2 * rows * width * hidden
    mixed = ((o_own_p, o_oth_p), (o_own_c, o_oth_c))
    stage = []
    for x, (o_own, o_oth) in zip(xs, mixed):
        z, x1, n3 = call(
            after_kernel,
            idx,
            [
                x,
                o_own,
                swap(o_oth, "tp", 1),
                swap(o_own, "tp", 2),
                swap(o_oth, "tp", 3),
                wo0,
                wo1,
                wo2,
                wo3,
                gains[1],
                biases[1],
                gains[2],
                biases[2],
            ],
            [((own, width), F32), ((own, width), F32), ((own, width), BF16)],
            flops=2 * own * width * width,
            name="after_attention",
        )
        n3t = swap(n3, "tp", 1)
        act, slope, keep, send = call(
            up_down_kernel,
            idx,
            [n3, n3t, *wu, *wd],
            [((rows, hidden), BF16), ((rows, hidden), BF16), ((own, width), F32), ((own, width), BF16)],
            flops=2 * big,
            name="up_down",
        )
        summed = (keep + swap(send, "tp", 1).astype(F32)).astype(BF16)
        stage.append((z, x1, n3, n3t, act, slope, summed, swap(summed, "tp", 2)))

    row = ((1, width), F32)
    later = []
    for (z, x1, n3, n3t, act, slope, summed, theirs), dy in zip(stage, dys):
        y, dm, dgain3, dbias3 = call(
            last_kernel,
            idx,
            [summed, theirs, x1, dy, gains[3], biases[3]],
            [((own, width), BF16), ((own, width), BF16), row, row],
            name="last_norm",
        )
        dmt = swap(dm, "tp", 1)
        du, keep, send = call(
            down_up_kernel,
            idx,
            [dm, dmt, *wu, *wd, slope],
            [((rows, hidden), BF16), ((own, width), F32), ((own, width), BF16)],
            flops=2 * big,
            name="down_up",
        )
        summed = (keep + swap(send, "tp", 1).astype(F32)).astype(BF16)
        later.append((y, dm, dmt, du, summed, swap(summed, "tp", 2), dgain3, dbias3))

    def stacked(first, second):
        return jnp.concatenate([*first, *second], axis=0)

    def joined(which_one, table):
        return stacked(*[[entry[i] for i in which_one] for entry in table])

    def weight_grad(left, right):
        return tn(left, right).astype(BF16)

    dm_all = joined((1, 2), later)
    grad_down = weight_grad(joined((4,), stage), dm_all)
    grad_up = weight_grad(joined((2, 3), stage), joined((3,), later))

    middle = []
    for (z, x1, *_), (_, _, _, _, summed, theirs, *_), dy in zip(stage, later, dys):
        dx1, dz, dgain1, dbias1, dgain2, dbias2 = call(
            middle_kernel,
            idx,
            [summed, theirs, x1, z, dy, gains[1], gains[2]],
            [((own, width), F32), ((own, width), BF16), row, row, row, row],
            name="middle_norms",
        )
        middle.append((dx1, dz, swap(dz, "tp", 1), dgain1, dbias1, dgain2, dbias2))
    grad_out = weight_grad(stacked(*mixed), joined((1, 2), middle))

    dqp, *grads = call(
        prompt_back_kernel,
        idx,
        [middle[0][1], middle[0][2], *wo, probs_p, qp, *keys, *values, *tables],
        [(wide_rows, BF16)] + [(wide_rows, F32)] * 8,
        [
            pltpu.VMEM(wide_rows, BF16),
            pltpu.VMEM((local, prompt_len), BF16),
            pltpu.VMEM((local, own), F32),
            pltpu.VMEM((local // HEAD, prompt_len, own), BF16),
        ],
        flops=4 * attention_flops,
        mib=48,
        name="attend_prompt_back",
    )
    dqc, dkc, dvc, *grads = call(
        cont_back_kernel,
        idx,
        [middle[1][1], middle[1][2], *wo, probs_c, probs_s, qc, kc, vc, *keys, *values, *grads, *tables],
        [(wide_rows, BF16)] * 11,
        [
            pltpu.VMEM(wide_rows, BF16),
            pltpu.VMEM((local, prompt_len), BF16),
            pltpu.VMEM((local, cont_len), BF16),
            pltpu.VMEM((local, cont_len), F32),
            pltpu.VMEM((pairs, prompt_len, 2 * cont_len), BF16),
            pltpu.VMEM((pairs, cont_len, 2 * cont_len), BF16),
            pltpu.VMEM((8, *wide_rows), F32),
        ],
        flops=4 * attention_flops,
        mib=48,
        name="attend_cont_back",
    )

    def to_owner(parts):
        ours, one, two, three = parts
        two = (two.astype(F32) + swap(three, "ctx", 1).astype(F32)).astype(BF16)
        return ours, swap(one, "ctx", 1), swap(two, "ctx", 2)

    dkp, dvp = call(
        unturn_kernel,
        idx,
        [*to_owner(grads[:4]), *to_owner(grads[4:]), *tables],
        [(wide_rows, BF16)] * 2,
        name="unturn",
    )

    dx = []
    firsts = []
    for x, (dx1, *_), gradient in zip(xs, middle, ((dqp, dkp, dvp), (dqc, dkc, dvc))):
        keep, send = call(
            functools.partial(input_kernel, True),
            idx,
            [*gradient, *wq, *wk, *wv],
            [((own, width), F32), ((own, width), BF16)],
            flops=3 * qkv_flops,
            name="input_back",
        )
        summed = (keep + swap(send, "tp", 1).astype(F32)).astype(BF16)
        out, dgain0, dbias0 = call(
            first_kernel,
            idx,
            [summed, swap(summed, "tp", 2), x, dx1, gains[0]],
            [((own, width), BF16), row, row],
            name="first_norm",
        )
        dx.append(out)
        firsts.append((dgain0, dbias0))
    n1 = jnp.concatenate([n1p, n1c], axis=0)
    grad_query, grad_key, grad_value = (
        weight_grad(n1, jnp.concatenate(pair, axis=0)) for pair in ((dqp, dqc), (dkp, dkc), (dvp, dvc))
    )

    def over_ctx(part):
        quarter = part.shape[0] // 4
        four = part.reshape(4, quarter, part.shape[1])
        near, far = ctx & 1, ctx & 2

        def pick(value, index):
            return lax.dynamic_index_in_dim(value, index, 0, keepdims=False)

        mine_two = jnp.stack([pick(four, ctx), pick(four, ctx ^ 2)])
        send_two = jnp.stack([pick(four, ctx ^ 1), pick(four, ctx ^ 3)])
        mine_two = mine_two.astype(F32) + swap(send_two, "ctx", 1).astype(F32)
        one = (mine_two[0] + swap(mine_two[1].astype(BF16), "ctx", 2).astype(F32)).astype(BF16)
        two = jnp.stack([one, swap(one, "ctx", 2)])
        other = swap(two, "ctx", 1)
        blocks = jnp.concatenate([two, other], axis=0)
        result = jnp.stack([pick(blocks, jnp.array([0, 2, 1, 3])[ctx ^ i]) for i in range(4)])
        return result.reshape(part.shape).astype(F32)

    def reduced(grad, dim):
        if shards == 2:
            size = grad.shape[dim] // 2
            ours = lax.dynamic_slice_in_dim(grad, shard * size, size, dim)
            theirs = lax.dynamic_slice_in_dim(grad, (1 - shard) * size, size, dim)
            part = (ours.astype(F32) + swap(theirs, "shard", 1).astype(F32)).astype(BF16)
        else:
            part = lax.psum_scatter(grad, "shard", scatter_dimension=dim, tiled=True)
        return over_ctx(part)

    small = [None] * 8
    for first, (_, _, _, dgain1, dbias1, dgain2, dbias2), (*_, dgain3, dbias3) in zip(firsts, middle, later):
        for place, term in zip(
            range(8), (first[0], dgain1, dgain2, dgain3, first[1], dbias1, dbias2, dbias3)
        ):
            small[place] = term if small[place] is None else small[place] + term
    small = jnp.concatenate(small, axis=0)
    small = small + swap(small, "tp", 1)
    if shards == 2:
        size = width // 2
        small = lax.dynamic_slice_in_dim(small, shard * size, size, 1) + swap(
            lax.dynamic_slice_in_dim(small, (1 - shard) * size, size, 1), "shard", 1
        )
    else:
        small = lax.psum_scatter(small, "shard", scatter_dimension=1, tiled=True)
    small = small + swap(small, "ctx", 1)
    small = small + swap(small, "ctx", 2)

    def whole(value, shape):
        other = swap(value, "tp", 1)
        first = jnp.where(core == 0, value, other)
        second = jnp.where(core == 0, other, value)
        return jnp.concatenate([first, second], axis=0).reshape(shape)

    return (
        whole(later[0][0], prompt_x.shape),
        whole(later[1][0], cont_x.shape),
        whole(dx[0], prompt_x.shape),
        whole(dx[1], cont_x.shape),
        reduced(grad_query, 0),
        reduced(grad_key, 0),
        reduced(grad_value, 0),
        reduced(grad_out, 1),
        reduced(grad_up, 0),
        reduced(grad_down, 1),
        small[:4],
        small[4:],
    )


def solution(mesh):
    placed = (
        P("shard", "ctx", None),
        P(("shard", "ctx"), None, None),
        P(("shard", "ctx")),
        P("shard", "tp"),
        P("shard", "tp"),
        P("shard", "tp"),
        P("tp", "shard"),
        P("shard", "tp"),
        P("tp", "shard"),
        P(None, "shard"),
        P(None, "shard"),
        P("shard", "ctx", None),
        P(("shard", "ctx"), None, None),
    )
    rows = (P("shard", "ctx", None), P(("shard", "ctx"), None, None))
    return jax.shard_map(
        per_device,
        mesh=mesh,
        in_specs=placed,
        out_specs=rows + rows + placed[3:11],
        check_vma=False,
    )
```

```python
import functools

import jax
import jax.numpy as jnp
import numpy as np
from jax import lax
from jax.experimental import pallas as pl
from jax.experimental.pallas import tpu as pltpu
from jax.sharding import PartitionSpec as P

F32 = jnp.float32
BF16 = jnp.bfloat16
HEAD = 64
EPSILON = 1e-05
ROPE_BASE = 10000.0
GELU_COEF = 0.7978845608028654
MASKED = -1e30
MIB = 1024 * 1024
TILE = 128
TILE = 128
TILE = 128
TILE = 128
TILE = 128
TILE = 128
TILE = 128
TILE = 128


def nn(left, right):
    return jnp.dot(left, right, preferred_element_type=F32)


def nt(left, right):
    return lax.dot_general(left, right, (((1,), (1,)), ((), ())), preferred_element_type=F32)


def tn(left, right):
    return lax.dot_general(left, right, (((0,), (0,)), ((), ())), preferred_element_type=F32)


def mean(value):
    return jnp.mean(value, axis=-1, keepdims=True)


def norm(value):
    centred = value - mean(value)
    inverse = lax.rsqrt(mean(centred * centred) + EPSILON)
    return centred * inverse, inverse


def norm_back(normed, inverse, cotangent, gain):
    scaled = cotangent * gain
    return (scaled - mean(scaled) - normed * mean(scaled * normed)) * inverse


def tiles(count, body):
    @pl.loop(0, count // TILE)
    def _(step):
        body(at(step * TILE, TILE))


def at(start, size):
    return pl.ds(pl.multiple_of(start, size), size)


def turn(value, start, tables, sign):
    rows, width = value.shape
    cosine, minus, plus = (
        jnp.concatenate([tables[i, at(start, rows), :]] * (width // 128), axis=1) for i in range(3)
    )
    left = pltpu.roll(value, width - HEAD // 2, 1)
    right = pltpu.roll(value, HEAD // 2, 1)
    return value * cosine + sign * (left * minus + right * plus)


def head_rows(value, head, count=1):
    which = lax.broadcasted_iota(jnp.int32, value.shape, 0) // (HEAD * count)
    return jnp.where(which == head, value, jnp.zeros_like(value))


def head_lanes(value, head):
    which = lax.broadcasted_iota(jnp.int32, value.shape, 1) // HEAD
    return jnp.where(which == head, value, jnp.zeros_like(value))


class Part:
    def __init__(self, array, rows, start):
        self.array, self.rows, self.start = array, rows, start
        self.shape, self.dtype = array.shape, array.dtype


class Far:
    def __init__(self, array):
        self.array = array
        self.shape, self.dtype = array.shape, array.dtype


class Stack:
    def __init__(self, arrays):
        self.arrays = list(arrays)
        self.rows = [a.shape[0] for a in arrays]
        self.shape, self.dtype = (sum(self.rows), *arrays[0].shape[1:]), arrays[0].dtype


class Coming:
    def __init__(self, ref, copy=None, pieces=()):
        self.ref, self.copy, self.pieces = ref, copy, pieces

    def __call__(self):
        if self.copy is not None:
            self.copy.wait()
            self.copy = None
        start = 0
        for piece, rows in self.pieces:
            self.ref[start : start + rows, :] = piece[...]
            start += rows
        self.pieces = ()
        return self.ref


class Going:
    def __init__(self, ref, kind, targets, semaphores):
        self.ref, self.kind, self.targets, self.semaphores = ref, kind, targets, semaphores
        self.copies = []

    def send(self, *index):
        if self.kind == "far":
            where = index if index else Ellipsis
            copy = pltpu.make_async_copy(self.ref.at[where], self.targets[0].at[where], next(self.semaphores))
            copy.start()
            self.copies.append(copy)

    def close(self):
        if self.kind == "cut":
            start = 0
            for target in self.targets:
                rows = target.shape[0]
                target[...] = self.ref[start : start + rows, :]
                start += rows
        elif not self.copies:
            self.send()
        for copy in self.copies:
            copy.wait()


SENDS = 40
PIECES = 3


def pieces_of(rows):
    tiles_of = rows // 16
    return [16 * (tiles_of // PIECES + (i < tiles_of % PIECES)) for i in range(PIECES)]


class Line:
    def __init__(self, idx):
        self.idx = idx

    def after(self, *values):
        *values, self.idx = lax.optimization_barrier((*values, self.idx))
        return values[0] if len(values) == 1 else values

    def call(self, kernel, inputs, outputs, scratch=(), name=None, margin=12):
        inputs = [Stack(a) if isinstance(a, list) else a for a in inputs]
        given = []
        for a in inputs:
            given += a.arrays if isinstance(a, Stack) else [a.array if isinstance(a, (Part, Far)) else a]
        places = [
            pl.BlockSpec(memory_space=pl.ANY if isinstance(a, Far) else pltpu.VMEM)
            for a in inputs
            for _ in (a.arrays if isinstance(a, Stack) else [a])
        ]
        kinds = [out[2] if len(out) > 2 else "" for out in outputs]
        pieces = [pieces_of(out[0][0]) if kind == "cut" else [out[0][0]] for out, kind in zip(outputs, kinds)]
        shapes = [
            jax.ShapeDtypeStruct((rows, *out[0][1:]), out[1]) for out, cuts in zip(outputs, pieces) for rows in cuts
        ]
        out_places = [
            pl.BlockSpec(memory_space=pl.ANY if kind == "far" else pltpu.VMEM)
            for kind, cuts in zip(kinds, pieces)
            for _ in cuts
        ]
        held = [pltpu.VMEM(a.shape, a.dtype) for a in inputs if isinstance(a, (Far, Stack))]
        held += [pltpu.VMEM(out[0], out[1]) for out, kind in zip(outputs, kinds) if kind]
        own = [*held, *scratch]
        size = sum(int(np.prod(a.shape)) * np.dtype(a.dtype).itemsize for a in own)

        def body(*refs):
            refs = list(refs)
            idx = refs.pop(0)
            sources = [refs.pop(0) for _ in given]
            targets = [refs.pop(0) for _ in shapes]
            semaphores = refs.pop()
            free = (semaphores.at[i] for i in range(SENDS))
            coming = []
            for value in inputs:
                if isinstance(value, Stack):
                    buffer = refs.pop(0)
                    coming.append(Coming(buffer, pieces=[(sources.pop(0), rows) for rows in value.rows]))
                    continue
                source, copy = sources.pop(0), None
                if isinstance(value, Part):
                    source = source.at[at(value.start(idx), value.rows), :]
                elif isinstance(value, Far):
                    buffer = refs.pop(0)
                    copy = pltpu.make_async_copy(source, buffer, next(free))
                    copy.start()
                    source = buffer
                coming.append(Coming(source, copy))
            going = []
            for kind, cuts in zip(kinds, pieces):
                mine = [targets.pop(0) for _ in cuts]
                going.append(Going(refs.pop(0) if kind else mine[0], kind, mine, free))
            kernel(idx, *coming, *going, *refs)
            for arrival in coming:
                arrival()
            for out in going:
                out.close()

        out = pl.pallas_call(
            body,
            out_shape=shapes,
            in_specs=[pl.BlockSpec(memory_space=pltpu.SMEM), *places],
            out_specs=out_places,
            scratch_shapes=[*own, pltpu.SemaphoreType.DMA((SENDS,))],
            compiler_params=pltpu.CompilerParams(vmem_limit_bytes=size + margin * MIB),
            cost_estimate=pl.CostEstimate(flops=1000, bytes_accessed=1000, transcendentals=0),
            name=name,
        )(self.idx, *given)
        out = list(out)
        out[-1], self.idx = lax.optimization_barrier((out[-1], self.idx))
        return [[out.pop(0) for _ in cuts] if kind == "cut" else out.pop(0) for kind, cuts in zip(kinds, pieces)]


def stack_kernel(idx, one, two, out):
    out.ref[0] = one()[...]
    out.ref[1] = two()[...]


def gains_kernel(idx, own, other, both):
    half = idx[1]
    part = own.ref.shape[1]
    for side, value in enumerate((own, other)):
        cols = at((half if side == 0 else 1 - half) * part, part)
        both.ref[:, cols] = value()[...].astype(F32)


def normed_rows(x, first, n1, start, count, gain, bias):
    @pl.loop(0, count // TILE)
    def _(step):
        normed, _ = norm(x[at(first + step * TILE, TILE), :].astype(F32))
        n1[at(start + step * TILE, TILE), :] = (normed * gain + bias).astype(BF16)


def pack_kernel(idx, wk, wv, wq, packed):
    local = wk.ref.shape[1]
    for i, w in enumerate((wk, wv, wq)):
        packed.ref[:, i * local : (i + 1) * local] = w()[...]


def normed_dots(n1, raw, half, own, other, which):
    rows, width = n1.shape
    part = width // 2
    local = raw.shape[1]
    cols = slice(which * local, (which + 1) * local)
    for start in range(0, rows, 256):
        raw[start : start + 256, :] = nn(n1[start : start + 256, at(half * part, part)], own[:, cols]) + nn(
            n1[start : start + 256, at((1 - half) * part, part)], other[:, cols]
        )


def normed_kernel(idx, x, gb, n1):
    core = idx[0]
    gb, x = gb(), x()
    own = x.shape[0] // 2
    for side in range(2):
        first = (core if side == 0 else 1 - core) * own
        normed_rows(x, first, n1.ref, side * own, own, gb[0:1, :], gb[4:5, :])


def qkv_kernel(prompt, idx, n1, w_own, w_oth, tables, out, raw):
    half, ctx = idx[1], idx[2]
    n1, w_own, w_oth = n1(), w_own(), w_oth()
    rows = n1.shape[0]
    own = rows // 2
    tables = tables()

    def place(start):
        if prompt:
            return ctx * own + start % own
        return tables.shape[1] - 128

    for which, scale in ((0, 1.0), (2, HEAD**-0.5)):
        normed_dots(n1, raw, half, w_own, w_oth, which)
        for start in range(0, rows, 128):
            turned = turn(raw[start : start + 128, :], place(start), tables, 1.0)
            out.ref[which, start : start + 128, :] = turned.astype(BF16) * BF16(scale)
    normed_dots(n1, raw, half, w_own, w_oth, 1)
    out.ref[1] = raw[...].astype(BF16)


def norm_pieces_kernel(idx, *refs):
    gb, out = refs[-2](), refs[-1]
    for i, x in enumerate(refs[:-2]):
        x = x()
        normed_rows(x, 0, out.ref, i * x.shape[0], x.shape[0], gb[0:1, :], gb[4:5, :])


def kv_kernel(blocks, idx, own_near, own_far, oth_near, oth_far, w_own, w_oth, tables, out, n1, raw):
    half, ctx, bit = idx[1], idx[2], idx[7]
    parts = [r() for r in (own_near, own_far, oth_near, oth_far)]
    tables = tables()
    w_own, w_oth = w_own(), w_oth()
    piece = parts[0].shape[0] // len(blocks)
    own = 2 * piece
    for i, block in enumerate(blocks):
        for place, x in zip((bit, 1 - bit, 2 + bit, 3 - bit), parts):
            n1[at(place * piece, piece), :] = x[i * piece : (i + 1) * piece, :]
        normed_dots(n1, raw, half, w_own, w_oth, 0)
        for start in range(0, 2 * own, 128):
            turned = turn(raw[start : start + 128, :], (ctx ^ block) * own + start % own, tables, 1.0)
            out.ref[2 * i, start : start + 128, :] = turned.astype(BF16)
        normed_dots(n1, raw, half, w_own, w_oth, 1)
        out.ref[2 * i + 1] = raw[...].astype(BF16)


def keys_values(near, two, one):
    near, two, one = near(), two(), one()
    return [near.at[0], two.at[0], two.at[2], one.at[0]], [near.at[1], two.at[1], two.at[3], one.at[1]]


def softmax_keys(scores):
    top = functools.reduce(jnp.maximum, [jnp.max(s, axis=0, keepdims=True) for s in scores])
    scores = [jnp.exp(s - top) for s in scores]
    inverse = 1.0 / sum(jnp.sum(s, axis=0, keepdims=True) for s in scores)
    return [(s * inverse).astype(BF16) for s in scores]


def prompt_kernel(idx, near, two, one, o_oth, o_own, p, vt, ot):
    ctx = idx[2]
    q = near().at[2]
    ks, vs = keys_values(near, two, one)
    own = o_own.ref.shape[0]
    width = q.shape[1]
    key = lax.broadcasted_iota(jnp.int32, (own, own), 0)
    row = lax.broadcasted_iota(jnp.int32, (own, own), 1)
    seen = key <= row
    for side, out in ((1, o_oth), (0, o_own)):
        rows = slice(side * own, (side + 1) * own)
        qt = q[rows, :].T
        for j in range(4):
            vt[:, j * own : (j + 1) * own] = vs[j][rows, :].T
        for head in range(width // HEAD):
            feats = slice(head * HEAD, (head + 1) * HEAD)
            qh = head_rows(qt, head)
            scores = []
            for j in range(4):
                part = nn(ks[j][rows, :], qh)
                if j == 0:
                    part = jnp.where(seen, part, MASKED)
                else:
                    part = part + jnp.where((ctx ^ j) < ctx, 0.0, MASKED).astype(F32)
                scores.append(part)
            for j, probs in enumerate(softmax_keys(scores)):
                p.ref[side, head, j * own : (j + 1) * own, :] = probs
            p.send(side, head)
            ot[feats, :] = nn(vt[feats, :], p.ref[side, head])
        out.ref[...] = ot[...].T.astype(BF16)
        out.send()


def cont_kernel(idx, mine_kvq, near, two, one, o_oth, o_own, p, vt, ot):
    mine_kvq = mine_kvq()
    k, v, q = (mine_kvq.at[i] for i in range(3))
    ks, vs = keys_values(near, two, one)
    own = o_own.ref.shape[0]
    width = q.shape[1]
    length = 128
    per = own // length
    key = lax.broadcasted_iota(jnp.int32, (length, 2 * length), 0)
    row = lax.broadcasted_iota(jnp.int32, (length, 2 * length), 1) % length
    seen = key <= row
    for c in [*range(per, 2 * per), *range(per)]:
        group = idx[3 + c]
        mine = slice(c * length, (c + 1) * length)
        theirs = at(group * own, own)
        qt = q[mine, :].T
        for j in range(4):
            vt[:, j * own : (j + 1) * own] = vs[j][theirs, :].T
        vt[:, 4 * own :] = v[mine, :].T
        for pair in range(width // HEAD // 2):
            feats = slice(pair * 2 * HEAD, (pair + 1) * 2 * HEAD)
            q2 = jnp.concatenate([head_rows(qt, 2 * pair), head_rows(qt, 2 * pair + 1)], axis=1)
            scores = [nn(ks[j][theirs, :], q2) for j in range(4)]
            scores.append(jnp.where(seen, nn(k[mine, :], q2), MASKED))
            probs = softmax_keys(scores)
            for j in range(4):
                p.ref[c, pair, j * own : (j + 1) * own, :] = probs[j]
            p.ref[c, pair, 4 * own :, :] = probs[4]
            p.send(c, pair)
            both = nn(vt[feats, :], p.ref[c, pair])
            first = pair * 2 * HEAD
            ot[first : first + HEAD, :] = both[:HEAD, :length]
            ot[first + HEAD : first + 2 * HEAD, :] = both[HEAD:, length:]
        out = o_own if c < per else o_oth
        place = c % per * length
        out.ref[place : place + length, :] = ot[...].T.astype(BF16)
        if c % per == per - 1:
            out.send()


def after_kernel(idx, w0, o0, w1, o1, w2, o2, w3, o3, x, gb, n3, z, x1):
    half = idx[1]
    part = z.ref.shape[1] // 2
    pairs = [(o(), w()) for o, w in ((o0, w0), (o1, w1), (o2, w2), (o3, w3))]
    for side in range(2):
        cols = at((half if side == 0 else 1 - half) * part, part)
        z.ref[:, cols] = sum(nn(o[...], w[side]) for o, w in pairs)
    z.send()
    x, gb = x(), gb()

    def one(rows):
        normed, _ = norm(z.ref[rows, :])
        after = x[rows, :].astype(F32) + (normed * gb[1:2, :] + gb[5:6, :])
        x1.ref[rows, :] = after
        normed, _ = norm(after)
        n3.ref[rows, :] = (normed * gb[2:3, :] + gb[6:7, :]).astype(BF16)

    tiles(x.shape[0], one)


def up_down_kernel(idx, n3o, wua, wub, n3t, wda, wdb, send, act, slope, keep):
    half = idx[1]
    own = n3o.ref.shape[0]
    part = n3o.ref.shape[1] // 2
    n3o, wua, wub = n3o(), wua(), wub()
    hidden = wua.shape[1]
    for side, n3 in enumerate((n3o, n3t)):
        if side == 1:
            n3 = n3()
        rows = slice(side * own, (side + 1) * own)
        for start in range(0, hidden, 256):
            cols = slice(start, start + 256)
            pre = nn(n3[:, at(half * part, part)], wua[:, cols]) + nn(
                n3[:, at((1 - half) * part, part)], wub[:, cols]
            )
            square = pre * pre
            tanh = jnp.tanh(GELU_COEF * (pre + 0.044715 * pre * square))
            up = 0.5 * (1.0 + tanh)
            act.ref[rows, cols] = (pre * up).astype(BF16)
            inner = GELU_COEF * (1.0 + (3.0 * 0.044715) * square)
            slope.ref[rows, cols] = (up + 0.5 * pre * (1.0 - tanh * tanh) * inner).astype(BF16)
        act.send(rows)
        slope.send(rows)
    weights = (wda(), wdb())
    for out, rows in ((send, slice(own, 2 * own)), (keep, slice(0, own))):
        for side, w in enumerate(weights):
            cols = at((half if side == 0 else 1 - half) * part, part)
            out.ref[:, cols] = nn(act.ref[rows, :], w[...]).astype(out.ref.dtype)
        out.send()


def last_kernel(idx, mine, theirs, x1, cotangent, gb, dm, y, grads):
    mine, theirs, cotangent, gb, x1 = mine(), theirs(), cotangent(), gb(), x1()
    grads.ref[...] = jnp.zeros_like(grads.ref)

    def one(rows):
        total = mine[rows, :].astype(F32) + theirs[rows, :].astype(F32)
        normed, inverse = norm(total)
        y.ref[rows, :] = (x1[rows, :] + (normed * gb[3:4, :] + gb[7:8, :])).astype(BF16)
        dy = cotangent[rows, :].astype(F32)
        dm.ref[rows, :] = norm_back(normed, inverse, dy, gb[3:4, :]).astype(BF16)
        grads.ref[0:1, :] += jnp.sum(dy * normed, axis=0, keepdims=True)
        grads.ref[1:2, :] += jnp.sum(dy, axis=0, keepdims=True)

    tiles(mine.shape[0], one)


def down_up_kernel(idx, dmo, wda, wdb, slope, dmt, wua, wub, send, du, keep):
    half = idx[1]
    own = dmo.ref.shape[0]
    part = dmo.ref.shape[1] // 2
    dmo, wda, wdb, slope = dmo(), wda(), wdb(), slope()
    for side, dm in enumerate((dmo, dmt)):
        if side == 1:
            dm = dm()
        rows = slice(side * own, (side + 1) * own)
        for start in range(0, slope.shape[1], 256):
            cols = slice(start, start + 256)
            back = nt(dm[:, at(half * part, part)], wda[cols, :]) + nt(
                dm[:, at((1 - half) * part, part)], wdb[cols, :]
            )
            du.ref[rows, cols] = (back * slope[rows, cols].astype(F32)).astype(BF16)
        du.send(rows)
    weights = (wua(), wub())
    for out, rows in ((send, slice(own, 2 * own)), (keep, slice(0, own))):
        for side, w in enumerate(weights):
            cols = at((half if side == 0 else 1 - half) * part, part)
            out.ref[:, cols] = nt(du.ref[rows, :], w[...]).astype(out.ref.dtype)
        out.send()


def middle_kernel(idx, mine, theirs, x1, cotangent, gb, z, dz, dx1, grads):
    mine, theirs, x1, cotangent, gb, z = mine(), theirs(), x1(), cotangent(), gb(), z()
    grads.ref[...] = jnp.zeros_like(grads.ref)

    def one(rows):
        back = mine[rows, :].astype(F32) + theirs[rows, :].astype(F32)
        normed, inverse = norm(x1[rows, :])
        grads.ref[1:2, :] += jnp.sum(back * normed, axis=0, keepdims=True)
        grads.ref[3:4, :] += jnp.sum(back, axis=0, keepdims=True)
        after = cotangent[rows, :].astype(F32) + norm_back(normed, inverse, back, gb[2:3, :])
        dx1.ref[rows, :] = after
        normed, inverse = norm(z[rows, :])
        grads.ref[0:1, :] += jnp.sum(after * normed, axis=0, keepdims=True)
        grads.ref[2:3, :] += jnp.sum(after, axis=0, keepdims=True)
        dz.ref[rows, :] = norm_back(normed, inverse, after, gb[1:2, :]).astype(BF16)

    tiles(mine.shape[0], one)


def spread_out(half, dzo, dzt, wo, do):
    own = dzo.shape[0]
    part = dzo.shape[1] // 2
    for side, dz in enumerate((dzo, dzt)):
        do[side * own : (side + 1) * own, :] = (
            nt(dz[:, at(half * part, part)], wo[0]) + nt(dz[:, at((1 - half) * part, part)], wo[1])
        ).astype(BF16)


def prompt_back_kernel(idx, dzo, dzt, wo, near, two, one, p, tables, o_own, o_oth, dkv, dq, grad_out, do, kt, dqt, dst):
    half, ctx = idx[1], idx[2]
    dzo, dzt, wo = dzo(), dzt(), wo()
    spread_out(half, dzo, dzt, wo, do)
    q = near().at[2]
    ks, vs = keys_values(near, two, one)
    p = p()
    tables = tables()
    own = dzo.shape[0]
    width = q.shape[1]
    heads = width // HEAD
    mixed = (o_own(), o_oth())
    for start in range(0, dzo.shape[1], 512):
        cols = slice(start, start + 512)
        grad_out.ref[:, cols] = tn(mixed[0][...], dzo[:, cols]) + tn(mixed[1][...], dzt[:, cols])
    grad_out.send()
    for side in range(2):
        rows = slice(side * own, (side + 1) * own)
        dot = do[rows, :].T
        for j in range(4):
            kt[:, j * own : (j + 1) * own] = ks[j][rows, :].T
        for head in range(heads):
            feats = slice(head * HEAD, (head + 1) * HEAD)
            doh = head_rows(dot, head)
            probs = [p[side, head, j * own : (j + 1) * own, :].astype(F32) for j in range(4)]
            terms = [probs[j] * nn(vs[j][rows, :], doh) for j in range(4)]
            centre = sum(jnp.sum(t, axis=0, keepdims=True) for t in terms)
            for j in range(4):
                dst[head, j * own : (j + 1) * own, :] = (terms[j] - probs[j] * centre).astype(BF16)
            dqt[feats, :] = nn(kt[feats, :], dst[head]) * (HEAD**-0.5)
        for j in range(4):
            keys = slice(j * own, (j + 1) * own)
            dkv.ref[j, 0, rows, :] = sum(
                nn(dst[head, keys, :], head_lanes(q[rows, :], head)) for head in range(heads)
            )
            dkv.ref[j, 1, rows, :] = sum(
                nn(p[side, head, keys, :], head_lanes(do[rows, :], head)) for head in range(heads)
            )
        dqf = dqt[...].T
        for start in range(0, own, 128):
            dq.ref[side * own + start : side * own + start + 128, :] = turn(
                dqf[start : start + 128, :], ctx * own + start, tables, -1.0
            ).astype(BF16)


def cont_back_kernel(idx, dzo, dzt, wo, mine_kvq, near, two, one, p, adds, tables, o_own, o_oth, grad_out, *refs):
    outs = refs[:4]
    send, keep, dkvq = refs[4:7]
    do, kt, dqt, dst = refs[7:]
    half = idx[1]
    dzo, dzt, wo = dzo(), dzt(), wo()
    spread_out(half, dzo, dzt, wo, do)
    mine_kvq = mine_kvq()
    k, v, q = (mine_kvq.at[i] for i in range(3))
    ks, vs = keys_values(near, two, one)
    p, total = p(), adds()
    tables = tables()
    own = dzo.shape[0]
    width = q.shape[1]
    pairs = width // HEAD // 2
    length = 128
    last = tables.shape[1] - length
    mixed, grad_out = (o_own(), o_oth()), grad_out()
    part = dzo.shape[1] // 2
    for out, where in ((send, 1 - half), (keep, half)):
        cols = at(where * part, part)
        out.ref[...] = (
            grad_out[:, cols] + (tn(mixed[0][...], dzo[:, cols]) + tn(mixed[1][...], dzt[:, cols]))
        ).astype(BF16)
    for c in range(2 * own // length):
        group = idx[3 + c]
        mine = slice(c * length, (c + 1) * length)
        theirs = at(group * own, own)
        dot = do[mine, :].T
        for j in range(4):
            kt[:, j * own : (j + 1) * own] = ks[j][theirs, :].T
        kt[:, 4 * own :] = k[mine, :].T
        for pair in range(pairs):
            feats = slice(pair * 2 * HEAD, (pair + 1) * 2 * HEAD)
            do2 = jnp.concatenate([head_rows(dot, 2 * pair), head_rows(dot, 2 * pair + 1)], axis=1)
            probs = [p[c, pair, j * own : (j + 1) * own, :].astype(F32) for j in range(4)]
            probs.append(p[c, pair, 4 * own :, :].astype(F32))
            terms = [probs[j] * nn(vs[j][theirs, :], do2) for j in range(4)]
            terms.append(probs[4] * nn(v[mine, :], do2))
            centre = sum(jnp.sum(t, axis=0, keepdims=True) for t in terms)
            for j in range(4):
                dst[pair, j * own : (j + 1) * own, :] = (terms[j] - probs[j] * centre).astype(BF16)
            dst[pair, 4 * own :, :] = (terms[4] - probs[4] * centre).astype(BF16)
            both = nn(kt[feats, :], dst[pair]) * (HEAD**-0.5)
            first = pair * 2 * HEAD
            dqt[first : first + HEAD, :] = both[:HEAD, :length]
            dqt[first + HEAD : first + 2 * HEAD, :] = both[HEAD:, length:]
        q2, do2 = (
            [
                jnp.concatenate([head_lanes(t[mine, :], 2 * r), head_lanes(t[mine, :], 2 * r + 1)], axis=0)
                for r in range(pairs)
            ]
            for t in (q, do)
        )
        for j in range(4):
            keys = slice(j * own, (j + 1) * own)
            total[j, 0, theirs, :] += sum(nn(dst[r, keys, :], q2[r]) for r in range(pairs))
            total[j, 1, theirs, :] += sum(nn(p[c, r, keys, :], do2[r]) for r in range(pairs))
        dkf = sum(nn(dst[r, 4 * own :, :], q2[r]) for r in range(pairs))
        dkvq.ref[1, mine, :] = sum(nn(p[c, r, 4 * own :, :], do2[r]) for r in range(pairs)).astype(BF16)
        dkvq.ref[0, mine, :] = turn(dkf, last, tables, -1.0).astype(BF16)
        dkvq.ref[2, mine, :] = turn(dqt[...].T, last, tables, -1.0).astype(BF16)
    for j in (3, 2, 1, 0):
        outs[j].ref[...] = total[j].astype(BF16)
        outs[j].send()


def unturn_kernel(idx, own_kv, one, two, tables, dkv):
    ctx = idx[2]
    parts = [r() for r in (own_kv, one, two)]
    tables = tables()
    rows = dkv.ref.shape[1]
    own = rows // 2
    for start in range(0, rows, 128):
        r = slice(start, start + 128)
        total = sum(part[0, r, :].astype(F32) for part in parts)
        dkv.ref[0, r, :] = turn(total, ctx * own + start % own, tables, -1.0).astype(BF16)
    dkv.ref[1] = sum(part[1].astype(F32) for part in parts).astype(BF16)


def parts_of(*refs):
    first = refs[0]()
    if len(refs) == 1:
        return [first.at[i] for i in range(3)]
    return [first.at[0], first.at[1], refs[1]()]


def input_kernel(count, idx, *refs):
    half = idx[1]
    grads = parts_of(*refs[:count])
    w_own, w_oth, send, keep = refs[count:]
    weights = (w_own(), w_oth())
    local = grads[0].shape[1]
    own = keep.ref.shape[0]
    part = keep.ref.shape[1] // 2
    for out, rows in ((send, slice(own, 2 * own)), (keep, slice(0, own))):
        for side, w in enumerate(weights):
            cols = at((half if side == 0 else 1 - half) * part, part)
            total = sum(nt(d[rows, :], w[:, i * local : (i + 1) * local]) for i, d in enumerate(grads))
            out.ref[:, cols] = total.astype(out.ref.dtype)
        out.send()


def first_kernel(idx, mine, theirs, x, gb, dx1, dx, grads):
    mine, theirs, x, gb, dx1 = mine(), theirs(), x(), gb(), dx1()
    grads.ref[...] = jnp.zeros_like(grads.ref)

    def one(rows):
        back = mine[rows, :].astype(F32) + theirs[rows, :].astype(F32)
        normed, inverse = norm(x[rows, :].astype(F32))
        grads.ref[0:1, :] += jnp.sum(back * normed, axis=0, keepdims=True)
        grads.ref[1:2, :] += jnp.sum(back, axis=0, keepdims=True)
        dx.ref[rows, :] = (dx1[rows, :] + norm_back(normed, inverse, back, gb[0:1, :])).astype(BF16)

    tiles(mine.shape[0], one)


def cut_right(idx, pairs, send, keep):
    half = idx[1]
    part = send.ref.shape[1]
    for out, where in ((send, 1 - half), (keep, half)):
        cols = at(where * part, part)
        for start in range(0, out.ref.shape[0], 256):
            feats = slice(start, start + 256)
            out.ref[feats, :] = sum(tn(left[rows, feats], right[:, cols]) for left, rows, right in pairs).astype(
                BF16
            )
        out.send()


def grad_down_kernel(idx, act_a, act_b, a0, a1, b0, b1, send, keep):
    pairs = []
    for act, rights in ((act_a(), (a0, a1)), (act_b(), (b0, b1))):
        for i, right in enumerate(rights):
            right = right()
            own = right.shape[0]
            pairs.append((act, slice(i * own, (i + 1) * own), right))
    cut_right(idx, pairs, send, keep)


def grad_up_kernel(idx, a0, a1, b0, b1, du_a, du_b, send, keep):
    half = idx[1]
    lefts = [r() for r in (a0, a1, b0, b1)]
    rights = (du_a(), du_b())
    own = lefts[0].shape[0]
    part = send.ref.shape[0]
    for out, where in ((send, 1 - half), (keep, half)):
        for start in range(0, part, 256):
            feats = at(where * part + start, 256)
            for col in range(0, rights[0].shape[1], 512):
                out.ref[start : start + 256, col : col + 512] = sum(
                    tn(left[:, feats], rights[i // 2][(i % 2) * own : (i % 2 + 1) * own, col : col + 512])
                    for i, left in enumerate(lefts)
                ).astype(BF16)
        out.send()


def grad_qkv_kernel(idx, n1a, n1b, dkv_p, dq_p, dkvq_c, send, keep):
    half = idx[1]
    lefts = (n1a(), n1b())
    rights = (parts_of(dkv_p, dq_p), parts_of(dkvq_c))
    part = send.ref.shape[0]
    local = rights[0][0].shape[1]
    for out, where in ((send, 1 - half), (keep, half)):
        for start in range(0, part, 256):
            feats = at(where * part + start, 256)
            for i in range(3):
                out.ref[start : start + 256, i * local : (i + 1) * local] = sum(
                    tn(left[:, feats], right[i][...]) for left, right in zip(lefts, rights)
                ).astype(BF16)
        out.send()


def over_shard_kernel(idx, keep, came, send, mine):
    ctx = idx[2]
    keep, came = keep(), came()
    rows = keep.shape[0] // 4
    for out, order in ((send, (1, 3)), (mine, (0, 2))):
        for place, j in enumerate(order):
            r = at((ctx ^ j) * rows, rows)
            out.ref[place] = (keep[r, :].astype(F32) + came[r, :].astype(F32)).astype(BF16)


def over_shard_two_kernel(idx, keep, came, keep_out, came_out, send, mine):
    ctx = idx[2]
    keep, came, keep_out, came_out = keep(), came(), keep_out(), came_out()
    rows, few = keep.shape[0] // 4, keep_out.shape[0] // 4
    width, half = keep.shape[1], keep_out.shape[1] // 2
    for out, order in ((send, (1, 3)), (mine, (0, 2))):
        for place, j in enumerate(order):
            r, f = at((ctx ^ j) * rows, rows), at((ctx ^ j) * few, few)
            out.ref[place, :, :width] = (keep[r, :].astype(F32) + came[r, :].astype(F32)).astype(BF16)
            total = (keep_out[f, :].astype(F32) + came_out[f, :].astype(F32)).astype(BF16)
            out.ref[place, :few, width:] = total[:, :half]
            out.ref[place, few:, width:] = total[:, half:]


def near_kernel(idx, mine, came, send, keep):
    mine, came = mine(), came()
    send.ref[...] = (mine[1].astype(F32) + came[1].astype(F32)).astype(BF16)
    keep.ref[...] = mine[0].astype(F32) + came[0].astype(F32)


def far_kernel(idx, keep, came, total):
    total.ref[...] = (keep()[...] + came()[...].astype(F32)).astype(BF16)


def place_kernel(idx, q0, q1, q2, q3, out):
    ctx = idx[2]
    for j, quarter in enumerate((q0, q1, q2, q3)):
        quarter = quarter()
        out.ref[at((ctx ^ j) * quarter.shape[0], quarter.shape[0]), :] = quarter[...].astype(F32)


def place_two_kernel(idx, q0, q1, q2, q3, key, value, query, proj):
    ctx = idx[2]
    local = key.ref.shape[1]
    few, half = proj.ref.shape[0] // 4, proj.ref.shape[1] // 2
    for j, quarter in enumerate((q0, q1, q2, q3)):
        quarter = quarter()
        rows = at((ctx ^ j) * quarter.shape[0], quarter.shape[0])
        for i, out in enumerate((key, value, query)):
            out.ref[rows, :] = quarter[:, i * local : (i + 1) * local].astype(F32)
        rows = at((ctx ^ j) * few, few)
        proj.ref[rows, :half] = quarter[:few, 3 * local :].astype(F32)
        proj.ref[rows, half:] = quarter[few:, 3 * local :].astype(F32)


def whole_kernel(idx, *refs):
    core = idx[0]
    count = len(refs) // 3
    for i in range(count):
        out = refs[2 * count + i]
        for j, part in enumerate(refs[2 * i : 2 * i + 2]):
            part = part()
            rows = at((core if j == 0 else 1 - core) * part.shape[0], part.shape[0])
            out.ref[rows, :] = part[...]
        out.send()


def sum_kernel(idx, keep, came, total):
    keep, came = keep(), came()
    total.ref[...] = (keep[...] + came[...].astype(F32)).astype(BF16)


def add_kernel(idx, one, two, total):
    total.ref[...] = (one()[...].astype(F32) + two()[...].astype(F32)).astype(BF16)


def small_kernel(idx, first_a, first_b, mid_a, mid_b, last_a, last_b, out):
    first, mid, last = (a()[...] + b()[...] for a, b in ((first_a, first_b), (mid_a, mid_b), (last_a, last_b)))
    out.ref[0:1, :] = first[0:1, :]
    out.ref[1:3, :] = mid[0:2, :]
    out.ref[3:4, :] = last[0:1, :]
    out.ref[4:5, :] = first[1:2, :]
    out.ref[5:7, :] = mid[2:4, :]
    out.ref[7:8, :] = last[1:2, :]


def rope_tables(length):
    freqs = ROPE_BASE ** (-np.arange(HEAD // 2, dtype=np.float32) * np.float32(2.0 / HEAD))
    theta = np.arange(length, dtype=np.float32)[:, None] * freqs.astype(np.float32)[None, :]
    cosine, sine = np.cos(theta), np.sin(theta)
    none = np.zeros_like(sine)
    pairs = ((cosine, cosine), (-sine, none), (none, sine))
    return jnp.asarray(np.stack([np.tile(np.concatenate(pair, axis=1), (1, 2)) for pair in pairs]).astype(np.float32))


def swap(value, axis, bit):
    size = lax.axis_size(axis)
    return lax.ppermute(value, axis, [(i, i ^ bit) for i in range(size)])


class Reduction:
    def __init__(self, line, sends, keeps, dims):
        self.line, self.keeps = line, keeps
        self.pair = lax.axis_size("shard") == 2
        self.sends, self.dims = sends, dims
        self.came = [None] * len(keeps)

    def start(self, i=0, *with_these):
        if self.pair:
            self.came[i] = swap(self.line.after(self.sends[i]), "shard", 1)

    def arrived(self, i=0):
        if self.pair:
            self.came[i] = self.line.after(self.came[i])

    def over_shard(self):
        if not self.pair:
            self.total = []
            for send, keep, dim in zip(self.sends, self.keeps, self.dims):
                full = jnp.concatenate([keep, send], axis=dim)
                part = lax.psum_scatter(full, "shard", scatter_dimension=dim, tiled=True)
                self.total.append(lax.psum(part, "ctx").astype(F32))
            return
        rows, width = self.keeps[0].shape
        if len(self.keeps) > 1:
            width += self.keeps[1].size // rows
        pairs = [value for pair in zip(self.keeps, self.came) for value in pair]
        send, self.mine = self.line.call(
            over_shard_two_kernel if len(self.keeps) > 1 else over_shard_kernel,
            pairs,
            [((2, rows // 4, width), BF16)] * 2,
            name="over_shard",
        )
        self.moving = swap(send, "ctx", 1)

    def near(self):
        if self.pair:
            shape = self.mine.shape[1:]
            send, self.keep = self.line.call(
                near_kernel, [self.mine, self.moving], [(shape, BF16), (shape, F32)], name="near"
            )
            self.moving = swap(send, "ctx", 2)

    def far(self):
        if self.pair:
            (self.q0,) = self.line.call(
                far_kernel, [self.keep, self.moving], [(self.keep.shape, BF16)], name="far"
            )
            self.q2, self.q1 = swap(self.q0, "ctx", 2), swap(self.q0, "ctx", 1)

    def last(self):
        if self.pair:
            self.q2 = self.line.after(self.q2)
            self.q3 = swap(self.q2, "ctx", 1)

    def placed(self):
        if not self.pair:
            if len(self.keeps) == 1:
                return self.total
            return [*jnp.split(self.total[0], 3, axis=1), self.total[1]]
        rows, width = self.keeps[0].shape
        outs, kernel = [((rows, width), F32)], place_kernel
        if len(self.keeps) > 1:
            outs = [((rows, width // 3), F32)] * 3 + [(self.keeps[1].shape, F32)]
            kernel = place_two_kernel
        return self.line.call(kernel, [self.q0, self.q1, self.q2, self.q3], outs, name="place")


def per_device(
    prompt_x,
    cont_x,
    owner,
    w_query,
    w_key,
    w_value,
    w_out,
    w_up,
    w_down,
    ln_gain,
    ln_bias,
    prompt_grad,
    cont_grad,
):
    shards = lax.axis_size("shard")
    groups, block, width = prompt_x.shape
    conts, cont_len, _ = cont_x.shape
    local = w_query.shape[1]
    hidden = w_up.shape[1]
    rows = groups * block
    own = rows // 2
    piece = own // 2
    part = width // 2
    prompt_len = block * lax.axis_size("ctx")
    core = lax.axis_index("tp") % 2
    bit = lax.axis_index("tp") // 2
    shard = lax.axis_index("shard")
    ctx = lax.axis_index("ctx")
    xs = (prompt_x.reshape(rows, width), cont_x.reshape(rows, width))
    dys = (prompt_grad.reshape(rows, width), cont_grad.reshape(rows, width))

    def both(weight, dim):
        if shards == 2:
            return weight, swap(weight, "shard", 1)
        full = lax.all_gather(weight, "shard", axis=dim, tiled=True)
        return tuple(jnp.split(full, 2, axis=dim))

    half = shard if shards == 2 else jnp.zeros_like(shard)
    which = (owner - shard * groups).reshape(2, conts // 2)
    which = jnp.where(core == 1, which[::-1], which) ^ core
    idx = jnp.concatenate([jnp.stack([core, half, ctx]), which.reshape(conts), jnp.stack([bit])])
    line = Line(idx.astype(jnp.int32))

    small = both(jnp.concatenate([ln_gain, ln_bias], axis=0), 1)
    (gb,) = line.call(gains_kernel, list(small), [((8, width), F32)], name="gains")
    packed = jnp.concatenate([w_key, w_value, w_query], axis=1)
    if shards == 2:
        (packed,) = line.call(
            pack_kernel, [w_key, w_value, w_query], [((part, 3 * local), BF16)], name="pack"
        )
    wqkv = both(packed, 0)
    quarter = lax.dynamic_slice_in_dim(xs[0], core * own + bit * piece, piece, 0)
    far, near = swap(quarter, "ctx", 2), swap(quarter, "ctx", 1)
    tables = rope_tables(prompt_len + cont_len)

    wo = both(line.after(w_out), 1)
    n1p, n1c = (
        line.call(normed_kernel, [x, gb], [((rows, width), BF16)], name="norm_first")[0] for x in xs
    )
    wide_rows = (rows, local)
    raw = pltpu.VMEM(wide_rows, F32)
    chunks = []
    for prompt in (True, False):
        chunks += line.call(
            functools.partial(qkv_kernel, prompt),
            [n1p if prompt else n1c, *wqkv, tables],
            [((3, *wide_rows), BF16)],
            [raw],
            name="qkv_prompt" if prompt else "qkv_cont",
        )
        if prompt:
            (normed,) = line.call(norm_pieces_kernel, [near, far, gb], [((own, width), BF16)], name="norm_pieces")
            both_near = [normed, swap(normed, "tp", 2)]
            far, w_up = line.after(far, w_up)
            last_near = swap(far, "ctx", 1)
            wu = both(w_up, 0)
    kvq_p, kvq_c = chunks
    (wo0,) = line.call(stack_kernel, wo, [((2, *wo[0].shape), BF16)], name="stack_out")
    both_near.append(swap(line.after(normed), "tp", 1))
    (normed,) = line.call(norm_pieces_kernel, [last_near, gb], [((piece, width), BF16)], name="norm_piece")
    one_near = [normed, swap(normed, "tp", 2), swap(normed, "tp", 1)]
    both_near[1] = line.after(both_near[1])
    both_near.append(swap(both_near[1], "tp", 1))
    seen = [kvq_p]

    def far_keys(blocks, parts):
        seen.extend(
            line.call(
                functools.partial(kv_kernel, blocks),
                [*parts, *wqkv, tables],
                [((2 * len(blocks), *wide_rows), BF16)],
                [pltpu.VMEM((rows, width), BF16), raw],
                name="far_keys",
            )
        )

    far_keys((1, 2), both_near)
    wo0 = line.after(wo0)
    wo2, wo1 = swap(wo0, "tp", 2), swap(wo0, "tp", 1)
    one_near[1] = line.after(one_near[1])
    one_near.append(swap(one_near[1], "tp", 1))
    far_keys((3,), one_near)

    half_o = ((own, local), BF16)
    o_oth_p, o_own_p, probs_p = line.call(
        prompt_kernel,
        seen,
        [half_o, half_o, ((2, local // HEAD, prompt_len, own), BF16, "far")],
        [pltpu.VMEM((local, prompt_len), BF16), pltpu.VMEM((local, own), F32)],
        name="attend_prompt",
    )
    wo1, wo2, *wu, w_down = line.after(wo1, wo2, *wu, w_down)
    wo3 = swap(wo2, "tp", 1)
    wd = both(w_down, 1)
    pairs = local // HEAD // 2
    mixed = [(o_own_p, o_oth_p)]

    def gathered(o_own, o_oth):
        return o_own, swap(o_oth, "tp", 1), swap(o_own, "tp", 2), swap(o_oth, "tp", 3)

    full_o = [gathered(o_own_p, o_oth_p)]
    all_len = prompt_len + cont_len
    o_oth_c, o_own_c, probs_c = line.call(
        cont_kernel,
        [kvq_c, *seen],
        [half_o, half_o, ((conts, pairs, all_len, 2 * cont_len), BF16, "far")],
        [pltpu.VMEM((local, all_len), BF16), pltpu.VMEM((local, cont_len), F32)],
        name="attend_cont",
    )
    mixed.append((o_own_c, o_oth_c))
    full_o.append(gathered(o_own_c, o_oth_c))

    def mine(value):
        return Part(value, own, lambda idx: idx[0] * own)

    own_rows, own_rows_f = ((own, width), BF16), ((own, width), F32)
    own_pieces = (*own_rows, "cut")

    def swapped(pieces):
        return [swap(piece, "tp", 1) for piece in pieces]

    def summed(keep, send):
        came = swapped(send)
        (total,) = line.call(sum_kernel, [keep, came], [own_rows], name="sum_cores")
        return total, swap(total, "tp", 2)

    stage = []
    for x, os in zip(xs, full_o):
        n3, z, x1 = line.call(
            after_kernel,
            [wo0, os[0], wo1, os[1], wo2, os[2], wo3, os[3], mine(x), gb],
            [own_pieces, own_rows_f, own_rows_f],
            name="after_attention",
        )
        n3t = swapped(n3)
        send, act, slope, keep = line.call(
            up_down_kernel,
            [n3, *wu, n3t, *wd],
            [own_pieces, ((rows, hidden), BF16), ((rows, hidden), BF16), own_rows_f],
            name="up_down",
        )
        stage.append((z, x1, n3, n3t, act, slope, *summed(keep, send)))

    later = []
    for i, dy in enumerate(dys):
        z, x1, n3, n3t, act, slope, total, theirs = stage[i]
        dm, y, grads_last = line.call(
            last_kernel,
            [total, theirs, x1, mine(dy), gb],
            [own_pieces, own_rows, ((2, width), F32)],
            name="last_norm",
        )
        dmt = swapped(dm)
        send, du, keep = line.call(
            down_up_kernel,
            [dm, *wd, slope, dmt, *wu],
            [own_pieces, ((rows, hidden), BF16), own_rows_f],
            name="down_up",
        )
        later.append((y, dm, dmt, du, *summed(keep, send), grads_last))

    middle = []

    def middle_norms(i):
        z, x1 = stage[i][:2]
        total, theirs = later[i][4:6]
        dz, dx1, grads_middle = line.call(
            middle_kernel,
            [total, theirs, x1, mine(dys[i]), gb, z],
            [own_pieces, own_rows_f, ((4, width), F32)],
            name="middle_norms",
        )
        middle.append((dx1, dz, swapped(dz), grads_middle))

    y_p, y_c = later[0][0], later[1][0]

    def assembled(*pairs):
        return line.call(
            whole_kernel,
            [value for pair in pairs for value in pair],
            [((rows, width), BF16)] * len(pairs),
            name="whole",
        )

    middle_norms(0)
    send, keep = line.call(
        grad_down_kernel,
        [stage[0][4], stage[1][4], *later[0][1:3], *later[1][1:3]],
        [((hidden, part), BF16)] * 2,
        name="grad_down",
    )
    down = Reduction(line, [send], [keep], (1,))
    down.start()
    pair_rows = (2, *wide_rows)
    grads, dqp, grad_out = line.call(
        prompt_back_kernel,
        [*middle[0][1:3], *[Far(a) for a in (wo0, *seen, probs_p)], tables, *[Far(o) for o in mixed[0]]],
        [((4, *pair_rows), F32, "far"), (wide_rows, BF16), ((local, width), F32, "far")],
        [
            pltpu.VMEM(wide_rows, BF16),
            pltpu.VMEM((local, prompt_len), BF16),
            pltpu.VMEM((local, own), F32),
            pltpu.VMEM((local // HEAD, prompt_len, own), BF16),
        ],
        name="attend_prompt_back",
    )
    send, keep = line.call(
        grad_up_kernel,
        [*stage[0][2:4], *stage[1][2:4], later[0][3], later[1][3]],
        [((part, hidden), BF16)] * 2,
        name="grad_up",
    )
    middle_norms(1)
    down.over_shard()
    up = Reduction(line, [send], [keep], (0,))
    up.start()
    *grads, send_out, keep_out, dkvq_c = line.call(
        cont_back_kernel,
        [*middle[1][1:3], *[Far(a) for a in (wo0, kvq_c, *seen, probs_c, grads)], tables]
        + [*[Far(o) for o in mixed[1]], Far(grad_out)],
        [(pair_rows, BF16)] * 4 + [((local, part), BF16)] * 2 + [((3, *wide_rows), BF16)],
        [
            pltpu.VMEM(wide_rows, BF16),
            pltpu.VMEM((local, all_len), BF16),
            pltpu.VMEM((local, cont_len), F32),
            pltpu.VMEM((pairs, all_len, 2 * cont_len), BF16),
        ],
        name="attend_cont_back",
    )
    kv3 = swap(grads[3], "ctx", 1)
    dx = []
    firsts = []

    def input_back(gradient):
        send, keep = line.call(
            functools.partial(input_kernel, len(gradient)),
            [*gradient, *[Far(w) for w in wqkv]],
            [own_pieces, own_rows_f],
            name="input_back",
        )
        return keep, send

    def first_norm(i, pair):
        out, grads_first = line.call(
            first_kernel,
            [*pair, mine(xs[i]), gb, Far(middle[i][0])],
            [own_rows, ((2, width), F32)],
            name="first_norm",
        )
        dx.append(out)
        firsts.append(grads_first)

    down.near()
    totals_c = summed(*input_back((dkvq_c,)))
    (kv2,) = line.call(add_kernel, [grads[2], kv3], [(pair_rows, BF16)], name="add_kv")
    kv2 = swap(kv2, "ctx", 2)
    kv1 = swap(line.after(grads[1]), "ctx", 1)
    up.over_shard()
    first_norm(1, totals_c)
    down.far()
    up.near()
    (dkv_p,) = line.call(
        unturn_kernel, [grads[0], kv1, kv2, tables], [(pair_rows, BF16)], name="unturn"
    )
    send, keep = line.call(
        grad_qkv_kernel,
        [Far(n1p), Far(n1c), dkv_p, Far(dqp), Far(dkvq_c)],
        [((part, 3 * local), BF16)] * 2,
        name="grad_qkv",
    )
    qkv = Reduction(line, [send, send_out], [keep, keep_out], (0, 1))
    qkv.start(0)
    totals_p = summed(*input_back((dkv_p, Far(dqp))))
    down.last()
    up.far()
    qkv.start(1)
    qkv.over_shard()
    first_norm(0, totals_p)
    (small,) = line.call(
        small_kernel,
        [firsts[1], firsts[0], middle[0][3], middle[1][3], later[0][6], later[1][6]],
        [((8, width), F32)],
        name="small",
    )
    small = small + swap(small, "tp", 1)
    (grad_down,) = down.placed()
    up.last()
    qkv.near()
    small = line.after(small)
    if shards == 2:
        small = lax.dynamic_slice_in_dim(small, shard * part, part, 1) + swap(
            lax.dynamic_slice_in_dim(small, (1 - shard) * part, part, 1), "shard", 1
        )
    else:
        small = lax.psum_scatter(small, "shard", scatter_dimension=1, tiled=True)
    small = small + swap(small, "ctx", 1)
    halves = line.after(y_p, y_c, dx[1], dx[0])
    others = [swap(value, "tp", 1) for value in halves]
    (grad_up,) = up.placed()
    qkv.far()
    small = small + swap(line.after(small), "ctx", 2)
    yp, yc, dxp, dxc = assembled(*zip(halves, others))
    qkv.last()
    grad_key, grad_value, grad_query, grad_out = qkv.placed()
    return (
        yp.reshape(prompt_x.shape),
        yc.reshape(cont_x.shape),
        dxp.reshape(prompt_x.shape),
        dxc.reshape(cont_x.shape),
        grad_query,
        grad_key,
        grad_value,
        grad_out,
        grad_up,
        grad_down,
        small[:4],
        small[4:],
    )


def solution(mesh):
    placed = (
        P("shard", "ctx", None),
        P(("shard", "ctx"), None, None),
        P(("shard", "ctx")),
        P("shard", "tp"),
        P("shard", "tp"),
        P("shard", "tp"),
        P("tp", "shard"),
        P("shard", "tp"),
        P("tp", "shard"),
        P(None, "shard"),
        P(None, "shard"),
        P("shard", "ctx", None),
        P(("shard", "ctx"), None, None),
    )
    rows = (P("shard", "ctx", None), P(("shard", "ctx"), None, None))
    return jax.shard_map(
        per_device,
        mesh=mesh,
        in_specs=placed,
        out_specs=rows + rows + placed[3:11],
        check_vma=False,
    )
```

```python
import functools

import jax
import jax.numpy as jnp
import numpy as np
from jax import lax
from jax.experimental import pallas as pl
from jax.experimental.pallas import tpu as pltpu
from jax.sharding import PartitionSpec as P

F32 = jnp.float32
BF16 = jnp.bfloat16
HEAD = 64
EPSILON = 1e-05
ROPE_BASE = 10000.0
GELU_COEF = 0.7978845608028654
MASKED = -1e30
MIB = 1024 * 1024
TILE = 128
TILE = 128
TILE = 128
TILE = 128
TILE = 128
TILE = 128
TILE = 128
TILE = 128


def nn(left, right):
    return jnp.dot(left, right, preferred_element_type=F32)


def nt(left, right):
    return lax.dot_general(left, right, (((1,), (1,)), ((), ())), preferred_element_type=F32)


def tn(left, right):
    return lax.dot_general(left, right, (((0,), (0,)), ((), ())), preferred_element_type=F32)


def mean(value):
    return jnp.mean(value, axis=-1, keepdims=True)


def norm(value):
    centred = value - mean(value)
    inverse = lax.rsqrt(mean(centred * centred) + EPSILON)
    return centred * inverse, inverse


def norm_back(normed, inverse, cotangent, gain):
    scaled = cotangent * gain
    return (scaled - mean(scaled) - normed * mean(scaled * normed)) * inverse


def tiles(count, body):
    @pl.loop(0, count // TILE)
    def _(step):
        body(at(step * TILE, TILE))


def at(start, size):
    return pl.ds(pl.multiple_of(start, size), size)


def turn(value, start, tables, sign):
    rows, width = value.shape
    cosine, minus, plus = (
        jnp.concatenate([tables[i, at(start, rows), :]] * (width // 128), axis=1) for i in range(3)
    )
    left = pltpu.roll(value, width - HEAD // 2, 1)
    right = pltpu.roll(value, HEAD // 2, 1)
    return value * cosine + sign * (left * minus + right * plus)


def head_rows(value, head, count=1):
    which = lax.broadcasted_iota(jnp.int32, value.shape, 0) // (HEAD * count)
    return jnp.where(which == head, value, jnp.zeros_like(value))


def head_lanes(value, head):
    which = lax.broadcasted_iota(jnp.int32, value.shape, 1) // HEAD
    return jnp.where(which == head, value, jnp.zeros_like(value))


class Part:
    def __init__(self, array, rows, start):
        self.array, self.rows, self.start = array, rows, start
        self.shape, self.dtype = array.shape, array.dtype


class Far:
    def __init__(self, array):
        self.array = array
        self.shape, self.dtype = array.shape, array.dtype


class Stack:
    def __init__(self, arrays):
        self.arrays = list(arrays)
        self.rows = [a.shape[0] for a in arrays]
        self.shape, self.dtype = (sum(self.rows), *arrays[0].shape[1:]), arrays[0].dtype


class Coming:
    def __init__(self, ref, copy=None, pieces=()):
        self.ref, self.copy, self.pieces = ref, copy, pieces

    def __call__(self):
        if self.copy is not None:
            self.copy.wait()
            self.copy = None
        start = 0
        for piece, rows in self.pieces:
            self.ref[start : start + rows, :] = piece[...]
            start += rows
        self.pieces = ()
        return self.ref


class Going:
    def __init__(self, ref, kind, targets, semaphores):
        self.ref, self.kind, self.targets, self.semaphores = ref, kind, targets, semaphores
        self.copies = []

    def send(self, *index):
        if self.kind == "far":
            where = index if index else Ellipsis
            copy = pltpu.make_async_copy(self.ref.at[where], self.targets[0].at[where], next(self.semaphores))
            copy.start()
            self.copies.append(copy)

    def close(self):
        if self.kind == "cut":
            start = 0
            for target in self.targets:
                rows = target.shape[0]
                target[...] = self.ref[start : start + rows, :]
                start += rows
        elif not self.copies:
            self.send()
        for copy in self.copies:
            copy.wait()


SENDS = 40
PIECES = 3


def pieces_of(rows):
    tiles_of = rows // 16
    return [16 * (tiles_of // PIECES + (i < tiles_of % PIECES)) for i in range(PIECES)]


class Line:
    def __init__(self, idx):
        self.idx = idx

    def after(self, *values):
        *values, self.idx = lax.optimization_barrier((*values, self.idx))
        return values[0] if len(values) == 1 else values

    def call(self, kernel, inputs, outputs, scratch=(), name=None, margin=12):
        inputs = [Stack(a) if isinstance(a, list) else a for a in inputs]
        given = []
        for a in inputs:
            given += a.arrays if isinstance(a, Stack) else [a.array if isinstance(a, (Part, Far)) else a]
        places = [
            pl.BlockSpec(memory_space=pl.ANY if isinstance(a, Far) else pltpu.VMEM)
            for a in inputs
            for _ in (a.arrays if isinstance(a, Stack) else [a])
        ]
        kinds = [out[2] if len(out) > 2 else "" for out in outputs]
        pieces = [pieces_of(out[0][0]) if kind == "cut" else [out[0][0]] for out, kind in zip(outputs, kinds)]
        shapes = [
            jax.ShapeDtypeStruct((rows, *out[0][1:]), out[1]) for out, cuts in zip(outputs, pieces) for rows in cuts
        ]
        out_places = [
            pl.BlockSpec(memory_space=pl.ANY if kind == "far" else pltpu.VMEM)
            for kind, cuts in zip(kinds, pieces)
            for _ in cuts
        ]
        held = [pltpu.VMEM(a.shape, a.dtype) for a in inputs if isinstance(a, (Far, Stack))]
        held += [pltpu.VMEM(out[0], out[1]) for out, kind in zip(outputs, kinds) if kind]
        own = [*held, *scratch]
        size = sum(int(np.prod(a.shape)) * np.dtype(a.dtype).itemsize for a in own)

        def body(*refs):
            refs = list(refs)
            idx = refs.pop(0)
            sources = [refs.pop(0) for _ in given]
            targets = [refs.pop(0) for _ in shapes]
            semaphores = refs.pop()
            free = (semaphores.at[i] for i in range(SENDS))
            coming = []
            for value in inputs:
                if isinstance(value, Stack):
                    buffer = refs.pop(0)
                    coming.append(Coming(buffer, pieces=[(sources.pop(0), rows) for rows in value.rows]))
                    continue
                source, copy = sources.pop(0), None
                if isinstance(value, Part):
                    source = source.at[at(value.start(idx), value.rows), :]
                elif isinstance(value, Far):
                    buffer = refs.pop(0)
                    copy = pltpu.make_async_copy(source, buffer, next(free))
                    copy.start()
                    source = buffer
                coming.append(Coming(source, copy))
            going = []
            for kind, cuts in zip(kinds, pieces):
                mine = [targets.pop(0) for _ in cuts]
                going.append(Going(refs.pop(0) if kind else mine[0], kind, mine, free))
            kernel(idx, *coming, *going, *refs)
            for arrival in coming:
                arrival()
            for out in going:
                out.close()

        out = pl.pallas_call(
            body,
            out_shape=shapes,
            in_specs=[pl.BlockSpec(memory_space=pltpu.SMEM), *places],
            out_specs=out_places,
            scratch_shapes=[*own, pltpu.SemaphoreType.DMA((SENDS,))],
            compiler_params=pltpu.CompilerParams(vmem_limit_bytes=size + margin * MIB),
            cost_estimate=pl.CostEstimate(flops=1000, bytes_accessed=1000, transcendentals=0),
            name=name,
        )(self.idx, *given)
        out = list(out)
        out[-1], self.idx = lax.optimization_barrier((out[-1], self.idx))
        return [[out.pop(0) for _ in cuts] if kind == "cut" else out.pop(0) for kind, cuts in zip(kinds, pieces)]


def stack_kernel(idx, one, two, out):
    out.ref[0] = one()[...]
    out.ref[1] = two()[...]


def gains_kernel(idx, own, other, both):
    half = idx[1]
    part = own.ref.shape[1]
    for side, value in enumerate((own, other)):
        cols = at((half if side == 0 else 1 - half) * part, part)
        both.ref[:, cols] = value()[...].astype(F32)


def normed_rows(x, first, n1, start, count, gain, bias):
    @pl.loop(0, count // TILE)
    def _(step):
        normed, _ = norm(x[at(first + step * TILE, TILE), :].astype(F32))
        n1[at(start + step * TILE, TILE), :] = (normed * gain + bias).astype(BF16)


def pack_kernel(idx, wk, wv, wq, packed):
    local = wk.ref.shape[1]
    for i, w in enumerate((wk, wv, wq)):
        packed.ref[:, i * local : (i + 1) * local] = w()[...]


def normed_dots(n1, raw, half, own, other, which):
    rows, width = n1.shape
    part = width // 2
    local = raw.shape[1]
    cols = slice(which * local, (which + 1) * local)
    for start in range(0, rows, 256):
        raw[start : start + 256, :] = nn(n1[start : start + 256, at(half * part, part)], own[:, cols]) + nn(
            n1[start : start + 256, at((1 - half) * part, part)], other[:, cols]
        )


def normed_kernel(idx, x, gb, n1):
    core = idx[0]
    gb, x = gb(), x()
    own = x.shape[0] // 2
    for side in range(2):
        first = (core if side == 0 else 1 - core) * own
        normed_rows(x, first, n1.ref, side * own, own, gb[0:1, :], gb[4:5, :])


def qkv_kernel(prompt, idx, n1, w_own, w_oth, tables, out, raw):
    half, ctx = idx[1], idx[2]
    n1, w_own, w_oth = n1(), w_own(), w_oth()
    rows = n1.shape[0]
    own = rows // 2
    tables = tables()

    def place(start):
        if prompt:
            return ctx * own + start % own
        return tables.shape[1] - 128

    for which, scale in ((0, 1.0), (2, HEAD**-0.5)):
        normed_dots(n1, raw, half, w_own, w_oth, which)
        for start in range(0, rows, 128):
            turned = turn(raw[start : start + 128, :], place(start), tables, 1.0)
            out.ref[which, start : start + 128, :] = turned.astype(BF16) * BF16(scale)
    normed_dots(n1, raw, half, w_own, w_oth, 1)
    out.ref[1] = raw[...].astype(BF16)


def norm_pieces_kernel(idx, *refs):
    gb, out = refs[-2](), refs[-1]
    for i, x in enumerate(refs[:-2]):
        x = x()
        normed_rows(x, 0, out.ref, i * x.shape[0], x.shape[0], gb[0:1, :], gb[4:5, :])


def kv_kernel(blocks, idx, own_near, own_far, oth_near, oth_far, w_own, w_oth, tables, out, n1, raw):
    half, ctx, bit = idx[1], idx[2], idx[7]
    parts = [r() for r in (own_near, own_far, oth_near, oth_far)]
    tables = tables()
    w_own, w_oth = w_own(), w_oth()
    piece = parts[0].shape[0] // len(blocks)
    own = 2 * piece
    for i, block in enumerate(blocks):
        for place, x in zip((bit, 1 - bit, 2 + bit, 3 - bit), parts):
            n1[at(place * piece, piece), :] = x[i * piece : (i + 1) * piece, :]
        normed_dots(n1, raw, half, w_own, w_oth, 0)
        for start in range(0, 2 * own, 128):
            turned = turn(raw[start : start + 128, :], (ctx ^ block) * own + start % own, tables, 1.0)
            out.ref[2 * i, start : start + 128, :] = turned.astype(BF16)
        normed_dots(n1, raw, half, w_own, w_oth, 1)
        out.ref[2 * i + 1] = raw[...].astype(BF16)


def keys_values(near, two, one):
    near, two, one = near(), two(), one()
    return [near.at[0], two.at[0], two.at[2], one.at[0]], [near.at[1], two.at[1], two.at[3], one.at[1]]


def softmax_keys(scores):
    top = functools.reduce(jnp.maximum, [jnp.max(s, axis=0, keepdims=True) for s in scores])
    scores = [jnp.exp(s - top) for s in scores]
    inverse = 1.0 / sum(jnp.sum(s, axis=0, keepdims=True) for s in scores)
    return [(s * inverse).astype(BF16) for s in scores]


def prompt_kernel(idx, near, two, one, o_oth, o_own, p, vt, ot):
    ctx = idx[2]
    q = near().at[2]
    ks, vs = keys_values(near, two, one)
    own = o_own.ref.shape[0]
    width = q.shape[1]
    key = lax.broadcasted_iota(jnp.int32, (own, own), 0)
    row = lax.broadcasted_iota(jnp.int32, (own, own), 1)
    seen = key <= row
    for side, out in ((1, o_oth), (0, o_own)):
        rows = slice(side * own, (side + 1) * own)
        qt = q[rows, :].T
        for j in range(4):
            vt[:, j * own : (j + 1) * own] = vs[j][rows, :].T
        for head in range(width // HEAD):
            feats = slice(head * HEAD, (head + 1) * HEAD)
            qh = head_rows(qt, head)
            scores = []
            for j in range(4):
                part = nn(ks[j][rows, :], qh)
                if j == 0:
                    part = jnp.where(seen, part, MASKED)
                else:
                    part = part + jnp.where((ctx ^ j) < ctx, 0.0, MASKED).astype(F32)
                scores.append(part)
            for j, probs in enumerate(softmax_keys(scores)):
                p.ref[side, head, j * own : (j + 1) * own, :] = probs
            p.send(side, head)
            ot[feats, :] = nn(vt[feats, :], p.ref[side, head])
        out.ref[...] = ot[...].T.astype(BF16)
        out.send()


def cont_kernel(idx, mine_kvq, near, two, one, o_oth, o_own, p, vt, ot):
    mine_kvq = mine_kvq()
    k, v, q = (mine_kvq.at[i] for i in range(3))
    ks, vs = keys_values(near, two, one)
    own = o_own.ref.shape[0]
    width = q.shape[1]
    length = 128
    per = own // length
    key = lax.broadcasted_iota(jnp.int32, (length, 2 * length), 0)
    row = lax.broadcasted_iota(jnp.int32, (length, 2 * length), 1) % length
    seen = key <= row
    for c in [*range(per, 2 * per), *range(per)]:
        group = idx[3 + c]
        mine = slice(c * length, (c + 1) * length)
        theirs = at(group * own, own)
        qt = q[mine, :].T
        for j in range(4):
            vt[:, j * own : (j + 1) * own] = vs[j][theirs, :].T
        vt[:, 4 * own :] = v[mine, :].T
        for pair in range(width // HEAD // 2):
            feats = slice(pair * 2 * HEAD, (pair + 1) * 2 * HEAD)
            q2 = jnp.concatenate([head_rows(qt, 2 * pair), head_rows(qt, 2 * pair + 1)], axis=1)
            scores = [nn(ks[j][theirs, :], q2) for j in range(4)]
            scores.append(jnp.where(seen, nn(k[mine, :], q2), MASKED))
            probs = softmax_keys(scores)
            for j in range(4):
                p.ref[c, pair, j * own : (j + 1) * own, :] = probs[j]
            p.ref[c, pair, 4 * own :, :] = probs[4]
            p.send(c, pair)
            both = nn(vt[feats, :], p.ref[c, pair])
            first = pair * 2 * HEAD
            ot[first : first + HEAD, :] = both[:HEAD, :length]
            ot[first + HEAD : first + 2 * HEAD, :] = both[HEAD:, length:]
        out = o_own if c < per else o_oth
        place = c % per * length
        out.ref[place : place + length, :] = ot[...].T.astype(BF16)
        if c % per == per - 1:
            out.send()


def after_kernel(idx, w0, o0, w1, o1, w2, o2, w3, o3, x, gb, n3, z, x1):
    half = idx[1]
    part = z.ref.shape[1] // 2
    pairs = [(o(), w()) for o, w in ((o0, w0), (o1, w1), (o2, w2), (o3, w3))]
    for side in range(2):
        cols = at((half if side == 0 else 1 - half) * part, part)
        z.ref[:, cols] = sum(nn(o[...], w[side]) for o, w in pairs)
    z.send()
    x, gb = x(), gb()

    def one(rows):
        normed, _ = norm(z.ref[rows, :])
        after = x[rows, :].astype(F32) + (normed * gb[1:2, :] + gb[5:6, :])
        x1.ref[rows, :] = after
        normed, _ = norm(after)
        n3.ref[rows, :] = (normed * gb[2:3, :] + gb[6:7, :]).astype(BF16)

    tiles(x.shape[0], one)


def up_down_kernel(idx, n3o, wua, wub, n3t, wda, wdb, send, act, slope, keep):
    half = idx[1]
    own = n3o.ref.shape[0]
    part = n3o.ref.shape[1] // 2
    n3o, wua, wub = n3o(), wua(), wub()
    hidden = wua.shape[1]
    for side, n3 in enumerate((n3o, n3t)):
        if side == 1:
            n3 = n3()
        rows = slice(side * own, (side + 1) * own)
        for start in range(0, hidden, 256):
            cols = slice(start, start + 256)
            pre = nn(n3[:, at(half * part, part)], wua[:, cols]) + nn(
                n3[:, at((1 - half) * part, part)], wub[:, cols]
            )
            square = pre * pre
            tanh = jnp.tanh(GELU_COEF * (pre + 0.044715 * pre * square))
            up = 0.5 * (1.0 + tanh)
            act.ref[rows, cols] = (pre * up).astype(BF16)
            inner = GELU_COEF * (1.0 + (3.0 * 0.044715) * square)
            slope.ref[rows, cols] = (up + 0.5 * pre * (1.0 - tanh * tanh) * inner).astype(BF16)
        act.send(rows)
        slope.send(rows)
    weights = (wda(), wdb())
    for out, rows in ((send, slice(own, 2 * own)), (keep, slice(0, own))):
        for side, w in enumerate(weights):
            cols = at((half if side == 0 else 1 - half) * part, part)
            out.ref[:, cols] = nn(act.ref[rows, :], w[...]).astype(out.ref.dtype)
        out.send()


def last_kernel(idx, mine, theirs, x1, cotangent, gb, dm, y, grads):
    mine, theirs, cotangent, gb, x1 = mine(), theirs(), cotangent(), gb(), x1()
    grads.ref[...] = jnp.zeros_like(grads.ref)

    def one(rows):
        total = mine[rows, :].astype(F32) + theirs[rows, :].astype(F32)
        normed, inverse = norm(total)
        y.ref[rows, :] = (x1[rows, :] + (normed * gb[3:4, :] + gb[7:8, :])).astype(BF16)
        dy = cotangent[rows, :].astype(F32)
        dm.ref[rows, :] = norm_back(normed, inverse, dy, gb[3:4, :]).astype(BF16)
        grads.ref[0:1, :] += jnp.sum(dy * normed, axis=0, keepdims=True)
        grads.ref[1:2, :] += jnp.sum(dy, axis=0, keepdims=True)

    tiles(mine.shape[0], one)


def down_up_kernel(idx, dmo, wda, wdb, slope, dmt, wua, wub, send, du, keep):
    half = idx[1]
    own = dmo.ref.shape[0]
    part = dmo.ref.shape[1] // 2
    dmo, wda, wdb, slope = dmo(), wda(), wdb(), slope()
    for side, dm in enumerate((dmo, dmt)):
        if side == 1:
            dm = dm()
        rows = slice(side * own, (side + 1) * own)
        for start in range(0, slope.shape[1], 256):
            cols = slice(start, start + 256)
            back = nt(dm[:, at(half * part, part)], wda[cols, :]) + nt(
                dm[:, at((1 - half) * part, part)], wdb[cols, :]
            )
            du.ref[rows, cols] = (back * slope[rows, cols].astype(F32)).astype(BF16)
        du.send(rows)
    weights = (wua(), wub())
    for out, rows in ((send, slice(own, 2 * own)), (keep, slice(0, own))):
        for side, w in enumerate(weights):
            cols = at((half if side == 0 else 1 - half) * part, part)
            out.ref[:, cols] = nt(du.ref[rows, :], w[...]).astype(out.ref.dtype)
        out.send()


def middle_kernel(idx, mine, theirs, x1, cotangent, gb, z, dz, dx1, grads):
    mine, theirs, x1, cotangent, gb, z = mine(), theirs(), x1(), cotangent(), gb(), z()
    grads.ref[...] = jnp.zeros_like(grads.ref)

    def one(rows):
        back = mine[rows, :].astype(F32) + theirs[rows, :].astype(F32)
        normed, inverse = norm(x1[rows, :])
        grads.ref[1:2, :] += jnp.sum(back * normed, axis=0, keepdims=True)
        grads.ref[3:4, :] += jnp.sum(back, axis=0, keepdims=True)
        after = cotangent[rows, :].astype(F32) + norm_back(normed, inverse, back, gb[2:3, :])
        dx1.ref[rows, :] = after
        normed, inverse = norm(z[rows, :])
        grads.ref[0:1, :] += jnp.sum(after * normed, axis=0, keepdims=True)
        grads.ref[2:3, :] += jnp.sum(after, axis=0, keepdims=True)
        dz.ref[rows, :] = norm_back(normed, inverse, after, gb[1:2, :]).astype(BF16)

    tiles(mine.shape[0], one)


def spread_out(half, dzo, dzt, wo, do):
    own = dzo.shape[0]
    part = dzo.shape[1] // 2
    for side, dz in enumerate((dzo, dzt)):
        do[side * own : (side + 1) * own, :] = (
            nt(dz[:, at(half * part, part)], wo[0]) + nt(dz[:, at((1 - half) * part, part)], wo[1])
        ).astype(BF16)


def prompt_back_kernel(idx, dzo, dzt, wo, near, two, one, p, tables, o_own, o_oth, dkv, dq, grad_out, do, kt, dqt, dst):
    half, ctx = idx[1], idx[2]
    dzo, dzt, wo = dzo(), dzt(), wo()
    spread_out(half, dzo, dzt, wo, do)
    q = near().at[2]
    ks, vs = keys_values(near, two, one)
    p = p()
    tables = tables()
    own = dzo.shape[0]
    width = q.shape[1]
    heads = width // HEAD
    mixed = (o_own(), o_oth())
    for start in range(0, dzo.shape[1], 512):
        cols = slice(start, start + 512)
        grad_out.ref[:, cols] = tn(mixed[0][...], dzo[:, cols]) + tn(mixed[1][...], dzt[:, cols])
    grad_out.send()
    for side in range(2):
        rows = slice(side * own, (side + 1) * own)
        dot = do[rows, :].T
        for j in range(4):
            kt[:, j * own : (j + 1) * own] = ks[j][rows, :].T
        for head in range(heads):
            feats = slice(head * HEAD, (head + 1) * HEAD)
            doh = head_rows(dot, head)
            probs = [p[side, head, j * own : (j + 1) * own, :].astype(F32) for j in range(4)]
            terms = [probs[j] * nn(vs[j][rows, :], doh) for j in range(4)]
            centre = sum(jnp.sum(t, axis=0, keepdims=True) for t in terms)
            for j in range(4):
                dst[head, j * own : (j + 1) * own, :] = (terms[j] - probs[j] * centre).astype(BF16)
            dqt[feats, :] = nn(kt[feats, :], dst[head]) * (HEAD**-0.5)
        for j in range(4):
            keys = slice(j * own, (j + 1) * own)
            dkv.ref[j, 0, rows, :] = sum(
                nn(dst[head, keys, :], head_lanes(q[rows, :], head)) for head in range(heads)
            )
            dkv.ref[j, 1, rows, :] = sum(
                nn(p[side, head, keys, :], head_lanes(do[rows, :], head)) for head in range(heads)
            )
        dqf = dqt[...].T
        for start in range(0, own, 128):
            dq.ref[side * own + start : side * own + start + 128, :] = turn(
                dqf[start : start + 128, :], ctx * own + start, tables, -1.0
            ).astype(BF16)


def cont_back_kernel(idx, dzo, dzt, wo, mine_kvq, near, two, one, p, adds, tables, o_own, o_oth, grad_out, *refs):
    outs = refs[:4]
    send, keep, dkvq = refs[4:7]
    do, kt, dqt, dst = refs[7:]
    half = idx[1]
    dzo, dzt, wo = dzo(), dzt(), wo()
    spread_out(half, dzo, dzt, wo, do)
    mine_kvq = mine_kvq()
    k, v, q = (mine_kvq.at[i] for i in range(3))
    ks, vs = keys_values(near, two, one)
    p, total = p(), adds()
    tables = tables()
    own = dzo.shape[0]
    width = q.shape[1]
    pairs = width // HEAD // 2
    length = 128
    last = tables.shape[1] - length
    mixed, grad_out = (o_own(), o_oth()), grad_out()
    part = dzo.shape[1] // 2
    for out, where in ((send, 1 - half), (keep, half)):
        cols = at(where * part, part)
        out.ref[...] = (
            grad_out[:, cols] + (tn(mixed[0][...], dzo[:, cols]) + tn(mixed[1][...], dzt[:, cols]))
        ).astype(BF16)
    for c in range(2 * own // length):
        group = idx[3 + c]
        mine = slice(c * length, (c + 1) * length)
        theirs = at(group * own, own)
        dot = do[mine, :].T
        for j in range(4):
            kt[:, j * own : (j + 1) * own] = ks[j][theirs, :].T
        kt[:, 4 * own :] = k[mine, :].T
        for pair in range(pairs):
            feats = slice(pair * 2 * HEAD, (pair + 1) * 2 * HEAD)
            do2 = jnp.concatenate([head_rows(dot, 2 * pair), head_rows(dot, 2 * pair + 1)], axis=1)
            probs = [p[c, pair, j * own : (j + 1) * own, :].astype(F32) for j in range(4)]
            probs.append(p[c, pair, 4 * own :, :].astype(F32))
            terms = [probs[j] * nn(vs[j][theirs, :], do2) for j in range(4)]
            terms.append(probs[4] * nn(v[mine, :], do2))
            centre = sum(jnp.sum(t, axis=0, keepdims=True) for t in terms)
            for j in range(4):
                dst[pair, j * own : (j + 1) * own, :] = (terms[j] - probs[j] * centre).astype(BF16)
            dst[pair, 4 * own :, :] = (terms[4] - probs[4] * centre).astype(BF16)
            both = nn(kt[feats, :], dst[pair]) * (HEAD**-0.5)
            first = pair * 2 * HEAD
            dqt[first : first + HEAD, :] = both[:HEAD, :length]
            dqt[first + HEAD : first + 2 * HEAD, :] = both[HEAD:, length:]
        q2, do2 = (
            [
                jnp.concatenate([head_lanes(t[mine, :], 2 * r), head_lanes(t[mine, :], 2 * r + 1)], axis=0)
                for r in range(pairs)
            ]
            for t in (q, do)
        )
        for j in range(4):
            keys = slice(j * own, (j + 1) * own)
            total[j, 0, theirs, :] += sum(nn(dst[r, keys, :], q2[r]) for r in range(pairs))
            total[j, 1, theirs, :] += sum(nn(p[c, r, keys, :], do2[r]) for r in range(pairs))
        dkf = sum(nn(dst[r, 4 * own :, :], q2[r]) for r in range(pairs))
        dkvq.ref[1, mine, :] = sum(nn(p[c, r, 4 * own :, :], do2[r]) for r in range(pairs)).astype(BF16)
        dkvq.ref[0, mine, :] = turn(dkf, last, tables, -1.0).astype(BF16)
        dkvq.ref[2, mine, :] = turn(dqt[...].T, last, tables, -1.0).astype(BF16)
    for j in (3, 2, 1, 0):
        outs[j].ref[...] = total[j].astype(BF16)
        outs[j].send()


def unturn_kernel(idx, own_kv, one, two, tables, dkv):
    ctx = idx[2]
    parts = [r() for r in (own_kv, one, two)]
    tables = tables()
    rows = dkv.ref.shape[1]
    own = rows // 2
    for start in range(0, rows, 128):
        r = slice(start, start + 128)
        total = sum(part[0, r, :].astype(F32) for part in parts)
        dkv.ref[0, r, :] = turn(total, ctx * own + start % own, tables, -1.0).astype(BF16)
    dkv.ref[1] = sum(part[1].astype(F32) for part in parts).astype(BF16)


def parts_of(*refs):
    first = refs[0]()
    if len(refs) == 1:
        return [first.at[i] for i in range(3)]
    return [first.at[0], first.at[1], refs[1]()]


def input_kernel(count, idx, *refs):
    half = idx[1]
    grads = parts_of(*refs[:count])
    w_own, w_oth, send, keep = refs[count:]
    weights = (w_own(), w_oth())
    local = grads[0].shape[1]
    own = keep.ref.shape[0]
    part = keep.ref.shape[1] // 2
    for out, rows in ((send, slice(own, 2 * own)), (keep, slice(0, own))):
        for side, w in enumerate(weights):
            cols = at((half if side == 0 else 1 - half) * part, part)
            total = sum(nt(d[rows, :], w[:, i * local : (i + 1) * local]) for i, d in enumerate(grads))
            out.ref[:, cols] = total.astype(out.ref.dtype)
        out.send()


def first_kernel(idx, mine, theirs, x, gb, dx1, dx, grads):
    mine, theirs, x, gb, dx1 = mine(), theirs(), x(), gb(), dx1()
    grads.ref[...] = jnp.zeros_like(grads.ref)

    def one(rows):
        back = mine[rows, :].astype(F32) + theirs[rows, :].astype(F32)
        normed, inverse = norm(x[rows, :].astype(F32))
        grads.ref[0:1, :] += jnp.sum(back * normed, axis=0, keepdims=True)
        grads.ref[1:2, :] += jnp.sum(back, axis=0, keepdims=True)
        dx.ref[rows, :] = (dx1[rows, :] + norm_back(normed, inverse, back, gb[0:1, :])).astype(BF16)

    tiles(mine.shape[0], one)


def cut_right(idx, pairs, send, keep):
    half = idx[1]
    part = send.ref.shape[1]
    for out, where in ((send, 1 - half), (keep, half)):
        cols = at(where * part, part)
        for start in range(0, out.ref.shape[0], 256):
            feats = slice(start, start + 256)
            out.ref[feats, :] = sum(tn(left[rows, feats], right[:, cols]) for left, rows, right in pairs).astype(
                BF16
            )
        out.send()


def grad_down_kernel(idx, act_a, act_b, a0, a1, b0, b1, send, keep):
    pairs = []
    for act, rights in ((act_a(), (a0, a1)), (act_b(), (b0, b1))):
        for i, right in enumerate(rights):
            right = right()
            own = right.shape[0]
            pairs.append((act, slice(i * own, (i + 1) * own), right))
    cut_right(idx, pairs, send, keep)


def grad_up_kernel(idx, a0, a1, b0, b1, du_a, du_b, send, keep):
    half = idx[1]
    lefts = [r() for r in (a0, a1, b0, b1)]
    rights = (du_a(), du_b())
    own = lefts[0].shape[0]
    part = send.ref.shape[0]
    for out, where in ((send, 1 - half), (keep, half)):
        for start in range(0, part, 256):
            feats = at(where * part + start, 256)
            for col in range(0, rights[0].shape[1], 512):
                out.ref[start : start + 256, col : col + 512] = sum(
                    tn(left[:, feats], rights[i // 2][(i % 2) * own : (i % 2 + 1) * own, col : col + 512])
                    for i, left in enumerate(lefts)
                ).astype(BF16)
        out.send()


def grad_qkv_kernel(idx, n1a, n1b, dkv_p, dq_p, dkvq_c, send, keep):
    half = idx[1]
    lefts = (n1a(), n1b())
    rights = (parts_of(dkv_p, dq_p), parts_of(dkvq_c))
    part = send.ref.shape[0]
    local = rights[0][0].shape[1]
    for out, where in ((send, 1 - half), (keep, half)):
        for start in range(0, part, 256):
            feats = at(where * part + start, 256)
            for i in range(3):
                out.ref[start : start + 256, i * local : (i + 1) * local] = sum(
                    tn(left[:, feats], right[i][...]) for left, right in zip(lefts, rights)
                ).astype(BF16)
        out.send()


def over_shard_kernel(idx, keep, came, send, mine):
    ctx = idx[2]
    keep, came = keep(), came()
    rows = keep.shape[0] // 4
    for out, order in ((send, (1, 3)), (mine, (0, 2))):
        for place, j in enumerate(order):
            r = at((ctx ^ j) * rows, rows)
            out.ref[place] = (keep[r, :].astype(F32) + came[r, :].astype(F32)).astype(BF16)


def over_shard_two_kernel(idx, keep, came, keep_out, came_out, send, mine):
    ctx = idx[2]
    keep, came, keep_out, came_out = keep(), came(), keep_out(), came_out()
    rows, few = keep.shape[0] // 4, keep_out.shape[0] // 4
    width, half = keep.shape[1], keep_out.shape[1] // 2
    for out, order in ((send, (1, 3)), (mine, (0, 2))):
        for place, j in enumerate(order):
            r, f = at((ctx ^ j) * rows, rows), at((ctx ^ j) * few, few)
            out.ref[place, :, :width] = (keep[r, :].astype(F32) + came[r, :].astype(F32)).astype(BF16)
            total = (keep_out[f, :].astype(F32) + came_out[f, :].astype(F32)).astype(BF16)
            out.ref[place, :few, width:] = total[:, :half]
            out.ref[place, few:, width:] = total[:, half:]


def near_kernel(idx, mine, came, send, keep):
    mine, came = mine(), came()
    send.ref[...] = (mine[1].astype(F32) + came[1].astype(F32)).astype(BF16)
    keep.ref[...] = mine[0].astype(F32) + came[0].astype(F32)


def far_kernel(idx, keep, came, total):
    total.ref[...] = (keep()[...] + came()[...].astype(F32)).astype(BF16)


def place_kernel(idx, q0, q1, q2, q3, out):
    ctx = idx[2]
    for j, quarter in enumerate((q0, q1, q2, q3)):
        quarter = quarter()
        out.ref[at((ctx ^ j) * quarter.shape[0], quarter.shape[0]), :] = quarter[...].astype(F32)


def place_two_kernel(idx, q0, q1, q2, q3, key, value, query, proj):
    ctx = idx[2]
    local = key.ref.shape[1]
    few, half = proj.ref.shape[0] // 4, proj.ref.shape[1] // 2
    for j, quarter in enumerate((q0, q1, q2, q3)):
        quarter = quarter()
        rows = at((ctx ^ j) * quarter.shape[0], quarter.shape[0])
        for i, out in enumerate((key, value, query)):
            out.ref[rows, :] = quarter[:, i * local : (i + 1) * local].astype(F32)
        rows = at((ctx ^ j) * few, few)
        proj.ref[rows, :half] = quarter[:few, 3 * local :].astype(F32)
        proj.ref[rows, half:] = quarter[few:, 3 * local :].astype(F32)


def whole_kernel(idx, *refs):
    core = idx[0]
    count = len(refs) // 3
    for i in range(count):
        out = refs[2 * count + i]
        for j, part in enumerate(refs[2 * i : 2 * i + 2]):
            part = part()
            rows = at((core if j == 0 else 1 - core) * part.shape[0], part.shape[0])
            out.ref[rows, :] = part[...]
        out.send()


def sum_kernel(idx, keep, came, total):
    keep, came = keep(), came()
    total.ref[...] = (keep[...] + came[...].astype(F32)).astype(BF16)


def add_kernel(idx, one, two, total):
    total.ref[...] = (one()[...].astype(F32) + two()[...].astype(F32)).astype(BF16)


def small_kernel(idx, first_a, first_b, mid_a, mid_b, last_a, last_b, out):
    first, mid, last = (a()[...] + b()[...] for a, b in ((first_a, first_b), (mid_a, mid_b), (last_a, last_b)))
    out.ref[0:1, :] = first[0:1, :]
    out.ref[1:3, :] = mid[0:2, :]
    out.ref[3:4, :] = last[0:1, :]
    out.ref[4:5, :] = first[1:2, :]
    out.ref[5:7, :] = mid[2:4, :]
    out.ref[7:8, :] = last[1:2, :]


def rope_tables(length):
    freqs = ROPE_BASE ** (-np.arange(HEAD // 2, dtype=np.float32) * np.float32(2.0 / HEAD))
    theta = np.arange(length, dtype=np.float32)[:, None] * freqs.astype(np.float32)[None, :]
    cosine, sine = np.cos(theta), np.sin(theta)
    none = np.zeros_like(sine)
    pairs = ((cosine, cosine), (-sine, none), (none, sine))
    return jnp.asarray(np.stack([np.tile(np.concatenate(pair, axis=1), (1, 2)) for pair in pairs]).astype(np.float32))


def swap(value, axis, bit):
    size = lax.axis_size(axis)
    return lax.ppermute(value, axis, [(i, i ^ bit) for i in range(size)])


class Reduction:
    def __init__(self, line, sends, keeps, dims):
        self.line, self.keeps = line, keeps
        self.pair = lax.axis_size("shard") == 2
        self.sends, self.dims = sends, dims
        self.came = [None] * len(keeps)

    def start(self, i=0, *with_these):
        if self.pair:
            self.came[i] = swap(self.line.after(self.sends[i]), "shard", 1)

    def arrived(self, i=0):
        if self.pair:
            self.came[i] = self.line.after(self.came[i])

    def over_shard(self):
        if not self.pair:
            self.total = []
            for send, keep, dim in zip(self.sends, self.keeps, self.dims):
                full = jnp.concatenate([keep, send], axis=dim)
                part = lax.psum_scatter(full, "shard", scatter_dimension=dim, tiled=True)
                self.total.append(lax.psum(part, "ctx").astype(F32))
            return
        rows, width = self.keeps[0].shape
        if len(self.keeps) > 1:
            width += self.keeps[1].size // rows
        pairs = [value for pair in zip(self.keeps, self.came) for value in pair]
        send, self.mine = self.line.call(
            over_shard_two_kernel if len(self.keeps) > 1 else over_shard_kernel,
            pairs,
            [((2, rows // 4, width), BF16)] * 2,
            name="over_shard",
        )
        self.moving = swap(send, "ctx", 1)

    def near(self):
        if self.pair:
            shape = self.mine.shape[1:]
            send, self.keep = self.line.call(
                near_kernel, [self.mine, self.moving], [(shape, BF16), (shape, F32)], name="near"
            )
            self.moving = swap(send, "ctx", 2)

    def far(self):
        if self.pair:
            (self.q0,) = self.line.call(
                far_kernel, [self.keep, self.moving], [(self.keep.shape, BF16)], name="far"
            )
            self.q2, self.q1 = swap(self.q0, "ctx", 2), swap(self.q0, "ctx", 1)

    def last(self):
        if self.pair:
            self.q2 = self.line.after(self.q2)
            self.q3 = swap(self.q2, "ctx", 1)

    def placed(self):
        if not self.pair:
            if len(self.keeps) == 1:
                return self.total
            return [*jnp.split(self.total[0], 3, axis=1), self.total[1]]
        rows, width = self.keeps[0].shape
        outs, kernel = [((rows, width), F32)], place_kernel
        if len(self.keeps) > 1:
            outs = [((rows, width // 3), F32)] * 3 + [(self.keeps[1].shape, F32)]
            kernel = place_two_kernel
        return self.line.call(kernel, [self.q0, self.q1, self.q2, self.q3], outs, name="place")


def per_device(
    prompt_x,
    cont_x,
    owner,
    w_query,
    w_key,
    w_value,
    w_out,
    w_up,
    w_down,
    ln_gain,
    ln_bias,
    prompt_grad,
    cont_grad,
):
    shards = lax.axis_size("shard")
    groups, block, width = prompt_x.shape
    conts, cont_len, _ = cont_x.shape
    local = w_query.shape[1]
    hidden = w_up.shape[1]
    rows = groups * block
    own = rows // 2
    piece = own // 2
    part = width // 2
    prompt_len = block * lax.axis_size("ctx")
    core = lax.axis_index("tp") % 2
    bit = lax.axis_index("tp") // 2
    shard = lax.axis_index("shard")
    ctx = lax.axis_index("ctx")
    xs = (prompt_x.reshape(rows, width), cont_x.reshape(rows, width))
    dys = (prompt_grad.reshape(rows, width), cont_grad.reshape(rows, width))

    def both(weight, dim):
        if shards == 2:
            return weight, swap(weight, "shard", 1)
        full = lax.all_gather(weight, "shard", axis=dim, tiled=True)
        return tuple(jnp.split(full, 2, axis=dim))

    half = shard if shards == 2 else jnp.zeros_like(shard)
    which = (owner - shard * groups).reshape(2, conts // 2)
    which = jnp.where(core == 1, which[::-1], which) ^ core
    idx = jnp.concatenate([jnp.stack([core, half, ctx]), which.reshape(conts), jnp.stack([bit])])
    line = Line(idx.astype(jnp.int32))

    small = both(jnp.concatenate([ln_gain, ln_bias], axis=0), 1)
    (gb,) = line.call(gains_kernel, list(small), [((8, width), F32)], name="gains")
    packed = jnp.concatenate([w_key, w_value, w_query], axis=1)
    if shards == 2:
        (packed,) = line.call(
            pack_kernel, [w_key, w_value, w_query], [((part, 3 * local), BF16)], name="pack"
        )
    wqkv = both(packed, 0)
    quarter = lax.dynamic_slice_in_dim(xs[0], core * own + bit * piece, piece, 0)
    far, near = swap(quarter, "ctx", 2), swap(quarter, "ctx", 1)
    tables = rope_tables(prompt_len + cont_len)

    wo = both(line.after(w_out), 1)
    n1p, n1c = (
        line.call(normed_kernel, [x, gb], [((rows, width), BF16)], name="norm_first")[0] for x in xs
    )
    wide_rows = (rows, local)
    raw = pltpu.VMEM(wide_rows, F32)
    chunks = []
    for prompt in (True, False):
        chunks += line.call(
            functools.partial(qkv_kernel, prompt),
            [n1p if prompt else n1c, *wqkv, tables],
            [((3, *wide_rows), BF16)],
            [raw],
            name="qkv_prompt" if prompt else "qkv_cont",
        )
        if prompt:
            (normed,) = line.call(norm_pieces_kernel, [near, far, gb], [((own, width), BF16)], name="norm_pieces")
            both_near = [normed, swap(normed, "tp", 2)]
            far, w_up = line.after(far, w_up)
            last_near = swap(far, "ctx", 1)
            wu = both(w_up, 0)
    kvq_p, kvq_c = chunks
    (wo0,) = line.call(stack_kernel, wo, [((2, *wo[0].shape), BF16)], name="stack_out")
    both_near.append(swap(line.after(normed), "tp", 1))
    (normed,) = line.call(norm_pieces_kernel, [last_near, gb], [((piece, width), BF16)], name="norm_piece")
    one_near = [normed, swap(normed, "tp", 2), swap(normed, "tp", 1)]
    both_near[1] = line.after(both_near[1])
    both_near.append(swap(both_near[1], "tp", 1))
    seen = [kvq_p]

    def far_keys(blocks, parts):
        seen.extend(
            line.call(
                functools.partial(kv_kernel, blocks),
                [*parts, *wqkv, tables],
                [((2 * len(blocks), *wide_rows), BF16)],
                [pltpu.VMEM((rows, width), BF16), raw],
                name="far_keys",
            )
        )

    far_keys((1, 2), both_near)
    wo0 = line.after(wo0)
    wo2, wo1 = swap(wo0, "tp", 2), swap(wo0, "tp", 1)
    one_near[1] = line.after(one_near[1])
    one_near.append(swap(one_near[1], "tp", 1))
    far_keys((3,), one_near)

    half_o = ((own, local), BF16)
    o_oth_p, o_own_p, probs_p = line.call(
        prompt_kernel,
        seen,
        [half_o, half_o, ((2, local // HEAD, prompt_len, own), BF16, "far")],
        [pltpu.VMEM((local, prompt_len), BF16), pltpu.VMEM((local, own), F32)],
        name="attend_prompt",
    )
    wo1, wo2, *wu, w_down = line.after(wo1, wo2, *wu, w_down)
    wo3 = swap(wo2, "tp", 1)
    wd = both(w_down, 1)
    pairs = local // HEAD // 2
    mixed = [(o_own_p, o_oth_p)]

    def gathered(o_own, o_oth):
        return o_own, swap(o_oth, "tp", 1), swap(o_own, "tp", 2), swap(o_oth, "tp", 3)

    full_o = [gathered(o_own_p, o_oth_p)]
    all_len = prompt_len + cont_len
    o_oth_c, o_own_c, probs_c = line.call(
        cont_kernel,
        [kvq_c, *seen],
        [half_o, half_o, ((conts, pairs, all_len, 2 * cont_len), BF16, "far")],
        [pltpu.VMEM((local, all_len), BF16), pltpu.VMEM((local, cont_len), F32)],
        name="attend_cont",
    )
    mixed.append((o_own_c, o_oth_c))
    full_o.append(gathered(o_own_c, o_oth_c))

    def mine(value):
        return Part(value, own, lambda idx: idx[0] * own)

    own_rows, own_rows_f = ((own, width), BF16), ((own, width), F32)
    own_pieces = (*own_rows, "cut")

    def swapped(pieces):
        return [swap(piece, "tp", 1) for piece in pieces]

    def summed(keep, send):
        came = swapped(send)
        (total,) = line.call(sum_kernel, [keep, came], [own_rows], name="sum_cores")
        return total, swap(total, "tp", 2)

    stage = []
    for x, os in zip(xs, full_o):
        n3, z, x1 = line.call(
            after_kernel,
            [wo0, os[0], wo1, os[1], wo2, os[2], wo3, os[3], mine(x), gb],
            [own_pieces, own_rows_f, own_rows_f],
            name="after_attention",
        )
        n3t = swapped(n3)
        send, act, slope, keep = line.call(
            up_down_kernel,
            [n3, *wu, n3t, *wd],
            [own_pieces, ((rows, hidden), BF16), ((rows, hidden), BF16), own_rows_f],
            name="up_down",
        )
        stage.append((z, x1, n3, n3t, act, slope, *summed(keep, send)))

    later = []
    for i, dy in enumerate(dys):
        z, x1, n3, n3t, act, slope, total, theirs = stage[i]
        dm, y, grads_last = line.call(
            last_kernel,
            [total, theirs, x1, mine(dy), gb],
            [own_pieces, own_rows, ((2, width), F32)],
            name="last_norm",
        )
        dmt = swapped(dm)
        send, du, keep = line.call(
            down_up_kernel,
            [dm, *wd, slope, dmt, *wu],
            [own_pieces, ((rows, hidden), BF16), own_rows_f],
            name="down_up",
        )
        later.append((y, dm, dmt, du, *summed(keep, send), grads_last))

    middle = []

    def middle_norms(i):
        z, x1 = stage[i][:2]
        total, theirs = later[i][4:6]
        dz, dx1, grads_middle = line.call(
            middle_kernel,
            [total, theirs, x1, mine(dys[i]), gb, z],
            [own_pieces, own_rows_f, ((4, width), F32)],
            name="middle_norms",
        )
        middle.append((dx1, dz, swapped(dz), grads_middle))

    y_p, y_c = later[0][0], later[1][0]

    def assembled(*pairs):
        return line.call(
            whole_kernel,
            [value for pair in pairs for value in pair],
            [((rows, width), BF16)] * len(pairs),
            name="whole",
        )

    middle_norms(0)
    send, keep = line.call(
        grad_down_kernel,
        [stage[0][4], stage[1][4], *later[0][1:3], *later[1][1:3]],
        [((hidden, part), BF16)] * 2,
        name="grad_down",
    )
    down = Reduction(line, [send], [keep], (1,))
    down.start()
    pair_rows = (2, *wide_rows)
    grads, dqp, grad_out = line.call(
        prompt_back_kernel,
        [*middle[0][1:3], *[Far(a) for a in (wo0, *seen, probs_p)], tables, *[Far(o) for o in mixed[0]]],
        [((4, *pair_rows), F32, "far"), (wide_rows, BF16), ((local, width), F32, "far")],
        [
            pltpu.VMEM(wide_rows, BF16),
            pltpu.VMEM((local, prompt_len), BF16),
            pltpu.VMEM((local, own), F32),
            pltpu.VMEM((local // HEAD, prompt_len, own), BF16),
        ],
        name="attend_prompt_back",
    )
    send, keep = line.call(
        grad_up_kernel,
        [*stage[0][2:4], *stage[1][2:4], later[0][3], later[1][3]],
        [((part, hidden), BF16)] * 2,
        name="grad_up",
    )
    middle_norms(1)
    down.over_shard()
    up = Reduction(line, [send], [keep], (0,))
    up.start()
    *grads, send_out, keep_out, dkvq_c = line.call(
        cont_back_kernel,
        [*middle[1][1:3], *[Far(a) for a in (wo0, kvq_c, *seen, probs_c, grads)], tables]
        + [*[Far(o) for o in mixed[1]], Far(grad_out)],
        [(pair_rows, BF16)] * 4 + [((local, part), BF16)] * 2 + [((3, *wide_rows), BF16)],
        [
            pltpu.VMEM(wide_rows, BF16),
            pltpu.VMEM((local, all_len), BF16),
            pltpu.VMEM((local, cont_len), F32),
            pltpu.VMEM((pairs, all_len, 2 * cont_len), BF16),
        ],
        name="attend_cont_back",
    )
    kv3 = swap(grads[3], "ctx", 1)
    dx = []
    firsts = []

    def input_back(gradient):
        send, keep = line.call(
            functools.partial(input_kernel, len(gradient)),
            [*gradient, *[Far(w) for w in wqkv]],
            [own_pieces, own_rows_f],
            name="input_back",
        )
        return keep, send

    def first_norm(i, pair):
        out, grads_first = line.call(
            first_kernel,
            [*pair, mine(xs[i]), gb, Far(middle[i][0])],
            [own_rows, ((2, width), F32)],
            name="first_norm",
        )
        dx.append(out)
        firsts.append(grads_first)

    down.near()
    totals_c = summed(*input_back((dkvq_c,)))
    down.far()
    up.arrived()
    (kv2,) = line.call(add_kernel, [grads[2], kv3], [(pair_rows, BF16)], name="add_kv")
    kv2, kv1 = swap(kv2, "ctx", 2), swap(line.after(grads[1]), "ctx", 1)
    qkv = Reduction(line, [None, send_out], [None, keep_out], (0, 1))
    qkv.start(1)
    first_norm(1, totals_c)
    qkv.arrived(1)
    (dkv_p,) = line.call(
        unturn_kernel, [grads[0], kv1, kv2, tables], [(pair_rows, BF16)], name="unturn"
    )
    qkv.sends[0], qkv.keeps[0] = line.call(
        grad_qkv_kernel,
        [Far(n1p), Far(n1c), dkv_p, Far(dqp), Far(dkvq_c)],
        [((part, 3 * local), BF16)] * 2,
        name="grad_qkv",
    )
    qkv.start(0)
    up.over_shard()
    totals_p = summed(*input_back((dkv_p, Far(dqp))))
    up.near()
    down.last()
    up.far()
    qkv.over_shard()
    first_norm(0, totals_p)
    (small,) = line.call(
        small_kernel,
        [firsts[1], firsts[0], middle[0][3], middle[1][3], later[0][6], later[1][6]],
        [((8, width), F32)],
        name="small",
    )
    small = small + swap(small, "tp", 1)
    up.last()
    qkv.near()
    small = line.after(small)
    if shards == 2:
        small = lax.dynamic_slice_in_dim(small, shard * part, part, 1) + swap(
            lax.dynamic_slice_in_dim(small, (1 - shard) * part, part, 1), "shard", 1
        )
    else:
        small = lax.psum_scatter(small, "shard", scatter_dimension=1, tiled=True)
    (grad_down,) = down.placed()
    qkv.far()
    small = line.after(small)
    small = small + swap(small, "ctx", 1)
    halves = line.after(y_p, y_c, dx[1], dx[0])
    others = [swap(value, "tp", 1) for value in halves]
    (grad_up,) = up.placed()
    small = line.after(small)
    small = small + swap(small, "ctx", 2)
    yp, yc, dxp, dxc = assembled(*zip(halves, others))
    qkv.last()
    grad_key, grad_value, grad_query, grad_out = qkv.placed()
    return (
        yp.reshape(prompt_x.shape),
        yc.reshape(cont_x.shape),
        dxp.reshape(prompt_x.shape),
        dxc.reshape(cont_x.shape),
        grad_query,
        grad_key,
        grad_value,
        grad_out,
        grad_up,
        grad_down,
        small[:4],
        small[4:],
    )


def solution(mesh):
    placed = (
        P("shard", "ctx", None),
        P(("shard", "ctx"), None, None),
        P(("shard", "ctx")),
        P("shard", "tp"),
        P("shard", "tp"),
        P("shard", "tp"),
        P("tp", "shard"),
        P("shard", "tp"),
        P("tp", "shard"),
        P(None, "shard"),
        P(None, "shard"),
        P("shard", "ctx", None),
        P(("shard", "ctx"), None, None),
    )
    rows = (P("shard", "ctx", None), P(("shard", "ctx"), None, None))
    return jax.shard_map(
        per_device,
        mesh=mesh,
        in_specs=placed,
        out_specs=rows + rows + placed[3:11],
        check_vma=False,
    )
```

```python
import functools

import jax
import jax.numpy as jnp
import numpy as np
from jax import lax
from jax.experimental import pallas as pl
from jax.experimental.pallas import tpu as pltpu
from jax.sharding import PartitionSpec as P

F32 = jnp.float32
BF16 = jnp.bfloat16
HEAD = 64
EPSILON = 1e-05
ROPE_BASE = 10000.0
GELU_COEF = 0.7978845608028654
MASKED = -1e30
MIB = 1024 * 1024
TILE = 128
TILE = 128
TILE = 128
TILE = 128
TILE = 128
TILE = 128
TILE = 128
TILE = 128


def nn(left, right):
    return jnp.dot(left, right, preferred_element_type=F32)


def nt(left, right):
    return lax.dot_general(left, right, (((1,), (1,)), ((), ())), preferred_element_type=F32)


def tn(left, right):
    return lax.dot_general(left, right, (((0,), (0,)), ((), ())), preferred_element_type=F32)


def mean(value):
    return jnp.mean(value, axis=-1, keepdims=True)


def norm(value):
    centred = value - mean(value)
    inverse = lax.rsqrt(mean(centred * centred) + EPSILON)
    return centred * inverse, inverse


def norm_back(normed, inverse, cotangent, gain):
    scaled = cotangent * gain
    return (scaled - mean(scaled) - normed * mean(scaled * normed)) * inverse


def tiles(count, body):
    @pl.loop(0, count // TILE)
    def _(step):
        body(at(step * TILE, TILE))


def at(start, size):
    return pl.ds(pl.multiple_of(start, size), size)


def turn(value, start, tables, sign):
    rows, width = value.shape
    cosine, minus, plus = (
        jnp.concatenate([tables[i, at(start, rows), :]] * (width // 128), axis=1) for i in range(3)
    )
    left = pltpu.roll(value, width - HEAD // 2, 1)
    right = pltpu.roll(value, HEAD // 2, 1)
    return value * cosine + sign * (left * minus + right * plus)


def head_rows(value, head, count=1):
    which = lax.broadcasted_iota(jnp.int32, value.shape, 0) // (HEAD * count)
    return jnp.where(which == head, value, jnp.zeros_like(value))


def head_lanes(value, head):
    which = lax.broadcasted_iota(jnp.int32, value.shape, 1) // HEAD
    return jnp.where(which == head, value, jnp.zeros_like(value))


class Part:
    def __init__(self, array, rows, start):
        self.array, self.rows, self.start = array, rows, start
        self.shape, self.dtype = array.shape, array.dtype


class Far:
    def __init__(self, array):
        self.array = array
        self.shape, self.dtype = array.shape, array.dtype


class Stack:
    def __init__(self, arrays):
        self.arrays = list(arrays)
        self.rows = [a.shape[0] for a in arrays]
        self.shape, self.dtype = (sum(self.rows), *arrays[0].shape[1:]), arrays[0].dtype


class Coming:
    def __init__(self, ref, copy=None, pieces=()):
        self.ref, self.copy, self.pieces = ref, copy, pieces

    def __call__(self):
        if self.copy is not None:
            self.copy.wait()
            self.copy = None
        start = 0
        for piece, rows in self.pieces:
            self.ref[start : start + rows, :] = piece[...]
            start += rows
        self.pieces = ()
        return self.ref


class Going:
    def __init__(self, ref, kind, targets, semaphores):
        self.ref, self.kind, self.targets, self.semaphores = ref, kind, targets, semaphores
        self.copies = []

    def send(self, *index):
        if self.kind == "far":
            where = index if index else Ellipsis
            copy = pltpu.make_async_copy(self.ref.at[where], self.targets[0].at[where], next(self.semaphores))
            copy.start()
            self.copies.append(copy)

    def close(self):
        if self.kind == "cut":
            start = 0
            for target in self.targets:
                rows = target.shape[0]
                target[...] = self.ref[start : start + rows, :]
                start += rows
        elif not self.copies:
            self.send()
        for copy in self.copies:
            copy.wait()


SENDS = 40
PIECES = 3


def pieces_of(rows):
    tiles_of = rows // 16
    return [16 * (tiles_of // PIECES + (i < tiles_of % PIECES)) for i in range(PIECES)]


class Line:
    def __init__(self, idx):
        self.idx = idx

    def after(self, *values):
        *values, self.idx = lax.optimization_barrier((*values, self.idx))
        return values[0] if len(values) == 1 else values

    def call(self, kernel, inputs, outputs, scratch=(), name=None, margin=12):
        inputs = [Stack(a) if isinstance(a, list) else a for a in inputs]
        given = []
        for a in inputs:
            given += a.arrays if isinstance(a, Stack) else [a.array if isinstance(a, (Part, Far)) else a]
        places = [
            pl.BlockSpec(memory_space=pl.ANY if isinstance(a, Far) else pltpu.VMEM)
            for a in inputs
            for _ in (a.arrays if isinstance(a, Stack) else [a])
        ]
        kinds = [out[2] if len(out) > 2 else "" for out in outputs]
        pieces = [pieces_of(out[0][0]) if kind == "cut" else [out[0][0]] for out, kind in zip(outputs, kinds)]
        shapes = [
            jax.ShapeDtypeStruct((rows, *out[0][1:]), out[1]) for out, cuts in zip(outputs, pieces) for rows in cuts
        ]
        out_places = [
            pl.BlockSpec(memory_space=pl.ANY if kind == "far" else pltpu.VMEM)
            for kind, cuts in zip(kinds, pieces)
            for _ in cuts
        ]
        held = [pltpu.VMEM(a.shape, a.dtype) for a in inputs if isinstance(a, (Far, Stack))]
        held += [pltpu.VMEM(out[0], out[1]) for out, kind in zip(outputs, kinds) if kind]
        own = [*held, *scratch]
        size = sum(int(np.prod(a.shape)) * np.dtype(a.dtype).itemsize for a in own)

        def body(*refs):
            refs = list(refs)
            idx = refs.pop(0)
            sources = [refs.pop(0) for _ in given]
            targets = [refs.pop(0) for _ in shapes]
            semaphores = refs.pop()
            free = (semaphores.at[i] for i in range(SENDS))
            coming = []
            for value in inputs:
                if isinstance(value, Stack):
                    buffer = refs.pop(0)
                    coming.append(Coming(buffer, pieces=[(sources.pop(0), rows) for rows in value.rows]))
                    continue
                source, copy = sources.pop(0), None
                if isinstance(value, Part):
                    source = source.at[at(value.start(idx), value.rows), :]
                elif isinstance(value, Far):
                    buffer = refs.pop(0)
                    copy = pltpu.make_async_copy(source, buffer, next(free))
                    copy.start()
                    source = buffer
                coming.append(Coming(source, copy))
            going = []
            for kind, cuts in zip(kinds, pieces):
                mine = [targets.pop(0) for _ in cuts]
                going.append(Going(refs.pop(0) if kind else mine[0], kind, mine, free))
            kernel(idx, *coming, *going, *refs)
            for arrival in coming:
                arrival()
            for out in going:
                out.close()

        out = pl.pallas_call(
            body,
            out_shape=shapes,
            in_specs=[pl.BlockSpec(memory_space=pltpu.SMEM), *places],
            out_specs=out_places,
            scratch_shapes=[*own, pltpu.SemaphoreType.DMA((SENDS,))],
            compiler_params=pltpu.CompilerParams(vmem_limit_bytes=size + margin * MIB),
            cost_estimate=pl.CostEstimate(flops=1000, bytes_accessed=1000, transcendentals=0),
            name=name,
        )(self.idx, *given)
        out = list(out)
        out[-1], self.idx = lax.optimization_barrier((out[-1], self.idx))
        return [[out.pop(0) for _ in cuts] if kind == "cut" else out.pop(0) for kind, cuts in zip(kinds, pieces)]


def stack_kernel(idx, one, two, out):
    out.ref[0] = one()[...]
    out.ref[1] = two()[...]


def gains_kernel(idx, own, other, both):
    half = idx[1]
    part = own.ref.shape[1]
    for side, value in enumerate((own, other)):
        cols = at((half if side == 0 else 1 - half) * part, part)
        both.ref[:, cols] = value()[...].astype(F32)


def normed_rows(x, first, n1, start, count, gain, bias):
    @pl.loop(0, count // TILE)
    def _(step):
        normed, _ = norm(x[at(first + step * TILE, TILE), :].astype(F32))
        n1[at(start + step * TILE, TILE), :] = (normed * gain + bias).astype(BF16)


def pack_kernel(idx, wk, wv, wq, packed):
    local = wk.ref.shape[1]
    for i, w in enumerate((wk, wv, wq)):
        packed.ref[:, i * local : (i + 1) * local] = w()[...]


def normed_dots(n1, raw, half, own, other, which):
    rows, width = n1.shape
    part = width // 2
    local = raw.shape[1]
    cols = slice(which * local, (which + 1) * local)
    for start in range(0, rows, 256):
        raw[start : start + 256, :] = nn(n1[start : start + 256, at(half * part, part)], own[:, cols]) + nn(
            n1[start : start + 256, at((1 - half) * part, part)], other[:, cols]
        )


def normed_kernel(idx, x, gb, n1):
    core = idx[0]
    gb, x = gb(), x()
    own = x.shape[0] // 2
    for side in range(2):
        first = (core if side == 0 else 1 - core) * own
        normed_rows(x, first, n1.ref, side * own, own, gb[0:1, :], gb[4:5, :])


def qkv_kernel(prompt, idx, n1, w_own, w_oth, tables, out, raw):
    half, ctx = idx[1], idx[2]
    n1, w_own, w_oth = n1(), w_own(), w_oth()
    rows = n1.shape[0]
    own = rows // 2
    tables = tables()

    def place(start):
        if prompt:
            return ctx * own + start % own
        return tables.shape[1] - 128

    for which, scale in ((0, 1.0), (2, HEAD**-0.5)):
        normed_dots(n1, raw, half, w_own, w_oth, which)
        for start in range(0, rows, 128):
            turned = turn(raw[start : start + 128, :], place(start), tables, 1.0)
            out.ref[which, start : start + 128, :] = turned.astype(BF16) * BF16(scale)
    normed_dots(n1, raw, half, w_own, w_oth, 1)
    out.ref[1] = raw[...].astype(BF16)


def norm_pieces_kernel(idx, *refs):
    gb, out = refs[-2](), refs[-1]
    for i, x in enumerate(refs[:-2]):
        x = x()
        normed_rows(x, 0, out.ref, i * x.shape[0], x.shape[0], gb[0:1, :], gb[4:5, :])


def kv_kernel(blocks, idx, own_near, own_far, oth_near, oth_far, w_own, w_oth, tables, out, kept, raw):
    half, ctx, bit = idx[1], idx[2], idx[7]
    parts = [r() for r in (own_near, own_far, oth_near, oth_far)]
    tables = tables()
    w_own, w_oth = w_own(), w_oth()
    piece = parts[0].shape[0] // len(blocks)
    own = 2 * piece
    for i, block in enumerate(blocks):
        n1 = kept.ref.at[i]
        for place, x in zip((bit, 1 - bit, 2 + bit, 3 - bit), parts):
            n1[at(place * piece, piece), :] = x[i * piece : (i + 1) * piece, :]
        normed_dots(n1, raw, half, w_own, w_oth, 0)
        for start in range(0, 2 * own, 128):
            turned = turn(raw[start : start + 128, :], (ctx ^ block) * own + start % own, tables, 1.0)
            out.ref[2 * i, start : start + 128, :] = turned.astype(BF16)
        normed_dots(n1, raw, half, w_own, w_oth, 1)
        out.ref[2 * i + 1] = raw[...].astype(BF16)


def keys_values(near, two, one):
    near, two, one = near(), two(), one()
    return [near.at[0], two.at[0], two.at[2], one.at[0]], [near.at[1], two.at[1], two.at[3], one.at[1]]


def softmax_keys(scores):
    top = functools.reduce(jnp.maximum, [jnp.max(s, axis=0, keepdims=True) for s in scores])
    scores = [jnp.exp(s - top) for s in scores]
    inverse = 1.0 / sum(jnp.sum(s, axis=0, keepdims=True) for s in scores)
    return [(s * inverse).astype(BF16) for s in scores]


def prompt_kernel(idx, near, two, one, o_oth, o_own, p, vt, ot):
    ctx = idx[2]
    q = near().at[2]
    ks, vs = keys_values(near, two, one)
    own = o_own.ref.shape[0]
    width = q.shape[1]
    key = lax.broadcasted_iota(jnp.int32, (own, own), 0)
    row = lax.broadcasted_iota(jnp.int32, (own, own), 1)
    seen = key <= row
    for side, out in ((1, o_oth), (0, o_own)):
        rows = slice(side * own, (side + 1) * own)
        qt = q[rows, :].T
        for j in range(4):
            vt[:, j * own : (j + 1) * own] = vs[j][rows, :].T
        for head in range(width // HEAD):
            feats = slice(head * HEAD, (head + 1) * HEAD)
            qh = head_rows(qt, head)
            scores = []
            for j in range(4):
                part = nn(ks[j][rows, :], qh)
                if j == 0:
                    part = jnp.where(seen, part, MASKED)
                else:
                    part = part + jnp.where((ctx ^ j) < ctx, 0.0, MASKED).astype(F32)
                scores.append(part)
            for j, probs in enumerate(softmax_keys(scores)):
                p.ref[side, head, j * own : (j + 1) * own, :] = probs
            p.send(side, head)
            ot[feats, :] = nn(vt[feats, :], p.ref[side, head])
        out.ref[...] = ot[...].T.astype(BF16)
        out.send()


def cont_kernel(idx, mine_kvq, near, two, one, o_oth, o_own, p, vt, ot):
    mine_kvq = mine_kvq()
    k, v, q = (mine_kvq.at[i] for i in range(3))
    ks, vs = keys_values(near, two, one)
    own = o_own.ref.shape[0]
    width = q.shape[1]
    length = 128
    per = own // length
    key = lax.broadcasted_iota(jnp.int32, (length, 2 * length), 0)
    row = lax.broadcasted_iota(jnp.int32, (length, 2 * length), 1) % length
    seen = key <= row
    for c in [*range(per, 2 * per), *range(per)]:
        group = idx[3 + c]
        mine = slice(c * length, (c + 1) * length)
        theirs = at(group * own, own)
        qt = q[mine, :].T
        for j in range(4):
            vt[:, j * own : (j + 1) * own] = vs[j][theirs, :].T
        vt[:, 4 * own :] = v[mine, :].T
        for pair in range(width // HEAD // 2):
            feats = slice(pair * 2 * HEAD, (pair + 1) * 2 * HEAD)
            q2 = jnp.concatenate([head_rows(qt, 2 * pair), head_rows(qt, 2 * pair + 1)], axis=1)
            scores = [nn(ks[j][theirs, :], q2) for j in range(4)]
            scores.append(jnp.where(seen, nn(k[mine, :], q2), MASKED))
            probs = softmax_keys(scores)
            for j in range(4):
                p.ref[c, pair, j * own : (j + 1) * own, :] = probs[j]
            p.ref[c, pair, 4 * own :, :] = probs[4]
            p.send(c, pair)
            both = nn(vt[feats, :], p.ref[c, pair])
            first = pair * 2 * HEAD
            ot[first : first + HEAD, :] = both[:HEAD, :length]
            ot[first + HEAD : first + 2 * HEAD, :] = both[HEAD:, length:]
        out = o_own if c < per else o_oth
        place = c % per * length
        out.ref[place : place + length, :] = ot[...].T.astype(BF16)
        if c % per == per - 1:
            out.send()


def after_kernel(idx, w0, o0, w1, o1, w2, o2, w3, o3, x, gb, n3, z, x1):
    half = idx[1]
    part = z.ref.shape[1] // 2
    pairs = [(o(), w()) for o, w in ((o0, w0), (o1, w1), (o2, w2), (o3, w3))]
    for side in range(2):
        cols = at((half if side == 0 else 1 - half) * part, part)
        z.ref[:, cols] = sum(nn(o[...], w[side]) for o, w in pairs)
    z.send()
    x, gb = x(), gb()

    def one(rows):
        normed, _ = norm(z.ref[rows, :])
        after = x[rows, :].astype(F32) + (normed * gb[1:2, :] + gb[5:6, :])
        x1.ref[rows, :] = after
        normed, _ = norm(after)
        n3.ref[rows, :] = (normed * gb[2:3, :] + gb[6:7, :]).astype(BF16)

    tiles(x.shape[0], one)


def up_down_kernel(idx, n3o, wua, wub, n3t, wda, wdb, send, act, slope, keep):
    half = idx[1]
    own = n3o.ref.shape[0]
    part = n3o.ref.shape[1] // 2
    n3o, wua, wub = n3o(), wua(), wub()
    hidden = wua.shape[1]
    for side, n3 in enumerate((n3o, n3t)):
        if side == 1:
            n3 = n3()
        rows = slice(side * own, (side + 1) * own)
        for start in range(0, hidden, 256):
            cols = slice(start, start + 256)
            pre = nn(n3[:, at(half * part, part)], wua[:, cols]) + nn(
                n3[:, at((1 - half) * part, part)], wub[:, cols]
            )
            square = pre * pre
            tanh = jnp.tanh(GELU_COEF * (pre + 0.044715 * pre * square))
            up = 0.5 * (1.0 + tanh)
            act.ref[rows, cols] = (pre * up).astype(BF16)
            inner = GELU_COEF * (1.0 + (3.0 * 0.044715) * square)
            slope.ref[rows, cols] = (up + 0.5 * pre * (1.0 - tanh * tanh) * inner).astype(BF16)
        act.send(rows)
        slope.send(rows)
    weights = (wda(), wdb())
    for out, rows in ((send, slice(own, 2 * own)), (keep, slice(0, own))):
        for side, w in enumerate(weights):
            cols = at((half if side == 0 else 1 - half) * part, part)
            out.ref[:, cols] = nn(act.ref[rows, :], w[...]).astype(out.ref.dtype)
        out.send()


def last_kernel(idx, mine, theirs, x1, cotangent, gb, dm, y, grads):
    mine, theirs, cotangent, gb, x1 = mine(), theirs(), cotangent(), gb(), x1()
    grads.ref[...] = jnp.zeros_like(grads.ref)

    def one(rows):
        total = mine[rows, :].astype(F32) + theirs[rows, :].astype(F32)
        normed, inverse = norm(total)
        y.ref[rows, :] = (x1[rows, :] + (normed * gb[3:4, :] + gb[7:8, :])).astype(BF16)
        dy = cotangent[rows, :].astype(F32)
        dm.ref[rows, :] = norm_back(normed, inverse, dy, gb[3:4, :]).astype(BF16)
        grads.ref[0:1, :] += jnp.sum(dy * normed, axis=0, keepdims=True)
        grads.ref[1:2, :] += jnp.sum(dy, axis=0, keepdims=True)

    tiles(mine.shape[0], one)


def down_up_kernel(idx, dmo, wda, wdb, slope, dmt, wua, wub, send, du, keep):
    half = idx[1]
    own = dmo.ref.shape[0]
    part = dmo.ref.shape[1] // 2
    dmo, wda, wdb, slope = dmo(), wda(), wdb(), slope()
    for side, dm in enumerate((dmo, dmt)):
        if side == 1:
            dm = dm()
        rows = slice(side * own, (side + 1) * own)
        for start in range(0, slope.shape[1], 256):
            cols = slice(start, start + 256)
            back = nt(dm[:, at(half * part, part)], wda[cols, :]) + nt(
                dm[:, at((1 - half) * part, part)], wdb[cols, :]
            )
            du.ref[rows, cols] = (back * slope[rows, cols].astype(F32)).astype(BF16)
        du.send(rows)
    weights = (wua(), wub())
    for out, rows in ((send, slice(own, 2 * own)), (keep, slice(0, own))):
        for side, w in enumerate(weights):
            cols = at((half if side == 0 else 1 - half) * part, part)
            out.ref[:, cols] = nt(du.ref[rows, :], w[...]).astype(out.ref.dtype)
        out.send()


def middle_kernel(idx, mine, theirs, x1, cotangent, gb, z, dz, dx1, grads):
    mine, theirs, x1, cotangent, gb, z = mine(), theirs(), x1(), cotangent(), gb(), z()
    grads.ref[...] = jnp.zeros_like(grads.ref)

    def one(rows):
        back = mine[rows, :].astype(F32) + theirs[rows, :].astype(F32)
        normed, inverse = norm(x1[rows, :])
        grads.ref[1:2, :] += jnp.sum(back * normed, axis=0, keepdims=True)
        grads.ref[3:4, :] += jnp.sum(back, axis=0, keepdims=True)
        after = cotangent[rows, :].astype(F32) + norm_back(normed, inverse, back, gb[2:3, :])
        dx1.ref[rows, :] = after
        normed, inverse = norm(z[rows, :])
        grads.ref[0:1, :] += jnp.sum(after * normed, axis=0, keepdims=True)
        grads.ref[2:3, :] += jnp.sum(after, axis=0, keepdims=True)
        dz.ref[rows, :] = norm_back(normed, inverse, after, gb[1:2, :]).astype(BF16)

    tiles(mine.shape[0], one)


def spread_out(half, dzo, dzt, wo, do):
    own = dzo.shape[0]
    part = dzo.shape[1] // 2
    for side, dz in enumerate((dzo, dzt)):
        do[side * own : (side + 1) * own, :] = (
            nt(dz[:, at(half * part, part)], wo[0]) + nt(dz[:, at((1 - half) * part, part)], wo[1])
        ).astype(BF16)


def prompt_back_kernel(idx, dzo, dzt, wo, near, two, one, p, tables, o_own, o_oth, dkv, dq, grad_out, do, kt, dqt, dst):
    half, ctx = idx[1], idx[2]
    dzo, dzt, wo = dzo(), dzt(), wo()
    spread_out(half, dzo, dzt, wo, do)
    q = near().at[2]
    ks, vs = keys_values(near, two, one)
    p = p()
    tables = tables()
    own = dzo.shape[0]
    width = q.shape[1]
    heads = width // HEAD
    mixed = (o_own(), o_oth())
    for start in range(0, dzo.shape[1], 512):
        cols = slice(start, start + 512)
        grad_out.ref[:, cols] = tn(mixed[0][...], dzo[:, cols]) + tn(mixed[1][...], dzt[:, cols])
    grad_out.send()
    for side in range(2):
        rows = slice(side * own, (side + 1) * own)
        dot = do[rows, :].T
        for j in range(4):
            kt[:, j * own : (j + 1) * own] = ks[j][rows, :].T
        for head in range(heads):
            feats = slice(head * HEAD, (head + 1) * HEAD)
            doh = head_rows(dot, head)
            probs = [p[side, head, j * own : (j + 1) * own, :].astype(F32) for j in range(4)]
            terms = [probs[j] * nn(vs[j][rows, :], doh) for j in range(4)]
            centre = sum(jnp.sum(t, axis=0, keepdims=True) for t in terms)
            for j in range(4):
                dst[head, j * own : (j + 1) * own, :] = (terms[j] - probs[j] * centre).astype(BF16)
            dqt[feats, :] = nn(kt[feats, :], dst[head]) * (HEAD**-0.5)
        for j in range(4):
            keys = slice(j * own, (j + 1) * own)
            dkv.ref[j, 0, rows, :] = sum(
                nn(dst[head, keys, :], head_lanes(q[rows, :], head)) for head in range(heads)
            )
            dkv.ref[j, 1, rows, :] = sum(
                nn(p[side, head, keys, :], head_lanes(do[rows, :], head)) for head in range(heads)
            )
        dqf = dqt[...].T
        for start in range(0, own, 128):
            dq.ref[side * own + start : side * own + start + 128, :] = turn(
                dqf[start : start + 128, :], ctx * own + start, tables, -1.0
            ).astype(BF16)


def cont_back_kernel(idx, dzo, dzt, wo, mine_kvq, near, two, one, p, adds, tables, o_own, o_oth, grad_out, *refs):
    send, keep, dkvq, blocks = refs[:4]
    do, kt, dqt, dst = refs[4:]
    half, ctx = idx[1], idx[2]
    dzo, dzt, wo = dzo(), dzt(), wo()
    spread_out(half, dzo, dzt, wo, do)
    mine_kvq = mine_kvq()
    k, v, q = (mine_kvq.at[i] for i in range(3))
    ks, vs = keys_values(near, two, one)
    p, total = p(), adds()
    tables = tables()
    own = dzo.shape[0]
    width = q.shape[1]
    pairs = width // HEAD // 2
    length = 128
    last = tables.shape[1] - length
    mixed, grad_out = (o_own(), o_oth()), grad_out()
    part = dzo.shape[1] // 2
    for out, where in ((send, 1 - half), (keep, half)):
        cols = at(where * part, part)
        out.ref[...] = (
            grad_out[:, cols] + (tn(mixed[0][...], dzo[:, cols]) + tn(mixed[1][...], dzt[:, cols]))
        ).astype(BF16)
    for c in range(2 * own // length):
        group = idx[3 + c]
        mine = slice(c * length, (c + 1) * length)
        theirs = at(group * own, own)
        dot = do[mine, :].T
        for j in range(4):
            kt[:, j * own : (j + 1) * own] = ks[j][theirs, :].T
        kt[:, 4 * own :] = k[mine, :].T
        for pair in range(pairs):
            feats = slice(pair * 2 * HEAD, (pair + 1) * 2 * HEAD)
            do2 = jnp.concatenate([head_rows(dot, 2 * pair), head_rows(dot, 2 * pair + 1)], axis=1)
            probs = [p[c, pair, j * own : (j + 1) * own, :].astype(F32) for j in range(4)]
            probs.append(p[c, pair, 4 * own :, :].astype(F32))
            terms = [probs[j] * nn(vs[j][theirs, :], do2) for j in range(4)]
            terms.append(probs[4] * nn(v[mine, :], do2))
            centre = sum(jnp.sum(t, axis=0, keepdims=True) for t in terms)
            for j in range(4):
                dst[pair, j * own : (j + 1) * own, :] = (terms[j] - probs[j] * centre).astype(BF16)
            dst[pair, 4 * own :, :] = (terms[4] - probs[4] * centre).astype(BF16)
            both = nn(kt[feats, :], dst[pair]) * (HEAD**-0.5)
            first = pair * 2 * HEAD
            dqt[first : first + HEAD, :] = both[:HEAD, :length]
            dqt[first + HEAD : first + 2 * HEAD, :] = both[HEAD:, length:]
        q2, do2 = (
            [
                jnp.concatenate([head_lanes(t[mine, :], 2 * r), head_lanes(t[mine, :], 2 * r + 1)], axis=0)
                for r in range(pairs)
            ]
            for t in (q, do)
        )
        for j in range(4):
            keys = slice(j * own, (j + 1) * own)
            total[j, 0, theirs, :] += sum(nn(dst[r, keys, :], q2[r]) for r in range(pairs))
            total[j, 1, theirs, :] += sum(nn(p[c, r, keys, :], do2[r]) for r in range(pairs))
        dkf = sum(nn(dst[r, 4 * own :, :], q2[r]) for r in range(pairs))
        dkvq.ref[1, mine, :] = sum(nn(p[c, r, 4 * own :, :], do2[r]) for r in range(pairs)).astype(BF16)
        dkvq.ref[0, mine, :] = turn(dkf, last, tables, -1.0).astype(BF16)
        dkvq.ref[2, mine, :] = turn(dqt[...].T, last, tables, -1.0).astype(BF16)
    for j in range(4):
        for start in range(0, 2 * own, 128):
            r = slice(start, start + 128)
            blocks.ref[j, 0, r, :] = turn(
                total[j, 0, r, :], (ctx ^ j) * own + start % own, tables, -1.0
            ).astype(BF16)
        blocks.ref[j, 1] = total[j, 1].astype(BF16)


def input_kernel(idx, dkvq, w_own, w_oth, send, keep):
    half = idx[1]
    dkvq, weights = dkvq(), (w_own(), w_oth())
    own = keep.ref.shape[0]
    part = keep.ref.shape[1] // 2
    local = dkvq.shape[2]
    for out, rows in ((send, slice(own, 2 * own)), (keep, slice(0, own))):
        for side, w in enumerate(weights):
            cols = at((half if side == 0 else 1 - half) * part, part)
            total = sum(nt(dkvq[i, rows, :], w[:, i * local : (i + 1) * local]) for i in range(3))
            out.ref[:, cols] = total.astype(out.ref.dtype)


def blocks_input_kernel(first, idx, dkv, dq, w_own, w_oth, send_a, send_b, keep):
    half = idx[1]
    dkv, dq, weights = dkv(), dq(), (w_own(), w_oth())
    own = keep.ref.shape[1]
    part = keep.ref.shape[2] // 2
    local = dq.shape[1]
    for i, send in enumerate((send_a, send_b)):
        j = first + i
        for mine, rows in ((False, slice(own, 2 * own)), (True, slice(0, own))):
            for side, w in enumerate(weights):
                cols = at((half if side == 0 else 1 - half) * part, part)
                total = nt(dkv[j, 0, rows, :], w[:, :local]) + nt(dkv[j, 1, rows, :], w[:, local : 2 * local])
                if j == 0:
                    total += nt(dq[rows, :], w[:, 2 * local :])
                if mine:
                    keep.ref[i, :, cols] = total
                else:
                    send.ref[:, cols] = total.astype(BF16)


def blocks_cores_kernel(idx, keep, came_a, came_b, send, mine):
    bit = idx[7]
    keep, came = keep(), (came_a(), came_b())
    piece = send.ref.shape[1]
    for out, where in ((send, 1 - bit), (mine, bit)):
        rows = at(where * piece, piece)
        for i in range(2):
            out.ref[i] = (keep[i, rows, :] + came[i][rows, :].astype(F32)).astype(out.ref.dtype)


def blocks_tp_kernel(idx, mine_a, came_a, mine_b, came_b, three, one, own_two):
    pairs = ((mine_a(), came_a()), (mine_b(), came_b()))

    def total(j):
        mine, came = pairs[j // 2]
        return mine[j % 2] + came[j % 2].astype(F32)

    three.ref[...] = total(3).astype(BF16)
    one.ref[...] = total(1).astype(BF16)
    own_two.ref[0] = total(0)
    own_two.ref[1] = total(2)


def two_kernel(idx, own_two, came, total):
    total.ref[...] = (own_two()[1] + came()[...].astype(F32)).astype(BF16)


def first_prompt_kernel(idx, own_two, one, two, x, gb, dx1, dx, grads):
    own_two, one, two, x, gb, dx1 = own_two(), one(), two(), x(), gb(), dx1()
    back = own_two[0] + one[...].astype(F32) + two[...].astype(F32)
    normed, inverse = norm(x[...].astype(F32))
    grads.ref[0:1, :] = jnp.sum(back * normed, axis=0, keepdims=True)
    grads.ref[1:2, :] = jnp.sum(back, axis=0, keepdims=True)
    dx.ref[...] = (dx1[...] + norm_back(normed, inverse, back, gb[0:1, :])).astype(BF16)


def first_kernel(idx, mine, theirs, x, gb, dx1, dx, grads):
    mine, theirs, x, gb, dx1 = mine(), theirs(), x(), gb(), dx1()
    grads.ref[...] = jnp.zeros_like(grads.ref)

    def one(rows):
        back = mine[rows, :].astype(F32) + theirs[rows, :].astype(F32)
        normed, inverse = norm(x[rows, :].astype(F32))
        grads.ref[0:1, :] += jnp.sum(back * normed, axis=0, keepdims=True)
        grads.ref[1:2, :] += jnp.sum(back, axis=0, keepdims=True)
        dx.ref[rows, :] = (dx1[rows, :] + norm_back(normed, inverse, back, gb[0:1, :])).astype(BF16)

    tiles(mine.shape[0], one)


def cut_right(idx, pairs, send, keep):
    half = idx[1]
    part = send.ref.shape[1]
    for out, where in ((send, 1 - half), (keep, half)):
        cols = at(where * part, part)
        for start in range(0, out.ref.shape[0], 256):
            feats = slice(start, start + 256)
            out.ref[feats, :] = sum(tn(left[rows, feats], right[:, cols]) for left, rows, right in pairs).astype(
                BF16
            )
        out.send()


def grad_down_kernel(idx, act_a, act_b, a0, a1, b0, b1, send, keep):
    pairs = []
    for act, rights in ((act_a(), (a0, a1)), (act_b(), (b0, b1))):
        for i, right in enumerate(rights):
            right = right()
            own = right.shape[0]
            pairs.append((act, slice(i * own, (i + 1) * own), right))
    cut_right(idx, pairs, send, keep)


def grad_up_kernel(idx, a0, a1, b0, b1, du_a, du_b, send, keep):
    half = idx[1]
    lefts = [r() for r in (a0, a1, b0, b1)]
    rights = (du_a(), du_b())
    own = lefts[0].shape[0]
    part = send.ref.shape[0]
    for out, where in ((send, 1 - half), (keep, half)):
        for start in range(0, part, 256):
            feats = at(where * part + start, 256)
            for col in range(0, rights[0].shape[1], 512):
                out.ref[start : start + 256, col : col + 512] = sum(
                    tn(left[:, feats], rights[i // 2][(i % 2) * own : (i % 2 + 1) * own, col : col + 512])
                    for i, left in enumerate(lefts)
                ).astype(BF16)
        out.send()


def grad_qkv_kernel(idx, dkv, dq, dkvq_c, send_out, keep_out, n1p, n1c, n1_two, n1_one, send, keep):
    half = idx[1]
    dkv, dq, dkvq_c, n1p, n1c, n1_two, n1_one = (r() for r in (dkv, dq, dkvq_c, n1p, n1c, n1_two, n1_one))
    part = send.ref.shape[0]
    local = dq.shape[1]
    lefts = (n1p, n1_two.at[0], n1_two.at[1], n1_one.at[0], n1c)
    for out, where in ((send, 1 - half), (keep, half)):
        for start in range(0, part, 256):
            feats = at(where * part + start, 256)
            for i in range(2):
                rights = [*[dkv[j, i] for j in range(4)], dkvq_c[i]]
                out.ref[start : start + 256, i * local : (i + 1) * local] = sum(
                    tn(left[:, feats], right) for left, right in zip(lefts, rights)
                ).astype(BF16)
            out.ref[start : start + 256, 2 * local : 3 * local] = (
                tn(n1p[:, feats], dq[...]) + tn(n1c[:, feats], dkvq_c[2])
            ).astype(BF16)
    for out, proj in ((send, send_out()), (keep, keep_out())):
        few, cols = proj.shape[0] // 4, proj.shape[1] // 2
        for j in range(8):
            out.ref[j * few : (j + 1) * few, 3 * local :] = proj[
                j // 2 * few : (j // 2 + 1) * few, j % 2 * cols : (j % 2 + 1) * cols
            ]


def over_shard_kernel(idx, keep, came, send, mine):
    ctx = idx[2]
    keep, came = keep(), came()
    rows = keep.shape[0] // 4
    for out, order in ((send, (1, 3)), (mine, (0, 2))):
        for place, j in enumerate(order):
            r = at((ctx ^ j) * rows, rows)
            out.ref[place] = (keep[r, :].astype(F32) + came[r, :].astype(F32)).astype(BF16)


def near_kernel(idx, mine, came, send, keep):
    mine, came = mine(), came()
    send.ref[...] = (mine[1].astype(F32) + came[1].astype(F32)).astype(BF16)
    keep.ref[...] = mine[0].astype(F32) + came[0].astype(F32)


def far_kernel(idx, keep, came, total):
    total.ref[...] = (keep()[...] + came()[...].astype(F32)).astype(BF16)


def place_kernel(idx, q0, q1, q2, q3, out):
    ctx = idx[2]
    for j, quarter in enumerate((q0, q1, q2, q3)):
        quarter = quarter()
        out.ref[at((ctx ^ j) * quarter.shape[0], quarter.shape[0]), :] = quarter[...].astype(F32)


def place_two_kernel(idx, q0, q1, q2, q3, key, value, query, proj):
    ctx = idx[2]
    local = key.ref.shape[1]
    few, half = proj.ref.shape[0] // 4, proj.ref.shape[1] // 2
    for j, quarter in enumerate((q0, q1, q2, q3)):
        quarter = quarter()
        rows = at((ctx ^ j) * quarter.shape[0], quarter.shape[0])
        for i, out in enumerate((key, value, query)):
            out.ref[rows, :] = quarter[:, i * local : (i + 1) * local].astype(F32)
        rows = at((ctx ^ j) * few, few)
        proj.ref[rows, :half] = quarter[:few, 3 * local :].astype(F32)
        proj.ref[rows, half:] = quarter[few:, 3 * local :].astype(F32)


def whole_kernel(idx, *refs):
    core = idx[0]
    count = len(refs) // 3
    for i in range(count):
        out = refs[2 * count + i]
        for j, part in enumerate(refs[2 * i : 2 * i + 2]):
            part = part()
            rows = at((core if j == 0 else 1 - core) * part.shape[0], part.shape[0])
            out.ref[rows, :] = part[...]
        out.send()


def whole_quarters_kernel(idx, *refs):
    core, bit = idx[0], idx[7]
    out = refs[-1]
    for place, part in zip((2 * core + bit, 2 * core + 1 - bit, 2 - 2 * core + bit, 3 - 2 * core - bit), refs):
        part = part()
        out.ref[at(place * part.shape[0], part.shape[0]), :] = part[...]


def sum_kernel(idx, keep, came, total):
    keep, came = keep(), came()
    total.ref[...] = (keep[...] + came[...].astype(F32)).astype(BF16)


def small_kernel(idx, first_a, first_b, mid_a, mid_b, last_a, last_b, out):
    first, mid, last = (a()[...] + b()[...] for a, b in ((first_a, first_b), (mid_a, mid_b), (last_a, last_b)))
    out.ref[0:1, :] = first[0:1, :]
    out.ref[1:3, :] = mid[0:2, :]
    out.ref[3:4, :] = last[0:1, :]
    out.ref[4:5, :] = first[1:2, :]
    out.ref[5:7, :] = mid[2:4, :]
    out.ref[7:8, :] = last[1:2, :]


def rope_tables(length):
    freqs = ROPE_BASE ** (-np.arange(HEAD // 2, dtype=np.float32) * np.float32(2.0 / HEAD))
    theta = np.arange(length, dtype=np.float32)[:, None] * freqs.astype(np.float32)[None, :]
    cosine, sine = np.cos(theta), np.sin(theta)
    none = np.zeros_like(sine)
    pairs = ((cosine, cosine), (-sine, none), (none, sine))
    return jnp.asarray(np.stack([np.tile(np.concatenate(pair, axis=1), (1, 2)) for pair in pairs]).astype(np.float32))


def swap(value, axis, bit):
    size = lax.axis_size(axis)
    return lax.ppermute(value, axis, [(i, i ^ bit) for i in range(size)])


class Reduction:
    def __init__(self, line, send, keep, dim, proj=None):
        self.line, self.send, self.keep, self.dim, self.proj = line, send, keep, dim, proj
        self.pair = lax.axis_size("shard") == 2

    def start(self):
        if self.pair:
            self.came = swap(self.line.after(self.send), "shard", 1)

    def arrived(self):
        if self.pair:
            self.came = self.line.after(self.came)

    def summed(self, send, keep, dim):
        full = jnp.concatenate([keep, send], axis=dim)
        part = lax.psum_scatter(full, "shard", scatter_dimension=dim, tiled=True)
        return lax.psum(part, "ctx").astype(F32)

    def over_shard(self):
        if self.pair:
            self.shape = rows, width = self.keep.shape
            send, self.mine = self.line.call(
                over_shard_kernel,
                [self.keep, self.came],
                [((2, rows // 4, width), BF16)] * 2,
                name="over_shard",
            )
            self.moving = swap(send, "ctx", 1)

    def near(self):
        if self.pair:
            shape = self.mine.shape[1:]
            send, self.keep = self.line.call(
                near_kernel, [self.mine, self.moving], [(shape, BF16), (shape, F32)], name="near"
            )
            self.moving = swap(send, "ctx", 2)

    def far(self):
        if self.pair:
            (self.q0,) = self.line.call(
                far_kernel, [self.keep, self.moving], [(self.keep.shape, BF16)], name="far"
            )
            self.q2, self.q1 = swap(self.q0, "ctx", 2), swap(self.q0, "ctx", 1)

    def last(self):
        if self.pair:
            self.q2 = self.line.after(self.q2)
            self.q3 = swap(self.q2, "ctx", 1)

    def settled(self):
        if self.pair:
            self.q1, self.q3 = self.line.after(self.q1, self.q3)

    def placed(self):
        if not self.pair:
            if self.proj is None:
                return [self.summed(self.send, self.keep, self.dim)]
            width = self.keep.shape[1] // 4 * 3
            total = self.summed(self.send[:, :width], self.keep[:, :width], self.dim)
            return [*jnp.split(total, 3, axis=1), self.summed(*self.proj, 1)]
        rows, width = self.shape
        outs, kernel = [((rows, width), F32)], place_kernel
        if self.proj is not None:
            outs = [((rows, width // 4), F32)] * 3 + [(self.proj[1].shape, F32)]
            kernel = place_two_kernel
        return self.line.call(kernel, [self.q0, self.q1, self.q2, self.q3], outs, name="place")


def per_device(
    prompt_x,
    cont_x,
    owner,
    w_query,
    w_key,
    w_value,
    w_out,
    w_up,
    w_down,
    ln_gain,
    ln_bias,
    prompt_grad,
    cont_grad,
):
    shards = lax.axis_size("shard")
    groups, block, width = prompt_x.shape
    conts, cont_len, _ = cont_x.shape
    local = w_query.shape[1]
    hidden = w_up.shape[1]
    rows = groups * block
    own = rows // 2
    piece = own // 2
    part = width // 2
    prompt_len = block * lax.axis_size("ctx")
    core = lax.axis_index("tp") % 2
    bit = lax.axis_index("tp") // 2
    shard = lax.axis_index("shard")
    ctx = lax.axis_index("ctx")
    xs = (prompt_x.reshape(rows, width), cont_x.reshape(rows, width))
    dys = (prompt_grad.reshape(rows, width), cont_grad.reshape(rows, width))

    def both(weight, dim):
        if shards == 2:
            return weight, swap(weight, "shard", 1)
        full = lax.all_gather(weight, "shard", axis=dim, tiled=True)
        return tuple(jnp.split(full, 2, axis=dim))

    half = shard if shards == 2 else jnp.zeros_like(shard)
    which = (owner - shard * groups).reshape(2, conts // 2)
    which = jnp.where(core == 1, which[::-1], which) ^ core
    idx = jnp.concatenate([jnp.stack([core, half, ctx]), which.reshape(conts), jnp.stack([bit])])
    line = Line(idx.astype(jnp.int32))

    small = both(jnp.concatenate([ln_gain, ln_bias], axis=0), 1)
    (gb,) = line.call(gains_kernel, list(small), [((8, width), F32)], name="gains")
    packed = jnp.concatenate([w_key, w_value, w_query], axis=1)
    if shards == 2:
        (packed,) = line.call(
            pack_kernel, [w_key, w_value, w_query], [((part, 3 * local), BF16)], name="pack"
        )
    wqkv = both(packed, 0)
    quarter = lax.dynamic_slice_in_dim(xs[0], core * own + bit * piece, piece, 0)
    far, near = swap(quarter, "ctx", 2), swap(quarter, "ctx", 1)
    tables = rope_tables(prompt_len + cont_len)

    wo = both(line.after(w_out), 1)
    n1p, n1c = (
        line.call(normed_kernel, [x, gb], [((rows, width), BF16)], name="norm_first")[0] for x in xs
    )
    wide_rows = (rows, local)
    raw = pltpu.VMEM(wide_rows, F32)
    chunks = []
    for prompt in (True, False):
        chunks += line.call(
            functools.partial(qkv_kernel, prompt),
            [n1p if prompt else n1c, *wqkv, tables],
            [((3, *wide_rows), BF16)],
            [raw],
            name="qkv_prompt" if prompt else "qkv_cont",
        )
        if prompt:
            (normed,) = line.call(norm_pieces_kernel, [near, far, gb], [((own, width), BF16)], name="norm_pieces")
            both_near = [normed, swap(normed, "tp", 2)]
            far, w_up = line.after(far, w_up)
            last_near = swap(far, "ctx", 1)
            wu = both(w_up, 0)
    kvq_p, kvq_c = chunks
    (wo0,) = line.call(stack_kernel, wo, [((2, *wo[0].shape), BF16)], name="stack_out")
    both_near.append(swap(line.after(normed), "tp", 1))
    (normed,) = line.call(norm_pieces_kernel, [last_near, gb], [((piece, width), BF16)], name="norm_piece")
    one_near = [normed, swap(normed, "tp", 2), swap(normed, "tp", 1)]
    both_near[1] = line.after(both_near[1])
    both_near.append(swap(both_near[1], "tp", 1))
    seen, far_normed = [kvq_p], []

    def far_keys(blocks, parts):
        seen.extend(
            line.call(
                functools.partial(kv_kernel, blocks),
                [*parts, *wqkv, tables],
                [((2 * len(blocks), *wide_rows), BF16), ((len(blocks), rows, width), BF16, "far")],
                [raw],
                name="far_keys",
            )
        )
        far_normed.append(seen.pop())

    far_keys((1, 2), both_near)
    wo0 = line.after(wo0)
    wo2, wo1 = swap(wo0, "tp", 2), swap(wo0, "tp", 1)
    one_near[1] = line.after(one_near[1])
    one_near.append(swap(one_near[1], "tp", 1))
    far_keys((3,), one_near)

    half_o = ((own, local), BF16)
    o_oth_p, o_own_p, probs_p = line.call(
        prompt_kernel,
        seen,
        [half_o, half_o, ((2, local // HEAD, prompt_len, own), BF16, "far")],
        [pltpu.VMEM((local, prompt_len), BF16), pltpu.VMEM((local, own), F32)],
        name="attend_prompt",
    )
    wo1, wo2, *wu, w_down = line.after(wo1, wo2, *wu, w_down)
    wo3 = swap(wo2, "tp", 1)
    wd = both(w_down, 1)
    pairs = local // HEAD // 2
    mixed = [(o_own_p, o_oth_p)]

    def gathered(o_own, o_oth):
        return o_own, swap(o_oth, "tp", 1), swap(o_own, "tp", 2), swap(o_oth, "tp", 3)

    full_o = [gathered(o_own_p, o_oth_p)]
    all_len = prompt_len + cont_len
    o_oth_c, o_own_c, probs_c = line.call(
        cont_kernel,
        [kvq_c, *seen],
        [half_o, half_o, ((conts, pairs, all_len, 2 * cont_len), BF16, "far")],
        [pltpu.VMEM((local, all_len), BF16), pltpu.VMEM((local, cont_len), F32)],
        name="attend_cont",
    )
    mixed.append((o_own_c, o_oth_c))
    full_o.append(gathered(o_own_c, o_oth_c))

    def mine(value):
        return Part(value, own, lambda idx: idx[0] * own)

    own_rows, own_rows_f = ((own, width), BF16), ((own, width), F32)
    own_pieces = (*own_rows, "cut")

    def swapped(pieces):
        return [swap(piece, "tp", 1) for piece in pieces]

    def summed(keep, send):
        came = swapped(send)
        (total,) = line.call(sum_kernel, [keep, came], [own_rows], name="sum_cores")
        return total, swap(total, "tp", 2)

    stage = []
    for x, os in zip(xs, full_o):
        n3, z, x1 = line.call(
            after_kernel,
            [wo0, os[0], wo1, os[1], wo2, os[2], wo3, os[3], mine(x), gb],
            [own_pieces, own_rows_f, own_rows_f],
            name="after_attention",
        )
        n3t = swapped(n3)
        send, act, slope, keep = line.call(
            up_down_kernel,
            [n3, *wu, n3t, *wd],
            [own_pieces, ((rows, hidden), BF16), ((rows, hidden), BF16), own_rows_f],
            name="up_down",
        )
        stage.append((z, x1, n3, n3t, act, slope, *summed(keep, send)))

    later = []
    for i, dy in enumerate(dys):
        z, x1, n3, n3t, act, slope, total, theirs = stage[i]
        dm, y, grads_last = line.call(
            last_kernel,
            [total, theirs, x1, mine(dy), gb],
            [own_pieces, own_rows, ((2, width), F32)],
            name="last_norm",
        )
        dmt = swapped(dm)
        send, du, keep = line.call(
            down_up_kernel,
            [dm, *wd, slope, dmt, *wu],
            [own_pieces, ((rows, hidden), BF16), own_rows_f],
            name="down_up",
        )
        later.append((y, dm, dmt, du, *summed(keep, send), grads_last))

    middle = []

    def middle_norms(i):
        z, x1 = stage[i][:2]
        total, theirs = later[i][4:6]
        dz, dx1, grads_middle = line.call(
            middle_kernel,
            [total, theirs, x1, mine(dys[i]), gb, z],
            [own_pieces, own_rows_f, ((4, width), F32)],
            name="middle_norms",
        )
        middle.append((dx1, dz, swapped(dz), grads_middle))

    y_p, y_c = later[0][0], later[1][0]

    def assembled(*pairs):
        return line.call(
            whole_kernel,
            [value for pair in pairs for value in pair],
            [((rows, width), BF16)] * len(pairs),
            name="whole",
        )

    middle_norms(0)
    send, keep = line.call(
        grad_down_kernel,
        [stage[0][4], stage[1][4], *later[0][1:3], *later[1][1:3]],
        [((hidden, part), BF16)] * 2,
        name="grad_down",
    )
    down = Reduction(line, send, keep, 1)
    down.start()
    y_p, y_c = line.after(y_p, y_c)
    y_others = [swap(value, "tp", 1) for value in (y_p, y_c)]
    pair_rows = (2, *wide_rows)
    grads, dqp, grad_out = line.call(
        prompt_back_kernel,
        [*middle[0][1:3], *[Far(a) for a in (wo0, *seen, probs_p)], tables, *[Far(o) for o in mixed[0]]],
        [((4, *pair_rows), F32, "far"), (wide_rows, BF16), ((local, width), F32, "far")],
        [
            pltpu.VMEM(wide_rows, BF16),
            pltpu.VMEM((local, prompt_len), BF16),
            pltpu.VMEM((local, own), F32),
            pltpu.VMEM((local // HEAD, prompt_len, own), BF16),
        ],
        name="attend_prompt_back",
    )
    y_others = line.after(*y_others)
    send, keep = line.call(
        grad_up_kernel,
        [*stage[0][2:4], *stage[1][2:4], later[0][3], later[1][3]],
        [((part, hidden), BF16)] * 2,
        name="grad_up",
    )
    middle_norms(1)
    down.over_shard()
    up = Reduction(line, send, keep, 0)
    up.start()
    send_out, keep_out, dkvq_c, dkv_p = line.call(
        cont_back_kernel,
        [*middle[1][1:3], *[Far(a) for a in (wo0, kvq_c, *seen, probs_c, grads)], tables]
        + [*[Far(o) for o in mixed[1]], Far(grad_out)],
        [((local, part), BF16)] * 2 + [((3, *wide_rows), BF16), ((4, *pair_rows), BF16)],
        [
            pltpu.VMEM(wide_rows, BF16),
            pltpu.VMEM((local, all_len), BF16),
            pltpu.VMEM((local, cont_len), F32),
            pltpu.VMEM((pairs, all_len, 2 * cont_len), BF16),
        ],
        name="attend_cont_back",
    )
    down.near()

    def blocks_input(first):
        return line.call(
            functools.partial(blocks_input_kernel, first),
            [dkv_p, Far(dqp), *[Far(w) for w in wqkv]],
            [own_rows] * 2 + [((2, own, width), F32)],
            name="input_blocks",
        )

    def blocks_cores(keep, came):
        send, mine = line.call(
            blocks_cores_kernel,
            [keep, *came],
            [((2, piece, width), BF16), ((2, piece, width), F32)],
            name="blocks_cores",
        )
        return mine, swap(send, "tp", 2)

    *sent, keep_a = blocks_input(0)
    came_a = swapped(sent)
    send, keep = line.call(
        grad_qkv_kernel,
        [dkv_p, Far(dqp), dkvq_c, send_out, keep_out, *[Far(a) for a in (n1p, n1c, *far_normed)]],
        [((part, 4 * local), BF16)] * 2,
        name="grad_qkv",
    )
    qkv = Reduction(line, send, keep, 0, (send_out, keep_out))
    *sent, keep_b = blocks_input(2)
    down.far()
    came_b = swapped(line.after(*sent))
    qkv.start()
    tp_a = blocks_cores(keep_a, came_a)
    up.over_shard()
    tp_b = blocks_cores(keep_b, came_b)
    send_c, keep_c = line.call(
        input_kernel, [dkvq_c, *[Far(w) for w in wqkv]], [own_pieces, own_rows_f], name="input_back"
    )
    yp, yc = assembled((y_p, y_others[0]), (y_c, y_others[1]))
    up.near()
    down.last()
    qkv.over_shard()
    totals_c = summed(keep_c, line.after(*send_c))
    three, one, own_two = line.call(
        blocks_tp_kernel,
        [*tp_a, *tp_b],
        [((piece, width), BF16)] * 2 + [((2, piece, width), F32)],
        name="blocks_tp",
    )
    three, one = swap(three, "ctx", 1), swap(one, "ctx", 1)
    up.far()
    (two,) = line.call(two_kernel, [own_two, three], [((piece, width), BF16)], name="blocks_two")
    two = swap(two, "ctx", 2)
    qkv.near()
    dxc, first_c = line.call(
        first_kernel,
        [*totals_c, mine(xs[1]), gb, Far(middle[1][0])],
        [own_rows, ((2, width), F32)],
        name="first_norm",
    )
    up.last()
    (grad_down,) = down.placed()
    qkv.far()
    dxp, first_p = line.call(
        first_prompt_kernel,
        [
            own_two,
            one,
            two,
            Part(xs[0], piece, lambda idx: idx[0] * own + idx[7] * piece),
            gb,
            Part(middle[0][0], piece, lambda idx: idx[7] * piece),
        ],
        [((piece, width), BF16), ((2, width), F32)],
        name="first_norm_prompt",
    )
    first_other, dxp_across = swap(first_p, "tp", 2), swap(dxp, "tp", 2)
    up.settled()
    first_p = first_p + line.after(first_other)
    (small,) = line.call(
        small_kernel,
        [first_c, first_p, middle[0][3], middle[1][3], later[0][6], later[1][6]],
        [((8, width), F32)],
        name="small",
    )
    small = small + swap(small, "tp", 1)
    qkv.last()
    dxp_across, small = line.after(dxp_across, small)
    dxp_parts = [dxp, dxp_across, swap(dxp, "tp", 1), swap(dxp_across, "tp", 1)]
    if shards == 2:
        small = lax.dynamic_slice_in_dim(small, shard * part, part, 1) + swap(
            lax.dynamic_slice_in_dim(small, (1 - shard) * part, part, 1), "shard", 1
        )
    else:
        small = lax.psum_scatter(small, "shard", scatter_dimension=1, tiled=True)
    dxc = line.after(dxc)
    dxc_other = swap(dxc, "tp", 1)
    (grad_up,) = up.placed()
    (dxc,) = assembled((dxc, dxc_other))
    small = line.after(small)
    small = small + swap(small, "ctx", 1)
    (dxp,) = line.call(whole_quarters_kernel, dxp_parts, [((rows, width), BF16)], name="whole_prompt")
    qkv.settled()
    small = line.after(small)
    small = small + swap(small, "ctx", 2)
    grad_key, grad_value, grad_query, grad_out = qkv.placed()
    return (
        yp.reshape(prompt_x.shape),
        yc.reshape(cont_x.shape),
        dxp.reshape(prompt_x.shape),
        dxc.reshape(cont_x.shape),
        grad_query,
        grad_key,
        grad_value,
        grad_out,
        grad_up,
        grad_down,
        small[:4],
        small[4:],
    )


def solution(mesh):
    placed = (
        P("shard", "ctx", None),
        P(("shard", "ctx"), None, None),
        P(("shard", "ctx")),
        P("shard", "tp"),
        P("shard", "tp"),
        P("shard", "tp"),
        P("tp", "shard"),
        P("shard", "tp"),
        P("tp", "shard"),
        P(None, "shard"),
        P(None, "shard"),
        P("shard", "ctx", None),
        P(("shard", "ctx"), None, None),
    )
    rows = (P("shard", "ctx", None), P(("shard", "ctx"), None, None))
    return jax.shard_map(
        per_device,
        mesh=mesh,
        in_specs=placed,
        out_specs=rows + rows + placed[3:11],
        check_vma=False,
    )
```

```python
import functools

import jax
import jax.numpy as jnp
import numpy as np
from jax import lax
from jax.experimental import pallas as pl
from jax.experimental.pallas import tpu as pltpu
from jax.sharding import PartitionSpec as P

F32 = jnp.float32
BF16 = jnp.bfloat16
HEAD = 64
EPSILON = 1e-05
ROPE_BASE = 10000.0
GELU_COEF = 0.7978845608028654
MASKED = -1e30
MIB = 1024 * 1024
TILE = 128
TILE = 128
TILE = 128
TILE = 128
TILE = 128
TILE = 128
TILE = 128
TILE = 128


def nn(left, right):
    return jnp.dot(left, right, preferred_element_type=F32)


def nt(left, right):
    return lax.dot_general(left, right, (((1,), (1,)), ((), ())), preferred_element_type=F32)


def tn(left, right):
    return lax.dot_general(left, right, (((0,), (0,)), ((), ())), preferred_element_type=F32)


def mean(value):
    return jnp.mean(value, axis=-1, keepdims=True)


def norm(value):
    centred = value - mean(value)
    inverse = lax.rsqrt(mean(centred * centred) + EPSILON)
    return centred * inverse, inverse


def norm_back(normed, inverse, cotangent, gain):
    scaled = cotangent * gain
    return (scaled - mean(scaled) - normed * mean(scaled * normed)) * inverse


def tiles(count, body):
    @pl.loop(0, count // TILE)
    def _(step):
        body(at(step * TILE, TILE))


def at(start, size):
    return pl.ds(pl.multiple_of(start, size), size)


def turn(value, start, tables, sign):
    rows, width = value.shape
    cosine, minus, plus = (
        jnp.concatenate([tables[i, at(start, rows), :]] * (width // 128), axis=1) for i in range(3)
    )
    left = pltpu.roll(value, width - HEAD // 2, 1)
    right = pltpu.roll(value, HEAD // 2, 1)
    return value * cosine + sign * (left * minus + right * plus)


def head_rows(value, head, count=1):
    which = lax.broadcasted_iota(jnp.int32, value.shape, 0) // (HEAD * count)
    return jnp.where(which == head, value, jnp.zeros_like(value))


def head_lanes(value, head):
    which = lax.broadcasted_iota(jnp.int32, value.shape, 1) // HEAD
    return jnp.where(which == head, value, jnp.zeros_like(value))


class Part:
    def __init__(self, array, rows, start):
        self.array, self.rows, self.start = array, rows, start
        self.shape, self.dtype = array.shape, array.dtype


class Far:
    def __init__(self, array):
        self.array = array
        self.shape, self.dtype = array.shape, array.dtype


class Stack:
    def __init__(self, arrays):
        self.arrays = list(arrays)
        self.rows = [a.shape[0] for a in arrays]
        self.shape, self.dtype = (sum(self.rows), *arrays[0].shape[1:]), arrays[0].dtype


class Coming:
    def __init__(self, ref, copy=None, pieces=()):
        self.ref, self.copy, self.pieces = ref, copy, pieces

    def __call__(self):
        if self.copy is not None:
            self.copy.wait()
            self.copy = None
        start = 0
        for piece, rows in self.pieces:
            self.ref[start : start + rows, :] = piece[...]
            start += rows
        self.pieces = ()
        return self.ref


class Going:
    def __init__(self, ref, kind, targets, semaphores):
        self.ref, self.kind, self.targets, self.semaphores = ref, kind, targets, semaphores
        self.copies = []

    def send(self, *index):
        if self.kind == "far":
            where = index if index else Ellipsis
            copy = pltpu.make_async_copy(self.ref.at[where], self.targets[0].at[where], next(self.semaphores))
            copy.start()
            self.copies.append(copy)

    def close(self):
        if self.kind == "cut":
            start = 0
            for target in self.targets:
                rows = target.shape[0]
                target[...] = self.ref[start : start + rows, :]
                start += rows
        elif not self.copies:
            self.send()
        for copy in self.copies:
            copy.wait()


SENDS = 40
PIECES = 3


def pieces_of(rows):
    tiles_of = rows // 16
    return [16 * (tiles_of // PIECES + (i < tiles_of % PIECES)) for i in range(PIECES)]


class Line:
    def __init__(self, idx):
        self.idx = idx

    def after(self, *values):
        *values, self.idx = lax.optimization_barrier((*values, self.idx))
        return values[0] if len(values) == 1 else values

    def call(self, kernel, inputs, outputs, scratch=(), name=None, margin=12):
        inputs = [Stack(a) if isinstance(a, list) else a for a in inputs]
        given = []
        for a in inputs:
            given += a.arrays if isinstance(a, Stack) else [a.array if isinstance(a, (Part, Far)) else a]
        places = [
            pl.BlockSpec(memory_space=pl.ANY if isinstance(a, Far) else pltpu.VMEM)
            for a in inputs
            for _ in (a.arrays if isinstance(a, Stack) else [a])
        ]
        kinds = [out[2] if len(out) > 2 else "" for out in outputs]
        pieces = [pieces_of(out[0][0]) if kind == "cut" else [out[0][0]] for out, kind in zip(outputs, kinds)]
        shapes = [
            jax.ShapeDtypeStruct((rows, *out[0][1:]), out[1]) for out, cuts in zip(outputs, pieces) for rows in cuts
        ]
        out_places = [
            pl.BlockSpec(memory_space=pl.ANY if kind == "far" else pltpu.VMEM)
            for kind, cuts in zip(kinds, pieces)
            for _ in cuts
        ]
        held = [pltpu.VMEM(a.shape, a.dtype) for a in inputs if isinstance(a, (Far, Stack))]
        held += [pltpu.VMEM(out[0], out[1]) for out, kind in zip(outputs, kinds) if kind]
        own = [*held, *scratch]
        size = sum(int(np.prod(a.shape)) * np.dtype(a.dtype).itemsize for a in own)

        def body(*refs):
            refs = list(refs)
            idx = refs.pop(0)
            sources = [refs.pop(0) for _ in given]
            targets = [refs.pop(0) for _ in shapes]
            semaphores = refs.pop()
            free = (semaphores.at[i] for i in range(SENDS))
            coming = []
            for value in inputs:
                if isinstance(value, Stack):
                    buffer = refs.pop(0)
                    coming.append(Coming(buffer, pieces=[(sources.pop(0), rows) for rows in value.rows]))
                    continue
                source, copy = sources.pop(0), None
                if isinstance(value, Part):
                    source = source.at[at(value.start(idx), value.rows), :]
                elif isinstance(value, Far):
                    buffer = refs.pop(0)
                    copy = pltpu.make_async_copy(source, buffer, next(free))
                    copy.start()
                    source = buffer
                coming.append(Coming(source, copy))
            going = []
            for kind, cuts in zip(kinds, pieces):
                mine = [targets.pop(0) for _ in cuts]
                going.append(Going(refs.pop(0) if kind else mine[0], kind, mine, free))
            kernel(idx, *coming, *going, *refs)
            for arrival in coming:
                arrival()
            for out in going:
                out.close()

        out = pl.pallas_call(
            body,
            out_shape=shapes,
            in_specs=[pl.BlockSpec(memory_space=pltpu.SMEM), *places],
            out_specs=out_places,
            scratch_shapes=[*own, pltpu.SemaphoreType.DMA((SENDS,))],
            compiler_params=pltpu.CompilerParams(vmem_limit_bytes=size + margin * MIB),
            cost_estimate=pl.CostEstimate(flops=1000, bytes_accessed=1000, transcendentals=0),
            name=name,
        )(self.idx, *given)
        out = list(out)
        out[-1], self.idx = lax.optimization_barrier((out[-1], self.idx))
        return [[out.pop(0) for _ in cuts] if kind == "cut" else out.pop(0) for kind, cuts in zip(kinds, pieces)]


def stack_kernel(idx, one, two, out):
    out.ref[0] = one()[...]
    out.ref[1] = two()[...]


def gains_kernel(idx, own, other, both):
    half = idx[1]
    part = own.ref.shape[1]
    for side, value in enumerate((own, other)):
        cols = at((half if side == 0 else 1 - half) * part, part)
        both.ref[:, cols] = value()[...].astype(F32)


def normed_rows(x, first, n1, start, count, gain, bias):
    @pl.loop(0, count // TILE)
    def _(step):
        normed, _ = norm(x[at(first + step * TILE, TILE), :].astype(F32))
        n1[at(start + step * TILE, TILE), :] = (normed * gain + bias).astype(BF16)


def pack_kernel(idx, wk, wv, wq, packed):
    local = wk.ref.shape[1]
    for i, w in enumerate((wk, wv, wq)):
        packed.ref[:, i * local : (i + 1) * local] = w()[...]


def pack_hidden_kernel(idx, wu, wd, packed):
    wu, wd = wu(), wd()
    part = wd.shape[1]
    packed.ref[0] = wu[...]
    packed.ref[1, :, :part] = wd[:part, :]
    packed.ref[1, :, part:] = wd[part:, :]


def unpack_hidden_kernel(idx, packed, wu, wd):
    packed = packed()
    part = wd.ref.shape[1]
    wu.ref[...] = packed[0]
    wd.ref[:part, :] = packed[1, :, :part]
    wd.ref[part:, :] = packed[1, :, part:]


def normed_dots(n1, raw, half, own, other, which):
    rows, width = n1.shape
    part = width // 2
    local = raw.shape[1]
    cols = slice(which * local, (which + 1) * local)
    for start in range(0, rows, 256):
        raw[start : start + 256, :] = nn(n1[start : start + 256, at(half * part, part)], own[:, cols]) + nn(
            n1[start : start + 256, at((1 - half) * part, part)], other[:, cols]
        )


def normed_kernel(idx, x, gb, n1):
    core = idx[0]
    gb, x = gb(), x()
    own = x.shape[0] // 2
    for side in range(2):
        first = (core if side == 0 else 1 - core) * own
        normed_rows(x, first, n1.ref, side * own, own, gb[0:1, :], gb[4:5, :])


def qkv_kernel(prompt, idx, n1, w_own, w_oth, tables, out, raw):
    half, ctx = idx[1], idx[2]
    n1, w_own, w_oth = n1(), w_own(), w_oth()
    rows = n1.shape[0]
    own = rows // 2
    tables = tables()

    def place(start):
        if prompt:
            return ctx * own + start % own
        return tables.shape[1] - 128

    for which, scale in ((0, 1.0), (2, HEAD**-0.5)):
        normed_dots(n1, raw, half, w_own, w_oth, which)
        for start in range(0, rows, 128):
            turned = turn(raw[start : start + 128, :], place(start), tables, 1.0)
            out.ref[which, start : start + 128, :] = turned.astype(BF16) * BF16(scale)
    normed_dots(n1, raw, half, w_own, w_oth, 1)
    out.ref[1] = raw[...].astype(BF16)


def norm_pieces_kernel(idx, *refs):
    gb, out = refs[-2](), refs[-1]
    for i, x in enumerate(refs[:-2]):
        x = x()
        normed_rows(x, 0, out.ref, i * x.shape[0], x.shape[0], gb[0:1, :], gb[4:5, :])


def kv_kernel(blocks, idx, own_near, own_far, oth_near, oth_far, w_own, w_oth, tables, out, kept, raw):
    half, ctx, bit = idx[1], idx[2], idx[7]
    parts = [r() for r in (own_near, own_far, oth_near, oth_far)]
    tables = tables()
    w_own, w_oth = w_own(), w_oth()
    piece = parts[0].shape[0] // len(blocks)
    own = 2 * piece
    for i, block in enumerate(blocks):
        n1 = kept.ref.at[i]
        for place, x in zip((bit, 1 - bit, 2 + bit, 3 - bit), parts):
            n1[at(place * piece, piece), :] = x[i * piece : (i + 1) * piece, :]
        normed_dots(n1, raw, half, w_own, w_oth, 0)
        for start in range(0, 2 * own, 128):
            turned = turn(raw[start : start + 128, :], (ctx ^ block) * own + start % own, tables, 1.0)
            out.ref[2 * i, start : start + 128, :] = turned.astype(BF16)
        normed_dots(n1, raw, half, w_own, w_oth, 1)
        out.ref[2 * i + 1] = raw[...].astype(BF16)


def keys_values(near, two, one):
    near, two, one = near(), two(), one()
    return [near.at[0], two.at[0], two.at[2], one.at[0]], [near.at[1], two.at[1], two.at[3], one.at[1]]


def softmax_keys(scores):
    top = functools.reduce(jnp.maximum, [jnp.max(s, axis=0, keepdims=True) for s in scores])
    scores = [jnp.exp(s - top) for s in scores]
    inverse = 1.0 / sum(jnp.sum(s, axis=0, keepdims=True) for s in scores)
    return [(s * inverse).astype(BF16) for s in scores]


def prompt_kernel(idx, near, two, one, o_oth, o_own, p, vt, ot):
    ctx = idx[2]
    q = near().at[2]
    ks, vs = keys_values(near, two, one)
    own = o_own.ref.shape[0]
    width = q.shape[1]
    key = lax.broadcasted_iota(jnp.int32, (own, own), 0)
    row = lax.broadcasted_iota(jnp.int32, (own, own), 1)
    seen = key <= row
    for side, out in ((1, o_oth), (0, o_own)):
        rows = slice(side * own, (side + 1) * own)
        qt = q[rows, :].T
        for j in range(4):
            vt[:, j * own : (j + 1) * own] = vs[j][rows, :].T
        for head in range(width // HEAD):
            feats = slice(head * HEAD, (head + 1) * HEAD)
            qh = head_rows(qt, head)
            scores = []
            for j in range(4):
                part = nn(ks[j][rows, :], qh)
                if j == 0:
                    part = jnp.where(seen, part, MASKED)
                else:
                    part = part + jnp.where((ctx ^ j) < ctx, 0.0, MASKED).astype(F32)
                scores.append(part)
            for j, probs in enumerate(softmax_keys(scores)):
                p.ref[side, head, j * own : (j + 1) * own, :] = probs
            p.send(side, head)
            ot[feats, :] = nn(vt[feats, :], p.ref[side, head])
        out.ref[...] = ot[...].T.astype(BF16)
        out.send()


def cont_kernel(idx, mine_kvq, near, two, one, o_oth, o_own, p, vt, ot):
    mine_kvq = mine_kvq()
    k, v, q = (mine_kvq.at[i] for i in range(3))
    ks, vs = keys_values(near, two, one)
    own = o_own.ref.shape[0]
    width = q.shape[1]
    length = 128
    per = own // length
    key = lax.broadcasted_iota(jnp.int32, (length, 2 * length), 0)
    row = lax.broadcasted_iota(jnp.int32, (length, 2 * length), 1) % length
    seen = key <= row
    for c in [*range(per, 2 * per), *range(per)]:
        group = idx[3 + c]
        mine = slice(c * length, (c + 1) * length)
        theirs = at(group * own, own)
        qt = q[mine, :].T
        for j in range(4):
            vt[:, j * own : (j + 1) * own] = vs[j][theirs, :].T
        vt[:, 4 * own :] = v[mine, :].T
        for pair in range(width // HEAD // 2):
            feats = slice(pair * 2 * HEAD, (pair + 1) * 2 * HEAD)
            q2 = jnp.concatenate([head_rows(qt, 2 * pair), head_rows(qt, 2 * pair + 1)], axis=1)
            scores = [nn(ks[j][theirs, :], q2) for j in range(4)]
            scores.append(jnp.where(seen, nn(k[mine, :], q2), MASKED))
            probs = softmax_keys(scores)
            for j in range(4):
                p.ref[c, pair, j * own : (j + 1) * own, :] = probs[j]
            p.ref[c, pair, 4 * own :, :] = probs[4]
            p.send(c, pair)
            both = nn(vt[feats, :], p.ref[c, pair])
            first = pair * 2 * HEAD
            ot[first : first + HEAD, :] = both[:HEAD, :length]
            ot[first + HEAD : first + 2 * HEAD, :] = both[HEAD:, length:]
        out = o_own if c < per else o_oth
        place = c % per * length
        out.ref[place : place + length, :] = ot[...].T.astype(BF16)
        if c % per == per - 1:
            out.send()


def after_kernel(idx, w0, o0, w1, o1, w2, o2, w3, o3, x, gb, n3, z, x1):
    half = idx[1]
    part = z.ref.shape[1] // 2
    pairs = [(o(), w()) for o, w in ((o0, w0), (o1, w1), (o2, w2), (o3, w3))]
    for side in range(2):
        cols = at((half if side == 0 else 1 - half) * part, part)
        z.ref[:, cols] = sum(nn(o[...], w[side]) for o, w in pairs)
    z.send()
    x, gb = x(), gb()

    def one(rows):
        normed, _ = norm(z.ref[rows, :])
        after = x[rows, :].astype(F32) + (normed * gb[1:2, :] + gb[5:6, :])
        x1.ref[rows, :] = after
        normed, _ = norm(after)
        n3.ref[rows, :] = (normed * gb[2:3, :] + gb[6:7, :]).astype(BF16)

    tiles(x.shape[0], one)


def up_down_kernel(idx, n3o, wua, wub, n3t, wda, wdb, send, act, slope, keep):
    half = idx[1]
    own = n3o.ref.shape[0]
    part = n3o.ref.shape[1] // 2
    n3o, wua, wub = n3o(), wua(), wub()
    hidden = wua.shape[1]
    for side, n3 in enumerate((n3o, n3t)):
        if side == 1:
            n3 = n3()
        rows = slice(side * own, (side + 1) * own)
        for start in range(0, hidden, 256):
            cols = slice(start, start + 256)
            pre = nn(n3[:, at(half * part, part)], wua[:, cols]) + nn(
                n3[:, at((1 - half) * part, part)], wub[:, cols]
            )
            square = pre * pre
            tanh = jnp.tanh(GELU_COEF * (pre + 0.044715 * pre * square))
            up = 0.5 * (1.0 + tanh)
            act.ref[rows, cols] = (pre * up).astype(BF16)
            inner = GELU_COEF * (1.0 + (3.0 * 0.044715) * square)
            slope.ref[rows, cols] = (up + 0.5 * pre * (1.0 - tanh * tanh) * inner).astype(BF16)
        act.send(rows)
        slope.send(rows)
    weights = (wda(), wdb())
    for out, rows in ((send, slice(own, 2 * own)), (keep, slice(0, own))):
        for side, w in enumerate(weights):
            cols = at((half if side == 0 else 1 - half) * part, part)
            out.ref[:, cols] = nn(act.ref[rows, :], w[...]).astype(out.ref.dtype)
        out.send()


def last_kernel(idx, mine, theirs, x1, cotangent, gb, dm, y, grads):
    mine, theirs, cotangent, gb, x1 = mine(), theirs(), cotangent(), gb(), x1()
    grads.ref[...] = jnp.zeros_like(grads.ref)

    def one(rows):
        total = mine[rows, :].astype(F32) + theirs[rows, :].astype(F32)
        normed, inverse = norm(total)
        y.ref[rows, :] = (x1[rows, :] + (normed * gb[3:4, :] + gb[7:8, :])).astype(BF16)
        dy = cotangent[rows, :].astype(F32)
        dm.ref[rows, :] = norm_back(normed, inverse, dy, gb[3:4, :]).astype(BF16)
        grads.ref[0:1, :] += jnp.sum(dy * normed, axis=0, keepdims=True)
        grads.ref[1:2, :] += jnp.sum(dy, axis=0, keepdims=True)

    tiles(mine.shape[0], one)


def down_up_kernel(idx, dmo, wda, wdb, slope, dmt, wua, wub, send, du, keep):
    half = idx[1]
    own = dmo.ref.shape[0]
    part = dmo.ref.shape[1] // 2
    dmo, wda, wdb, slope = dmo(), wda(), wdb(), slope()
    for side, dm in enumerate((dmo, dmt)):
        if side == 1:
            dm = dm()
        rows = slice(side * own, (side + 1) * own)
        for start in range(0, slope.shape[1], 256):
            cols = slice(start, start + 256)
            back = nt(dm[:, at(half * part, part)], wda[cols, :]) + nt(
                dm[:, at((1 - half) * part, part)], wdb[cols, :]
            )
            du.ref[rows, cols] = (back * slope[rows, cols].astype(F32)).astype(BF16)
        du.send(rows)
    weights = (wua(), wub())
    for out, rows in ((send, slice(own, 2 * own)), (keep, slice(0, own))):
        for side, w in enumerate(weights):
            cols = at((half if side == 0 else 1 - half) * part, part)
            out.ref[:, cols] = nt(du.ref[rows, :], w[...]).astype(out.ref.dtype)
        out.send()


def middle_kernel(idx, mine, theirs, x1, cotangent, gb, z, dz, dx1, grads):
    mine, theirs, x1, cotangent, gb, z = mine(), theirs(), x1(), cotangent(), gb(), z()
    grads.ref[...] = jnp.zeros_like(grads.ref)

    def one(rows):
        back = mine[rows, :].astype(F32) + theirs[rows, :].astype(F32)
        normed, inverse = norm(x1[rows, :])
        grads.ref[1:2, :] += jnp.sum(back * normed, axis=0, keepdims=True)
        grads.ref[3:4, :] += jnp.sum(back, axis=0, keepdims=True)
        after = cotangent[rows, :].astype(F32) + norm_back(normed, inverse, back, gb[2:3, :])
        dx1.ref[rows, :] = after
        normed, inverse = norm(z[rows, :])
        grads.ref[0:1, :] += jnp.sum(after * normed, axis=0, keepdims=True)
        grads.ref[2:3, :] += jnp.sum(after, axis=0, keepdims=True)
        dz.ref[rows, :] = norm_back(normed, inverse, after, gb[1:2, :]).astype(BF16)

    tiles(mine.shape[0], one)


def spread_out(half, dzo, dzt, wo, do):
    own = dzo.shape[0]
    part = dzo.shape[1] // 2
    for side, dz in enumerate((dzo, dzt)):
        do[side * own : (side + 1) * own, :] = (
            nt(dz[:, at(half * part, part)], wo[0]) + nt(dz[:, at((1 - half) * part, part)], wo[1])
        ).astype(BF16)


def prompt_back_kernel(idx, dzo, dzt, wo, near, two, one, p, tables, o_own, o_oth, dkv, dq, grad_out, do, kt, dqt, dst):
    half, ctx = idx[1], idx[2]
    dzo, dzt, wo = dzo(), dzt(), wo()
    spread_out(half, dzo, dzt, wo, do)
    q = near().at[2]
    ks, vs = keys_values(near, two, one)
    p = p()
    tables = tables()
    own = dzo.shape[0]
    width = q.shape[1]
    heads = width // HEAD
    mixed = (o_own(), o_oth())
    for start in range(0, dzo.shape[1], 512):
        cols = slice(start, start + 512)
        grad_out.ref[:, cols] = tn(mixed[0][...], dzo[:, cols]) + tn(mixed[1][...], dzt[:, cols])
    grad_out.send()
    for side in range(2):
        rows = slice(side * own, (side + 1) * own)
        dot = do[rows, :].T
        for j in range(4):
            kt[:, j * own : (j + 1) * own] = ks[j][rows, :].T
        for head in range(heads):
            feats = slice(head * HEAD, (head + 1) * HEAD)
            doh = head_rows(dot, head)
            probs = [p[side, head, j * own : (j + 1) * own, :].astype(F32) for j in range(4)]
            terms = [probs[j] * nn(vs[j][rows, :], doh) for j in range(4)]
            centre = sum(jnp.sum(t, axis=0, keepdims=True) for t in terms)
            for j in range(4):
                dst[head, j * own : (j + 1) * own, :] = (terms[j] - probs[j] * centre).astype(BF16)
            dqt[feats, :] = nn(kt[feats, :], dst[head]) * (HEAD**-0.5)
        for j in range(4):
            keys = slice(j * own, (j + 1) * own)
            dkv.ref[j, 0, rows, :] = sum(
                nn(dst[head, keys, :], head_lanes(q[rows, :], head)) for head in range(heads)
            )
            dkv.ref[j, 1, rows, :] = sum(
                nn(p[side, head, keys, :], head_lanes(do[rows, :], head)) for head in range(heads)
            )
        dqf = dqt[...].T
        for start in range(0, own, 128):
            dq.ref[side * own + start : side * own + start + 128, :] = turn(
                dqf[start : start + 128, :], ctx * own + start, tables, -1.0
            ).astype(BF16)


def cont_back_kernel(idx, dzo, dzt, wo, mine_kvq, near, two, one, p, adds, tables, o_own, o_oth, grad_out, *refs):
    send, keep, dkvq, blocks = refs[:4]
    do, kt, dqt, dst = refs[4:]
    half, ctx = idx[1], idx[2]
    dzo, dzt, wo = dzo(), dzt(), wo()
    spread_out(half, dzo, dzt, wo, do)
    mine_kvq = mine_kvq()
    k, v, q = (mine_kvq.at[i] for i in range(3))
    ks, vs = keys_values(near, two, one)
    p, total = p(), adds()
    tables = tables()
    own = dzo.shape[0]
    width = q.shape[1]
    pairs = width // HEAD // 2
    length = 128
    last = tables.shape[1] - length
    mixed, grad_out = (o_own(), o_oth()), grad_out()
    part = dzo.shape[1] // 2
    for out, where in ((send, 1 - half), (keep, half)):
        cols = at(where * part, part)
        out.ref[...] = (
            grad_out[:, cols] + (tn(mixed[0][...], dzo[:, cols]) + tn(mixed[1][...], dzt[:, cols]))
        ).astype(BF16)
    for c in range(2 * own // length):
        group = idx[3 + c]
        mine = slice(c * length, (c + 1) * length)
        theirs = at(group * own, own)
        dot = do[mine, :].T
        for j in range(4):
            kt[:, j * own : (j + 1) * own] = ks[j][theirs, :].T
        kt[:, 4 * own :] = k[mine, :].T
        for pair in range(pairs):
            feats = slice(pair * 2 * HEAD, (pair + 1) * 2 * HEAD)
            do2 = jnp.concatenate([head_rows(dot, 2 * pair), head_rows(dot, 2 * pair + 1)], axis=1)
            probs = [p[c, pair, j * own : (j + 1) * own, :].astype(F32) for j in range(4)]
            probs.append(p[c, pair, 4 * own :, :].astype(F32))
            terms = [probs[j] * nn(vs[j][theirs, :], do2) for j in range(4)]
            terms.append(probs[4] * nn(v[mine, :], do2))
            centre = sum(jnp.sum(t, axis=0, keepdims=True) for t in terms)
            for j in range(4):
                dst[pair, j * own : (j + 1) * own, :] = (terms[j] - probs[j] * centre).astype(BF16)
            dst[pair, 4 * own :, :] = (terms[4] - probs[4] * centre).astype(BF16)
            both = nn(kt[feats, :], dst[pair]) * (HEAD**-0.5)
            first = pair * 2 * HEAD
            dqt[first : first + HEAD, :] = both[:HEAD, :length]
            dqt[first + HEAD : first + 2 * HEAD, :] = both[HEAD:, length:]
        q2, do2 = (
            [
                jnp.concatenate([head_lanes(t[mine, :], 2 * r), head_lanes(t[mine, :], 2 * r + 1)], axis=0)
                for r in range(pairs)
            ]
            for t in (q, do)
        )
        for j in range(4):
            keys = slice(j * own, (j + 1) * own)
            total[j, 0, theirs, :] += sum(nn(dst[r, keys, :], q2[r]) for r in range(pairs))
            total[j, 1, theirs, :] += sum(nn(p[c, r, keys, :], do2[r]) for r in range(pairs))
        dkf = sum(nn(dst[r, 4 * own :, :], q2[r]) for r in range(pairs))
        dkvq.ref[1, mine, :] = sum(nn(p[c, r, 4 * own :, :], do2[r]) for r in range(pairs)).astype(BF16)
        dkvq.ref[0, mine, :] = turn(dkf, last, tables, -1.0).astype(BF16)
        dkvq.ref[2, mine, :] = turn(dqt[...].T, last, tables, -1.0).astype(BF16)
    for j in range(4):
        for start in range(0, 2 * own, 128):
            r = slice(start, start + 128)
            blocks.ref[j, 0, r, :] = turn(
                total[j, 0, r, :], (ctx ^ j) * own + start % own, tables, -1.0
            ).astype(BF16)
        blocks.ref[j, 1] = total[j, 1].astype(BF16)


def input_kernel(idx, dkvq, w_own, w_oth, send, keep):
    half = idx[1]
    dkvq, weights = dkvq(), (w_own(), w_oth())
    own = keep.ref.shape[0]
    part = keep.ref.shape[1] // 2
    local = dkvq.shape[2]
    for out, rows in ((send, slice(own, 2 * own)), (keep, slice(0, own))):
        for side, w in enumerate(weights):
            cols = at((half if side == 0 else 1 - half) * part, part)
            total = sum(nt(dkvq[i, rows, :], w[:, i * local : (i + 1) * local]) for i in range(3))
            out.ref[:, cols] = total.astype(out.ref.dtype)


def blocks_input_kernel(first, idx, dkv, dq, w_own, w_oth, send_a, send_b, keep):
    half = idx[1]
    dkv, dq, weights = dkv(), dq(), (w_own(), w_oth())
    own = keep.ref.shape[1]
    part = keep.ref.shape[2] // 2
    local = dq.shape[1]
    for i, send in enumerate((send_a, send_b)):
        j = first + i
        for mine, rows in ((False, slice(own, 2 * own)), (True, slice(0, own))):
            for side, w in enumerate(weights):
                cols = at((half if side == 0 else 1 - half) * part, part)
                total = nt(dkv[j, 0, rows, :], w[:, :local]) + nt(dkv[j, 1, rows, :], w[:, local : 2 * local])
                if j == 0:
                    total += nt(dq[rows, :], w[:, 2 * local :])
                if mine:
                    keep.ref[i, :, cols] = total
                else:
                    send.ref[:, cols] = total.astype(BF16)


def blocks_cores_kernel(idx, keep, came_a, came_b, send, mine):
    bit = idx[7]
    keep, came = keep(), (came_a(), came_b())
    piece = send.ref.shape[1]
    for out, where in ((send, 1 - bit), (mine, bit)):
        rows = at(where * piece, piece)
        for i in range(2):
            out.ref[i] = (keep[i, rows, :] + came[i][rows, :].astype(F32)).astype(out.ref.dtype)


def blocks_tp_kernel(idx, mine_a, came_a, mine_b, came_b, three, one, own_two):
    pairs = ((mine_a(), came_a()), (mine_b(), came_b()))

    def total(j):
        mine, came = pairs[j // 2]
        return mine[j % 2] + came[j % 2].astype(F32)

    three.ref[...] = total(3).astype(BF16)
    one.ref[...] = total(1).astype(BF16)
    own_two.ref[0] = total(0)
    own_two.ref[1] = total(2)


def two_kernel(idx, own_two, came, total):
    total.ref[...] = (own_two()[1] + came()[...].astype(F32)).astype(BF16)


def first_prompt_kernel(idx, own_two, one, two, x, gb, dx1, dx, grads):
    own_two, one, two, x, gb, dx1 = own_two(), one(), two(), x(), gb(), dx1()
    back = own_two[0] + one[...].astype(F32) + two[...].astype(F32)
    normed, inverse = norm(x[...].astype(F32))
    grads.ref[0:1, :] = jnp.sum(back * normed, axis=0, keepdims=True)
    grads.ref[1:2, :] = jnp.sum(back, axis=0, keepdims=True)
    dx.ref[...] = (dx1[...] + norm_back(normed, inverse, back, gb[0:1, :])).astype(BF16)


def first_kernel(idx, mine, theirs, x, gb, dx1, dx, grads):
    mine, theirs, x, gb, dx1 = mine(), theirs(), x(), gb(), dx1()
    grads.ref[...] = jnp.zeros_like(grads.ref)

    def one(rows):
        back = mine[rows, :].astype(F32) + theirs[rows, :].astype(F32)
        normed, inverse = norm(x[rows, :].astype(F32))
        grads.ref[0:1, :] += jnp.sum(back * normed, axis=0, keepdims=True)
        grads.ref[1:2, :] += jnp.sum(back, axis=0, keepdims=True)
        dx.ref[rows, :] = (dx1[rows, :] + norm_back(normed, inverse, back, gb[0:1, :])).astype(BF16)

    tiles(mine.shape[0], one)


def cut_right(idx, pairs, send, keep):
    half = idx[1]
    part = send.ref.shape[1]
    for out, where in ((send, 1 - half), (keep, half)):
        cols = at(where * part, part)
        for start in range(0, out.ref.shape[0], 256):
            feats = slice(start, start + 256)
            out.ref[feats, :] = sum(tn(left[rows, feats], right[:, cols]) for left, rows, right in pairs).astype(
                BF16
            )
        out.send()


def grad_down_kernel(idx, act_a, act_b, a0, a1, b0, b1, send, keep):
    pairs = []
    for act, rights in ((act_a(), (a0, a1)), (act_b(), (b0, b1))):
        for i, right in enumerate(rights):
            right = right()
            own = right.shape[0]
            pairs.append((act, slice(i * own, (i + 1) * own), right))
    cut_right(idx, pairs, send, keep)


def grad_up_kernel(idx, a0, a1, b0, b1, du_a, du_b, send, keep):
    half = idx[1]
    lefts = [r() for r in (a0, a1, b0, b1)]
    rights = (du_a(), du_b())
    own = lefts[0].shape[0]
    part = send.ref.shape[0]
    for out, where in ((send, 1 - half), (keep, half)):
        for start in range(0, part, 256):
            feats = at(where * part + start, 256)
            for col in range(0, rights[0].shape[1], 512):
                out.ref[start : start + 256, col : col + 512] = sum(
                    tn(left[:, feats], rights[i // 2][(i % 2) * own : (i % 2 + 1) * own, col : col + 512])
                    for i, left in enumerate(lefts)
                ).astype(BF16)
        out.send()


def grad_qkv_kernel(idx, dkv, dq, dkvq_c, send_out, keep_out, n1p, n1c, n1_two, n1_one, send, keep):
    half = idx[1]
    dkv, dq, dkvq_c, n1p, n1c, n1_two, n1_one = (r() for r in (dkv, dq, dkvq_c, n1p, n1c, n1_two, n1_one))
    part = send.ref.shape[0]
    local = dq.shape[1]
    lefts = (n1p, n1_two.at[0], n1_two.at[1], n1_one.at[0], n1c)
    for out, where in ((send, 1 - half), (keep, half)):
        for start in range(0, part, 256):
            feats = at(where * part + start, 256)
            for i in range(2):
                rights = [*[dkv[j, i] for j in range(4)], dkvq_c[i]]
                out.ref[start : start + 256, i * local : (i + 1) * local] = sum(
                    tn(left[:, feats], right) for left, right in zip(lefts, rights)
                ).astype(BF16)
            out.ref[start : start + 256, 2 * local : 3 * local] = (
                tn(n1p[:, feats], dq[...]) + tn(n1c[:, feats], dkvq_c[2])
            ).astype(BF16)
    for out, proj in ((send, send_out()), (keep, keep_out())):
        few, cols = proj.shape[0] // 4, proj.shape[1] // 2
        for j in range(8):
            out.ref[j * few : (j + 1) * few, 3 * local :] = proj[
                j // 2 * few : (j // 2 + 1) * few, j % 2 * cols : (j % 2 + 1) * cols
            ]


def over_shard_kernel(idx, keep, came, send, mine):
    ctx = idx[2]
    keep, came = keep(), came()
    rows = keep.shape[0] // 4
    for out, order in ((send, (1, 3)), (mine, (0, 2))):
        for place, j in enumerate(order):
            r = at((ctx ^ j) * rows, rows)
            out.ref[place] = (keep[r, :].astype(F32) + came[r, :].astype(F32)).astype(BF16)


def near_kernel(idx, mine, came, send, keep):
    mine, came = mine(), came()
    send.ref[...] = (mine[1].astype(F32) + came[1].astype(F32)).astype(BF16)
    keep.ref[...] = mine[0].astype(F32) + came[0].astype(F32)


def far_kernel(idx, keep, came, total):
    total.ref[...] = (keep()[...] + came()[...].astype(F32)).astype(BF16)


def place_kernel(idx, q0, q1, q2, q3, out):
    ctx = idx[2]
    for j, quarter in enumerate((q0, q1, q2, q3)):
        quarter = quarter()
        out.ref[at((ctx ^ j) * quarter.shape[0], quarter.shape[0]), :] = quarter[...].astype(F32)


def place_two_kernel(idx, q0, q1, q2, q3, key, value, query, proj):
    ctx = idx[2]
    local = key.ref.shape[1]
    few, half = proj.ref.shape[0] // 4, proj.ref.shape[1] // 2
    for j, quarter in enumerate((q0, q1, q2, q3)):
        quarter = quarter()
        rows = at((ctx ^ j) * quarter.shape[0], quarter.shape[0])
        for i, out in enumerate((key, value, query)):
            out.ref[rows, :] = quarter[:, i * local : (i + 1) * local].astype(F32)
        rows = at((ctx ^ j) * few, few)
        proj.ref[rows, :half] = quarter[:few, 3 * local :].astype(F32)
        proj.ref[rows, half:] = quarter[few:, 3 * local :].astype(F32)


def whole_kernel(idx, *refs):
    core = idx[0]
    count = len(refs) // 3
    for i in range(count):
        out = refs[2 * count + i]
        for j, part in enumerate(refs[2 * i : 2 * i + 2]):
            part = part()
            rows = at((core if j == 0 else 1 - core) * part.shape[0], part.shape[0])
            out.ref[rows, :] = part[...]
        out.send()


def whole_quarters_kernel(idx, *refs):
    core, bit = idx[0], idx[7]
    out = refs[-1]
    for place, part in zip((2 * core + bit, 2 * core + 1 - bit, 2 - 2 * core + bit, 3 - 2 * core - bit), refs):
        part = part()
        out.ref[at(place * part.shape[0], part.shape[0]), :] = part[...]


def sum_kernel(idx, keep, came, total):
    keep, came = keep(), came()
    total.ref[...] = (keep[...] + came[...].astype(F32)).astype(BF16)


def small_kernel(idx, first_a, first_b, mid_a, mid_b, last_a, last_b, out):
    first, mid, last = (a()[...] + b()[...] for a, b in ((first_a, first_b), (mid_a, mid_b), (last_a, last_b)))
    out.ref[0:1, :] = first[0:1, :]
    out.ref[1:3, :] = mid[0:2, :]
    out.ref[3:4, :] = last[0:1, :]
    out.ref[4:5, :] = first[1:2, :]
    out.ref[5:7, :] = mid[2:4, :]
    out.ref[7:8, :] = last[1:2, :]


def rope_tables(length):
    freqs = ROPE_BASE ** (-np.arange(HEAD // 2, dtype=np.float32) * np.float32(2.0 / HEAD))
    theta = np.arange(length, dtype=np.float32)[:, None] * freqs.astype(np.float32)[None, :]
    cosine, sine = np.cos(theta), np.sin(theta)
    none = np.zeros_like(sine)
    pairs = ((cosine, cosine), (-sine, none), (none, sine))
    return jnp.asarray(np.stack([np.tile(np.concatenate(pair, axis=1), (1, 2)) for pair in pairs]).astype(np.float32))


def swap(value, axis, bit):
    size = lax.axis_size(axis)
    return lax.ppermute(value, axis, [(i, i ^ bit) for i in range(size)])


class Reduction:
    def __init__(self, line, send, keep, dim, proj=None):
        self.line, self.send, self.keep, self.dim, self.proj = line, send, keep, dim, proj
        self.pair = lax.axis_size("shard") == 2

    def start(self):
        if self.pair:
            self.came = swap(self.line.after(self.send), "shard", 1)

    def arrived(self):
        if self.pair:
            self.came = self.line.after(self.came)

    def summed(self, send, keep, dim):
        full = jnp.concatenate([keep, send], axis=dim)
        part = lax.psum_scatter(full, "shard", scatter_dimension=dim, tiled=True)
        return lax.psum(part, "ctx").astype(F32)

    def over_shard(self):
        if self.pair:
            self.shape = rows, width = self.keep.shape
            send, self.mine = self.line.call(
                over_shard_kernel,
                [self.keep, self.came],
                [((2, rows // 4, width), BF16)] * 2,
                name="over_shard",
            )
            self.moving = swap(send, "ctx", 1)

    def near(self):
        if self.pair:
            shape = self.mine.shape[1:]
            send, self.keep = self.line.call(
                near_kernel, [self.mine, self.moving], [(shape, BF16), (shape, F32)], name="near"
            )
            self.moving = swap(send, "ctx", 2)

    def far(self):
        if self.pair:
            (self.q0,) = self.line.call(
                far_kernel, [self.keep, self.moving], [(self.keep.shape, BF16)], name="far"
            )
            self.q2, self.q1 = swap(self.q0, "ctx", 2), swap(self.q0, "ctx", 1)

    def last(self):
        if self.pair:
            self.q2 = self.line.after(self.q2)
            self.q3 = swap(self.q2, "ctx", 1)

    def settled(self):
        if self.pair:
            self.q1, self.q3 = self.line.after(self.q1, self.q3)

    def placed(self):
        if not self.pair:
            if self.proj is None:
                return [self.summed(self.send, self.keep, self.dim)]
            width = self.keep.shape[1] // 4 * 3
            total = self.summed(self.send[:, :width], self.keep[:, :width], self.dim)
            return [*jnp.split(total, 3, axis=1), self.summed(*self.proj, 1)]
        rows, width = self.shape
        outs, kernel = [((rows, width), F32)], place_kernel
        if self.proj is not None:
            outs = [((rows, width // 4), F32)] * 3 + [(self.proj[1].shape, F32)]
            kernel = place_two_kernel
        return self.line.call(kernel, [self.q0, self.q1, self.q2, self.q3], outs, name="place")


def per_device(
    prompt_x,
    cont_x,
    owner,
    w_query,
    w_key,
    w_value,
    w_out,
    w_up,
    w_down,
    ln_gain,
    ln_bias,
    prompt_grad,
    cont_grad,
):
    shards = lax.axis_size("shard")
    groups, block, width = prompt_x.shape
    conts, cont_len, _ = cont_x.shape
    local = w_query.shape[1]
    hidden = w_up.shape[1]
    rows = groups * block
    own = rows // 2
    piece = own // 2
    part = width // 2
    prompt_len = block * lax.axis_size("ctx")
    core = lax.axis_index("tp") % 2
    bit = lax.axis_index("tp") // 2
    shard = lax.axis_index("shard")
    ctx = lax.axis_index("ctx")
    xs = (prompt_x.reshape(rows, width), cont_x.reshape(rows, width))
    dys = (prompt_grad.reshape(rows, width), cont_grad.reshape(rows, width))

    def both(weight, dim):
        if shards == 2:
            return weight, swap(weight, "shard", 1)
        full = lax.all_gather(weight, "shard", axis=dim, tiled=True)
        return tuple(jnp.split(full, 2, axis=dim))

    half = shard if shards == 2 else jnp.zeros_like(shard)
    which = (owner - shard * groups).reshape(2, conts // 2)
    which = jnp.where(core == 1, which[::-1], which) ^ core
    idx = jnp.concatenate([jnp.stack([core, half, ctx]), which.reshape(conts), jnp.stack([bit])])
    line = Line(idx.astype(jnp.int32))

    small = both(jnp.concatenate([ln_gain, ln_bias], axis=0), 1)
    (gb,) = line.call(gains_kernel, list(small), [((8, width), F32)], name="gains")
    packed = jnp.concatenate([w_key, w_value, w_query], axis=1)
    if shards == 2:
        (packed,) = line.call(
            pack_kernel, [w_key, w_value, w_query], [((part, 3 * local), BF16)], name="pack"
        )
    wqkv = both(packed, 0)
    quarter = lax.dynamic_slice_in_dim(xs[0], core * own + bit * piece, piece, 0)
    far, near = swap(quarter, "ctx", 2), swap(quarter, "ctx", 1)
    tables = rope_tables(prompt_len + cont_len)

    wo = both(line.after(w_out), 1)
    n1p, n1c = (
        line.call(normed_kernel, [x, gb], [((rows, width), BF16)], name="norm_first")[0] for x in xs
    )
    if shards == 2:
        (hidden_packed,) = line.call(
            pack_hidden_kernel, [w_up, w_down], [((2, part, hidden), BF16)], name="pack_hidden"
        )
    wide_rows = (rows, local)
    raw = pltpu.VMEM(wide_rows, F32)
    chunks = []
    for prompt in (True, False):
        chunks += line.call(
            functools.partial(qkv_kernel, prompt),
            [n1p if prompt else n1c, *wqkv, tables],
            [((3, *wide_rows), BF16)],
            [raw],
            name="qkv_prompt" if prompt else "qkv_cont",
        )
        if prompt:
            (normed,) = line.call(norm_pieces_kernel, [near, far, gb], [((own, width), BF16)], name="norm_pieces")
            both_near = [normed, swap(normed, "tp", 2)]
            far, *wo = line.after(far, *wo)
            last_near = swap(far, "ctx", 1)
            if shards == 2:
                hidden_packed = swap(line.after(hidden_packed), "shard", 1)
    kvq_p, kvq_c = chunks
    both_near.append(swap(line.after(normed), "tp", 1))
    (normed,) = line.call(norm_pieces_kernel, [last_near, gb], [((piece, width), BF16)], name="norm_piece")
    one_near = [normed, swap(normed, "tp", 2), swap(normed, "tp", 1)]
    both_near[1] = line.after(both_near[1])
    both_near.append(swap(both_near[1], "tp", 1))
    seen, far_normed = [kvq_p], []

    def far_keys(blocks, parts):
        seen.extend(
            line.call(
                functools.partial(kv_kernel, blocks),
                [*parts, *wqkv, tables],
                [((2 * len(blocks), *wide_rows), BF16), ((len(blocks), rows, width), BF16, "far")],
                [raw],
                name="far_keys",
            )
        )
        far_normed.append(seen.pop())

    far_keys((1, 2), both_near)
    (wo0,) = line.call(stack_kernel, wo, [((2, *wo[0].shape), BF16)], name="stack_out")
    wo0 = line.after(wo0)
    wo2, wo1 = swap(wo0, "tp", 2), swap(wo0, "tp", 1)
    one_near[1] = line.after(one_near[1])
    one_near.append(swap(one_near[1], "tp", 1))
    far_keys((3,), one_near)

    half_o = ((own, local), BF16)
    o_oth_p, o_own_p, probs_p = line.call(
        prompt_kernel,
        seen,
        [half_o, half_o, ((2, local // HEAD, prompt_len, own), BF16, "far")],
        [pltpu.VMEM((local, prompt_len), BF16), pltpu.VMEM((local, own), F32)],
        name="attend_prompt",
    )
    wo1, wo2 = line.after(wo1, wo2)
    wo3 = swap(wo2, "tp", 1)
    pairs = local // HEAD // 2
    mixed = [(o_own_p, o_oth_p)]

    def gathered(o_own, o_oth):
        return o_own, swap(o_oth, "tp", 1), swap(o_own, "tp", 2), swap(o_oth, "tp", 3)

    full_o = [gathered(o_own_p, o_oth_p)]
    all_len = prompt_len + cont_len
    o_oth_c, o_own_c, probs_c = line.call(
        cont_kernel,
        [kvq_c, *seen],
        [half_o, half_o, ((conts, pairs, all_len, 2 * cont_len), BF16, "far")],
        [pltpu.VMEM((local, all_len), BF16), pltpu.VMEM((local, cont_len), F32)],
        name="attend_cont",
    )
    mixed.append((o_own_c, o_oth_c))
    full_o.append(gathered(o_own_c, o_oth_c))

    if shards == 2:
        others = line.call(
            unpack_hidden_kernel, [hidden_packed], [(w_up.shape, BF16), (w_down.shape, BF16)], name="unpack_hidden"
        )
        wu, wd = (w_up, others[0]), (w_down, others[1])
    else:
        wu, wd = both(w_up, 0), both(w_down, 1)

    def mine(value):
        return Part(value, own, lambda idx: idx[0] * own)

    own_rows, own_rows_f = ((own, width), BF16), ((own, width), F32)
    own_pieces = (*own_rows, "cut")

    def swapped(pieces):
        return [swap(piece, "tp", 1) for piece in pieces]

    def summed(keep, send):
        came = swapped(send)
        (total,) = line.call(sum_kernel, [keep, came], [own_rows], name="sum_cores")
        return total, swap(total, "tp", 2)

    stage = []
    for x, os in zip(xs, full_o):
        n3, z, x1 = line.call(
            after_kernel,
            [wo0, os[0], wo1, os[1], wo2, os[2], wo3, os[3], mine(x), gb],
            [own_pieces, own_rows_f, own_rows_f],
            name="after_attention",
        )
        n3t = swapped(n3)
        send, act, slope, keep = line.call(
            up_down_kernel,
            [n3, *wu, n3t, *wd],
            [own_pieces, ((rows, hidden), BF16), ((rows, hidden), BF16), own_rows_f],
            name="up_down",
        )
        stage.append((z, x1, n3, n3t, act, slope, *summed(keep, send)))

    later = []
    for i, dy in enumerate(dys):
        z, x1, n3, n3t, act, slope, total, theirs = stage[i]
        dm, y, grads_last = line.call(
            last_kernel,
            [total, theirs, x1, mine(dy), gb],
            [own_pieces, own_rows, ((2, width), F32)],
            name="last_norm",
        )
        dmt = swapped(dm)
        send, du, keep = line.call(
            down_up_kernel,
            [dm, *wd, slope, dmt, *wu],
            [own_pieces, ((rows, hidden), BF16), own_rows_f],
            name="down_up",
        )
        later.append((y, dm, dmt, du, *summed(keep, send), grads_last))

    middle = []

    def middle_norms(i):
        z, x1 = stage[i][:2]
        total, theirs = later[i][4:6]
        dz, dx1, grads_middle = line.call(
            middle_kernel,
            [total, theirs, x1, mine(dys[i]), gb, z],
            [own_pieces, own_rows_f, ((4, width), F32)],
            name="middle_norms",
        )
        middle.append((dx1, dz, swapped(dz), grads_middle))

    y_p, y_c = later[0][0], later[1][0]

    def assembled(*pairs):
        return line.call(
            whole_kernel,
            [value for pair in pairs for value in pair],
            [((rows, width), BF16)] * len(pairs),
            name="whole",
        )

    middle_norms(0)
    send, keep = line.call(
        grad_down_kernel,
        [stage[0][4], stage[1][4], *later[0][1:3], *later[1][1:3]],
        [((hidden, part), BF16)] * 2,
        name="grad_down",
    )
    down = Reduction(line, send, keep, 1)
    down.start()
    y_p, y_c = line.after(y_p, y_c)
    y_others = [swap(value, "tp", 1) for value in (y_p, y_c)]
    pair_rows = (2, *wide_rows)
    grads, dqp, grad_out = line.call(
        prompt_back_kernel,
        [*middle[0][1:3], *[Far(a) for a in (wo0, *seen, probs_p)], tables, *[Far(o) for o in mixed[0]]],
        [((4, *pair_rows), F32, "far"), (wide_rows, BF16), ((local, width), F32, "far")],
        [
            pltpu.VMEM(wide_rows, BF16),
            pltpu.VMEM((local, prompt_len), BF16),
            pltpu.VMEM((local, own), F32),
            pltpu.VMEM((local // HEAD, prompt_len, own), BF16),
        ],
        name="attend_prompt_back",
    )
    y_others = line.after(*y_others)
    send, keep = line.call(
        grad_up_kernel,
        [*stage[0][2:4], *stage[1][2:4], later[0][3], later[1][3]],
        [((part, hidden), BF16)] * 2,
        name="grad_up",
    )
    middle_norms(1)
    down.over_shard()
    up = Reduction(line, send, keep, 0)
    up.start()
    send_out, keep_out, dkvq_c, dkv_p = line.call(
        cont_back_kernel,
        [*middle[1][1:3], *[Far(a) for a in (wo0, kvq_c, *seen, probs_c, grads)], tables]
        + [*[Far(o) for o in mixed[1]], Far(grad_out)],
        [((local, part), BF16)] * 2 + [((3, *wide_rows), BF16), ((4, *pair_rows), BF16)],
        [
            pltpu.VMEM(wide_rows, BF16),
            pltpu.VMEM((local, all_len), BF16),
            pltpu.VMEM((local, cont_len), F32),
            pltpu.VMEM((pairs, all_len, 2 * cont_len), BF16),
        ],
        name="attend_cont_back",
    )
    down.near()

    def blocks_input(first):
        return line.call(
            functools.partial(blocks_input_kernel, first),
            [dkv_p, Far(dqp), *[Far(w) for w in wqkv]],
            [own_rows] * 2 + [((2, own, width), F32)],
            name="input_blocks",
        )

    def blocks_cores(keep, came):
        send, mine = line.call(
            blocks_cores_kernel,
            [keep, *came],
            [((2, piece, width), BF16), ((2, piece, width), F32)],
            name="blocks_cores",
        )
        return mine, swap(send, "tp", 2)

    *sent, keep_a = blocks_input(0)
    came_a = swapped(sent)
    send, keep = line.call(
        grad_qkv_kernel,
        [dkv_p, Far(dqp), dkvq_c, send_out, keep_out, *[Far(a) for a in (n1p, n1c, *far_normed)]],
        [((part, 4 * local), BF16)] * 2,
        name="grad_qkv",
    )
    qkv = Reduction(line, send, keep, 0, (send_out, keep_out))
    *sent, keep_b = blocks_input(2)
    down.far()
    came_b = swapped(line.after(*sent))
    qkv.start()
    tp_a = blocks_cores(keep_a, came_a)
    up.over_shard()
    tp_b = blocks_cores(keep_b, came_b)
    send_c, keep_c = line.call(
        input_kernel, [dkvq_c, *[Far(w) for w in wqkv]], [own_pieces, own_rows_f], name="input_back"
    )
    yp, yc = assembled((y_p, y_others[0]), (y_c, y_others[1]))
    up.near()
    down.last()
    qkv.over_shard()
    totals_c = summed(keep_c, line.after(*send_c))
    three, one, own_two = line.call(
        blocks_tp_kernel,
        [*tp_a, *tp_b],
        [((piece, width), BF16)] * 2 + [((2, piece, width), F32)],
        name="blocks_tp",
    )
    three, one = swap(three, "ctx", 1), swap(one, "ctx", 1)
    up.far()
    (two,) = line.call(two_kernel, [own_two, three], [((piece, width), BF16)], name="blocks_two")
    two = swap(two, "ctx", 2)
    qkv.near()
    dxc, first_c = line.call(
        first_kernel,
        [*totals_c, mine(xs[1]), gb, Far(middle[1][0])],
        [own_rows, ((2, width), F32)],
        name="first_norm",
    )
    up.last()
    (grad_down,) = down.placed()
    qkv.far()
    dxp, first_p = line.call(
        first_prompt_kernel,
        [
            own_two,
            one,
            two,
            Part(xs[0], piece, lambda idx: idx[0] * own + idx[7] * piece),
            gb,
            Part(middle[0][0], piece, lambda idx: idx[7] * piece),
        ],
        [((piece, width), BF16), ((2, width), F32)],
        name="first_norm_prompt",
    )
    first_other, dxp_across = swap(first_p, "tp", 2), swap(dxp, "tp", 2)
    up.settled()
    first_p = first_p + line.after(first_other)
    (small,) = line.call(
        small_kernel,
        [first_c, first_p, middle[0][3], middle[1][3], later[0][6], later[1][6]],
        [((8, width), F32)],
        name="small",
    )
    small = small + swap(small, "tp", 1)
    qkv.last()
    dxp_across, small = line.after(dxp_across, small)
    dxp_parts = [dxp, dxp_across, swap(dxp, "tp", 1), swap(dxp_across, "tp", 1)]
    if shards == 2:
        small = lax.dynamic_slice_in_dim(small, shard * part, part, 1) + swap(
            lax.dynamic_slice_in_dim(small, (1 - shard) * part, part, 1), "shard", 1
        )
    else:
        small = lax.psum_scatter(small, "shard", scatter_dimension=1, tiled=True)
    dxc = line.after(dxc)
    dxc_other = swap(dxc, "tp", 1)
    (grad_up,) = up.placed()
    (dxc,) = assembled((dxc, dxc_other))
    small = line.after(small)
    small = small + swap(small, "ctx", 1)
    (dxp,) = line.call(whole_quarters_kernel, dxp_parts, [((rows, width), BF16)], name="whole_prompt")
    qkv.settled()
    small = line.after(small)
    small = small + swap(small, "ctx", 2)
    grad_key, grad_value, grad_query, grad_out = qkv.placed()
    return (
        yp.reshape(prompt_x.shape),
        yc.reshape(cont_x.shape),
        dxp.reshape(prompt_x.shape),
        dxc.reshape(cont_x.shape),
        grad_query,
        grad_key,
        grad_value,
        grad_out,
        grad_up,
        grad_down,
        small[:4],
        small[4:],
    )


def solution(mesh):
    placed = (
        P("shard", "ctx", None),
        P(("shard", "ctx"), None, None),
        P(("shard", "ctx")),
        P("shard", "tp"),
        P("shard", "tp"),
        P("shard", "tp"),
        P("tp", "shard"),
        P("shard", "tp"),
        P("tp", "shard"),
        P(None, "shard"),
        P(None, "shard"),
        P("shard", "ctx", None),
        P(("shard", "ctx"), None, None),
    )
    rows = (P("shard", "ctx", None), P(("shard", "ctx"), None, None))
    return jax.shard_map(
        per_device,
        mesh=mesh,
        in_specs=placed,
        out_specs=rows + rows + placed[3:11],
        check_vma=False,
    )
```

```python
import functools

import jax
import jax.numpy as jnp
import numpy as np
from jax import lax
from jax.experimental import pallas as pl
from jax.experimental.pallas import tpu as pltpu
from jax.sharding import PartitionSpec as P

F32 = jnp.float32
BF16 = jnp.bfloat16
HEAD = 64
EPSILON = 1e-05
ROPE_BASE = 10000.0
GELU_COEF = 0.7978845608028654
MASKED = -1e30
MIB = 1024 * 1024
TILE = 128
TILE = 128
TILE = 128
TILE = 128
TILE = 128
TILE = 128
TILE = 128
TILE = 128


def nn(left, right):
    return jnp.dot(left, right, preferred_element_type=F32)


def nt(left, right):
    return lax.dot_general(left, right, (((1,), (1,)), ((), ())), preferred_element_type=F32)


def tn(left, right):
    return lax.dot_general(left, right, (((0,), (0,)), ((), ())), preferred_element_type=F32)


def mean(value):
    return jnp.mean(value, axis=-1, keepdims=True)


def norm(value):
    centred = value - mean(value)
    inverse = lax.rsqrt(mean(centred * centred) + EPSILON)
    return centred * inverse, inverse


def norm_back(normed, inverse, cotangent, gain):
    scaled = cotangent * gain
    return (scaled - mean(scaled) - normed * mean(scaled * normed)) * inverse


def tiles(count, body):
    @pl.loop(0, count // TILE, unroll=2 if count > TILE else 1)
    def _(step):
        body(at(step * TILE, TILE))


def at(start, size):
    return pl.ds(pl.multiple_of(start, size), size)


def turn(value, start, tables, sign):
    rows, width = value.shape
    cosine, minus, plus = (
        jnp.concatenate([tables[i, at(start, rows), :]] * (width // 128), axis=1) for i in range(3)
    )
    left = pltpu.roll(value, width - HEAD // 2, 1)
    right = pltpu.roll(value, HEAD // 2, 1)
    return value * cosine + sign * (left * minus + right * plus)


def head_rows(value, head, count=1):
    which = lax.broadcasted_iota(jnp.int32, value.shape, 0) // (HEAD * count)
    return jnp.where(which == head, value, jnp.zeros_like(value))


def head_lanes(value, head):
    which = lax.broadcasted_iota(jnp.int32, value.shape, 1) // HEAD
    return jnp.where(which == head, value, jnp.zeros_like(value))


class Part:
    def __init__(self, array, rows, start):
        self.array, self.rows, self.start = array, rows, start
        self.shape, self.dtype = array.shape, array.dtype


class Far:
    def __init__(self, array):
        self.array = array
        self.shape, self.dtype = array.shape, array.dtype


class Stack:
    def __init__(self, arrays):
        self.arrays = list(arrays)
        self.rows = [a.shape[0] for a in arrays]
        self.shape, self.dtype = (sum(self.rows), *arrays[0].shape[1:]), arrays[0].dtype


class Coming:
    def __init__(self, ref, copy=None, pieces=()):
        self.ref, self.copy, self.pieces = ref, copy, pieces

    def __call__(self):
        if self.copy is not None:
            self.copy.wait()
            self.copy = None
        start = 0
        for piece, rows in self.pieces:
            self.ref[start : start + rows, :] = piece[...]
            start += rows
        self.pieces = ()
        return self.ref


class Going:
    def __init__(self, ref, kind, targets, semaphores):
        self.ref, self.kind, self.targets, self.semaphores = ref, kind, targets, semaphores
        self.copies = []

    def send(self, *index):
        if self.kind == "far":
            where = index if index else Ellipsis
            copy = pltpu.make_async_copy(self.ref.at[where], self.targets[0].at[where], next(self.semaphores))
            copy.start()
            self.copies.append(copy)

    def close(self):
        if self.kind == "cut":
            start = 0
            for target in self.targets:
                rows = target.shape[0]
                target[...] = self.ref[start : start + rows, :]
                start += rows
        elif not self.copies:
            self.send()
        for copy in self.copies:
            copy.wait()


SENDS = 40
PIECES = 3


def pieces_of(rows):
    tiles_of = rows // 16
    return [16 * (tiles_of // PIECES + (i < tiles_of % PIECES)) for i in range(PIECES)]


class Line:
    def __init__(self, idx):
        self.idx = idx

    def after(self, *values):
        *values, self.idx = lax.optimization_barrier((*values, self.idx))
        return values[0] if len(values) == 1 else values

    def call(self, kernel, inputs, outputs, scratch=(), name=None, margin=12):
        inputs = [Stack(a) if isinstance(a, list) else a for a in inputs]
        given = []
        for a in inputs:
            given += a.arrays if isinstance(a, Stack) else [a.array if isinstance(a, (Part, Far)) else a]
        places = [
            pl.BlockSpec(memory_space=pl.ANY if isinstance(a, Far) else pltpu.VMEM)
            for a in inputs
            for _ in (a.arrays if isinstance(a, Stack) else [a])
        ]
        kinds = [out[2] if len(out) > 2 else "" for out in outputs]
        pieces = [pieces_of(out[0][0]) if kind == "cut" else [out[0][0]] for out, kind in zip(outputs, kinds)]
        shapes = [
            jax.ShapeDtypeStruct((rows, *out[0][1:]), out[1]) for out, cuts in zip(outputs, pieces) for rows in cuts
        ]
        out_places = [
            pl.BlockSpec(memory_space=pl.ANY if kind == "far" else pltpu.VMEM)
            for kind, cuts in zip(kinds, pieces)
            for _ in cuts
        ]
        held = [pltpu.VMEM(a.shape, a.dtype) for a in inputs if isinstance(a, (Far, Stack))]
        held += [pltpu.VMEM(out[0], out[1]) for out, kind in zip(outputs, kinds) if kind]
        own = [*held, *scratch]
        size = sum(int(np.prod(a.shape)) * np.dtype(a.dtype).itemsize for a in own)

        def body(*refs):
            refs = list(refs)
            idx = refs.pop(0)
            sources = [refs.pop(0) for _ in given]
            targets = [refs.pop(0) for _ in shapes]
            semaphores = refs.pop()
            free = (semaphores.at[i] for i in range(SENDS))
            coming = []
            for value in inputs:
                if isinstance(value, Stack):
                    buffer = refs.pop(0)
                    coming.append(Coming(buffer, pieces=[(sources.pop(0), rows) for rows in value.rows]))
                    continue
                source, copy = sources.pop(0), None
                if isinstance(value, Part):
                    source = source.at[at(value.start(idx), value.rows), :]
                elif isinstance(value, Far):
                    buffer = refs.pop(0)
                    copy = pltpu.make_async_copy(source, buffer, next(free))
                    copy.start()
                    source = buffer
                coming.append(Coming(source, copy))
            going = []
            for kind, cuts in zip(kinds, pieces):
                mine = [targets.pop(0) for _ in cuts]
                going.append(Going(refs.pop(0) if kind else mine[0], kind, mine, free))
            kernel(idx, *coming, *going, *refs)
            for arrival in coming:
                arrival()
            for out in going:
                out.close()

        out = pl.pallas_call(
            body,
            out_shape=shapes,
            in_specs=[pl.BlockSpec(memory_space=pltpu.SMEM), *places],
            out_specs=out_places,
            scratch_shapes=[*own, pltpu.SemaphoreType.DMA((SENDS,))],
            compiler_params=pltpu.CompilerParams(vmem_limit_bytes=size + margin * MIB),
            cost_estimate=pl.CostEstimate(flops=1000, bytes_accessed=1000, transcendentals=0),
            name=name,
        )(self.idx, *given)
        out = list(out)
        out[-1], self.idx = lax.optimization_barrier((out[-1], self.idx))
        return [[out.pop(0) for _ in cuts] if kind == "cut" else out.pop(0) for kind, cuts in zip(kinds, pieces)]


def stack_kernel(idx, one, two, out):
    out.ref[0] = one()[...]
    out.ref[1] = two()[...]


def gains_kernel(idx, own, other, both):
    half = idx[1]
    part = own.ref.shape[1]
    for side, value in enumerate((own, other)):
        cols = at((half if side == 0 else 1 - half) * part, part)
        both.ref[:, cols] = value()[...].astype(F32)


def normed_rows(x, first, n1, start, count, gain, bias):
    @pl.loop(0, count // TILE, unroll=2 if count > TILE else 1)
    def _(step):
        normed, _ = norm(x[at(first + step * TILE, TILE), :].astype(F32))
        n1[at(start + step * TILE, TILE), :] = (normed * gain + bias).astype(BF16)


def pack_kernel(idx, wk, wv, wq, packed):
    local = wk.ref.shape[1]
    for i, w in enumerate((wk, wv, wq)):
        packed.ref[:, i * local : (i + 1) * local] = w()[...]


def pack_hidden_kernel(idx, wu, wd, packed):
    wu, wd = wu(), wd()
    part = wd.shape[1]
    packed.ref[0] = wu[...]
    packed.ref[1, :, :part] = wd[:part, :]
    packed.ref[1, :, part:] = wd[part:, :]


def unpack_hidden_kernel(idx, packed, wu, wd):
    packed = packed()
    part = wd.ref.shape[1]
    wu.ref[...] = packed[0]
    wd.ref[:part, :] = packed[1, :, :part]
    wd.ref[part:, :] = packed[1, :, part:]


def normed_dots(n1, raw, half, own, other, which):
    rows, width = n1.shape
    part = width // 2
    local = raw.shape[1]
    cols = slice(which * local, (which + 1) * local)
    for start in range(0, rows, 256):
        raw[start : start + 256, :] = nn(n1[start : start + 256, at(half * part, part)], own[:, cols]) + nn(
            n1[start : start + 256, at((1 - half) * part, part)], other[:, cols]
        )


def normed_kernel(idx, x, gb, n1):
    core = idx[0]
    gb, x = gb(), x()
    own = x.shape[0] // 2
    for side in range(2):
        first = (core if side == 0 else 1 - core) * own
        normed_rows(x, first, n1.ref, side * own, own, gb[0:1, :], gb[4:5, :])


def qkv_kernel(prompt, idx, n1, w_own, w_oth, tables, out, raw):
    half, ctx = idx[1], idx[2]
    n1, w_own, w_oth = n1(), w_own(), w_oth()
    rows = n1.shape[0]
    own = rows // 2
    tables = tables()

    def place(start):
        if prompt:
            return ctx * own + start % own
        return tables.shape[1] - 128

    for which, scale in ((0, 1.0), (2, HEAD**-0.5)):
        normed_dots(n1, raw, half, w_own, w_oth, which)
        for start in range(0, rows, 128):
            turned = turn(raw[start : start + 128, :], place(start), tables, 1.0)
            out.ref[which, start : start + 128, :] = turned.astype(BF16) * BF16(scale)
    normed_dots(n1, raw, half, w_own, w_oth, 1)
    out.ref[1] = raw[...].astype(BF16)


def norm_pieces_kernel(idx, *refs):
    gb, out = refs[-2](), refs[-1]
    for i, x in enumerate(refs[:-2]):
        x = x()
        normed_rows(x, 0, out.ref, i * x.shape[0], x.shape[0], gb[0:1, :], gb[4:5, :])


def kv_kernel(blocks, idx, own_near, own_far, oth_near, oth_far, w_own, w_oth, tables, out, kept, raw):
    half, ctx, bit = idx[1], idx[2], idx[7]
    parts = [r() for r in (own_near, own_far, oth_near, oth_far)]
    tables = tables()
    w_own, w_oth = w_own(), w_oth()
    piece = parts[0].shape[0] // len(blocks)
    own = 2 * piece
    for i, block in enumerate(blocks):
        n1 = kept.ref.at[i]
        for place, x in zip((bit, 1 - bit, 2 + bit, 3 - bit), parts):
            n1[at(place * piece, piece), :] = x[i * piece : (i + 1) * piece, :]
        normed_dots(n1, raw, half, w_own, w_oth, 0)
        for start in range(0, 2 * own, 128):
            turned = turn(raw[start : start + 128, :], (ctx ^ block) * own + start % own, tables, 1.0)
            out.ref[2 * i, start : start + 128, :] = turned.astype(BF16)
        normed_dots(n1, raw, half, w_own, w_oth, 1)
        out.ref[2 * i + 1] = raw[...].astype(BF16)


def keys_values(near, two, one):
    near, two, one = near(), two(), one()
    return [near.at[0], two.at[0], two.at[2], one.at[0]], [near.at[1], two.at[1], two.at[3], one.at[1]]


def softmax_keys(scores):
    top = functools.reduce(jnp.maximum, [jnp.max(s, axis=0, keepdims=True) for s in scores])
    scores = [jnp.exp(s - top) for s in scores]
    inverse = 1.0 / sum(jnp.sum(s, axis=0, keepdims=True) for s in scores)
    return [(s * inverse).astype(BF16) for s in scores]


def prompt_kernel(idx, near, two, one, o_oth, o_own, p, vt, ot):
    ctx = idx[2]
    q = near().at[2]
    ks, vs = keys_values(near, two, one)
    own = o_own.ref.shape[0]
    width = q.shape[1]
    key = lax.broadcasted_iota(jnp.int32, (own, own), 0)
    row = lax.broadcasted_iota(jnp.int32, (own, own), 1)
    seen = key <= row
    for side, out in ((1, o_oth), (0, o_own)):
        rows = slice(side * own, (side + 1) * own)
        qt = q[rows, :].T
        for j in range(4):
            vt[:, j * own : (j + 1) * own] = vs[j][rows, :].T
        for head in range(width // HEAD):
            feats = slice(head * HEAD, (head + 1) * HEAD)
            qh = head_rows(qt, head)
            scores = []
            for j in range(4):
                part = nn(ks[j][rows, :], qh)
                if j == 0:
                    part = jnp.where(seen, part, MASKED)
                else:
                    part = part + jnp.where((ctx ^ j) < ctx, 0.0, MASKED).astype(F32)
                scores.append(part)
            for j, probs in enumerate(softmax_keys(scores)):
                p.ref[side, head, j * own : (j + 1) * own, :] = probs
            p.send(side, head)
            ot[feats, :] = nn(vt[feats, :], p.ref[side, head])
        out.ref[...] = ot[...].T.astype(BF16)
        out.send()


def cont_kernel(idx, mine_kvq, near, two, one, o_oth, o_own, p, vt, ot):
    mine_kvq = mine_kvq()
    k, v, q = (mine_kvq.at[i] for i in range(3))
    ks, vs = keys_values(near, two, one)
    own = o_own.ref.shape[0]
    width = q.shape[1]
    length = 128
    per = own // length
    key = lax.broadcasted_iota(jnp.int32, (length, 2 * length), 0)
    row = lax.broadcasted_iota(jnp.int32, (length, 2 * length), 1) % length
    seen = key <= row
    for c in [*range(per, 2 * per), *range(per)]:
        group = idx[3 + c]
        mine = slice(c * length, (c + 1) * length)
        theirs = at(group * own, own)
        qt = q[mine, :].T
        for j in range(4):
            vt[:, j * own : (j + 1) * own] = vs[j][theirs, :].T
        vt[:, 4 * own :] = v[mine, :].T
        for pair in range(width // HEAD // 2):
            feats = slice(pair * 2 * HEAD, (pair + 1) * 2 * HEAD)
            q2 = jnp.concatenate([head_rows(qt, 2 * pair), head_rows(qt, 2 * pair + 1)], axis=1)
            scores = [nn(ks[j][theirs, :], q2) for j in range(4)]
            scores.append(jnp.where(seen, nn(k[mine, :], q2), MASKED))
            probs = softmax_keys(scores)
            for j in range(4):
                p.ref[c, pair, j * own : (j + 1) * own, :] = probs[j]
            p.ref[c, pair, 4 * own :, :] = probs[4]
            p.send(c, pair)
            both = nn(vt[feats, :], p.ref[c, pair])
            first = pair * 2 * HEAD
            ot[first : first + HEAD, :] = both[:HEAD, :length]
            ot[first + HEAD : first + 2 * HEAD, :] = both[HEAD:, length:]
        out = o_own if c < per else o_oth
        place = c % per * length
        out.ref[place : place + length, :] = ot[...].T.astype(BF16)
        if c % per == per - 1:
            out.send()


def after_kernel(idx, w0, o0, w1, o1, w2, o2, w3, o3, x, gb, n3, z, x1):
    half = idx[1]
    part = z.ref.shape[1] // 2
    pairs = [(o(), w()) for o, w in ((o0, w0), (o1, w1), (o2, w2), (o3, w3))]
    for side in range(2):
        cols = at((half if side == 0 else 1 - half) * part, part)
        z.ref[:, cols] = sum(nn(o[...], w[side]) for o, w in pairs)
    z.send()
    x, gb = x(), gb()

    def one(rows):
        normed, _ = norm(z.ref[rows, :])
        after = x[rows, :].astype(F32) + (normed * gb[1:2, :] + gb[5:6, :])
        x1.ref[rows, :] = after
        normed, _ = norm(after)
        n3.ref[rows, :] = (normed * gb[2:3, :] + gb[6:7, :]).astype(BF16)

    tiles(x.shape[0], one)


def up_down_kernel(idx, n3o, wua, wub, n3t, wda, wdb, send, act, slope, keep):
    half = idx[1]
    own = n3o.ref.shape[0]
    part = n3o.ref.shape[1] // 2
    n3o, wua, wub = n3o(), wua(), wub()
    hidden = wua.shape[1]
    for side, n3 in enumerate((n3o, n3t)):
        if side == 1:
            n3 = n3()
        rows = slice(side * own, (side + 1) * own)
        for start in range(0, hidden, 256):
            cols = slice(start, start + 256)
            pre = nn(n3[:, at(half * part, part)], wua[:, cols]) + nn(
                n3[:, at((1 - half) * part, part)], wub[:, cols]
            )
            square = pre * pre
            tanh = jnp.tanh(GELU_COEF * (pre + 0.044715 * pre * square))
            up = 0.5 * (1.0 + tanh)
            act.ref[rows, cols] = (pre * up).astype(BF16)
            inner = GELU_COEF * (1.0 + (3.0 * 0.044715) * square)
            slope.ref[rows, cols] = (up + 0.5 * pre * (1.0 - tanh * tanh) * inner).astype(BF16)
        act.send(rows)
        slope.send(rows)
    weights = (wda(), wdb())
    for out, rows in ((send, slice(own, 2 * own)), (keep, slice(0, own))):
        for side, w in enumerate(weights):
            cols = at((half if side == 0 else 1 - half) * part, part)
            out.ref[:, cols] = nn(act.ref[rows, :], w[...]).astype(out.ref.dtype)
        out.send()


def last_kernel(idx, mine, theirs, x1, cotangent, gb, dm, y, grads):
    mine, theirs, cotangent, gb, x1 = mine(), theirs(), cotangent(), gb(), x1()
    grads.ref[...] = jnp.zeros_like(grads.ref)

    def one(rows):
        total = mine[rows, :].astype(F32) + theirs[rows, :].astype(F32)
        normed, inverse = norm(total)
        y.ref[rows, :] = (x1[rows, :] + (normed * gb[3:4, :] + gb[7:8, :])).astype(BF16)
        dy = cotangent[rows, :].astype(F32)
        dm.ref[rows, :] = norm_back(normed, inverse, dy, gb[3:4, :]).astype(BF16)
        grads.ref[0:1, :] += jnp.sum(dy * normed, axis=0, keepdims=True)
        grads.ref[1:2, :] += jnp.sum(dy, axis=0, keepdims=True)

    tiles(mine.shape[0], one)


def down_up_kernel(idx, dmo, wda, wdb, slope, dmt, wua, wub, send, du, keep):
    half = idx[1]
    own = dmo.ref.shape[0]
    part = dmo.ref.shape[1] // 2
    dmo, wda, wdb, slope = dmo(), wda(), wdb(), slope()
    for side, dm in enumerate((dmo, dmt)):
        if side == 1:
            dm = dm()
        rows = slice(side * own, (side + 1) * own)
        for start in range(0, slope.shape[1], 256):
            cols = slice(start, start + 256)
            back = nt(dm[:, at(half * part, part)], wda[cols, :]) + nt(
                dm[:, at((1 - half) * part, part)], wdb[cols, :]
            )
            du.ref[rows, cols] = (back * slope[rows, cols].astype(F32)).astype(BF16)
        du.send(rows)
    weights = (wua(), wub())
    for out, rows in ((send, slice(own, 2 * own)), (keep, slice(0, own))):
        for side, w in enumerate(weights):
            cols = at((half if side == 0 else 1 - half) * part, part)
            out.ref[:, cols] = nt(du.ref[rows, :], w[...]).astype(out.ref.dtype)
        out.send()


def middle_kernel(idx, mine, theirs, x1, cotangent, gb, z, dz, dx1, grads):
    mine, theirs, x1, cotangent, gb, z = mine(), theirs(), x1(), cotangent(), gb(), z()
    grads.ref[...] = jnp.zeros_like(grads.ref)

    def one(rows):
        back = mine[rows, :].astype(F32) + theirs[rows, :].astype(F32)
        normed, inverse = norm(x1[rows, :])
        grads.ref[1:2, :] += jnp.sum(back * normed, axis=0, keepdims=True)
        grads.ref[3:4, :] += jnp.sum(back, axis=0, keepdims=True)
        after = cotangent[rows, :].astype(F32) + norm_back(normed, inverse, back, gb[2:3, :])
        dx1.ref[rows, :] = after
        normed, inverse = norm(z[rows, :])
        grads.ref[0:1, :] += jnp.sum(after * normed, axis=0, keepdims=True)
        grads.ref[2:3, :] += jnp.sum(after, axis=0, keepdims=True)
        dz.ref[rows, :] = norm_back(normed, inverse, after, gb[1:2, :]).astype(BF16)

    tiles(mine.shape[0], one)


def spread_out(half, dzo, dzt, wo, do):
    own = dzo.shape[0]
    part = dzo.shape[1] // 2
    for side, dz in enumerate((dzo, dzt)):
        do[side * own : (side + 1) * own, :] = (
            nt(dz[:, at(half * part, part)], wo[0]) + nt(dz[:, at((1 - half) * part, part)], wo[1])
        ).astype(BF16)


def prompt_back_kernel(idx, dzo, dzt, wo, near, two, one, p, tables, o_own, o_oth, dkv, dq, grad_out, do, kt, dqt, dst):
    half, ctx = idx[1], idx[2]
    dzo, dzt, wo = dzo(), dzt(), wo()
    spread_out(half, dzo, dzt, wo, do)
    q = near().at[2]
    ks, vs = keys_values(near, two, one)
    p = p()
    tables = tables()
    own = dzo.shape[0]
    width = q.shape[1]
    heads = width // HEAD
    mixed = (o_own(), o_oth())
    for start in range(0, dzo.shape[1], 512):
        cols = slice(start, start + 512)
        grad_out.ref[:, cols] = tn(mixed[0][...], dzo[:, cols]) + tn(mixed[1][...], dzt[:, cols])
    grad_out.send()
    for side in range(2):
        rows = slice(side * own, (side + 1) * own)
        dot = do[rows, :].T
        for j in range(4):
            kt[:, j * own : (j + 1) * own] = ks[j][rows, :].T
        for head in range(heads):
            feats = slice(head * HEAD, (head + 1) * HEAD)
            doh = head_rows(dot, head)
            probs = [p[side, head, j * own : (j + 1) * own, :].astype(F32) for j in range(4)]
            terms = [probs[j] * nn(vs[j][rows, :], doh) for j in range(4)]
            centre = sum(jnp.sum(t, axis=0, keepdims=True) for t in terms)
            for j in range(4):
                dst[head, j * own : (j + 1) * own, :] = (terms[j] - probs[j] * centre).astype(BF16)
            dqt[feats, :] = nn(kt[feats, :], dst[head]) * (HEAD**-0.5)
        for j in range(4):
            keys = slice(j * own, (j + 1) * own)
            dkv.ref[j, 0, rows, :] = sum(
                nn(dst[head, keys, :], head_lanes(q[rows, :], head)) for head in range(heads)
            )
            dkv.ref[j, 1, rows, :] = sum(
                nn(p[side, head, keys, :], head_lanes(do[rows, :], head)) for head in range(heads)
            )
        dqf = dqt[...].T
        for start in range(0, own, 128):
            dq.ref[side * own + start : side * own + start + 128, :] = turn(
                dqf[start : start + 128, :], ctx * own + start, tables, -1.0
            ).astype(BF16)


def cont_back_kernel(idx, dzo, dzt, wo, mine_kvq, near, two, one, p, adds, tables, o_own, o_oth, grad_out, *refs):
    send, keep, dkvq, blocks = refs[:4]
    do, kt, dqt, dst = refs[4:]
    half, ctx = idx[1], idx[2]
    dzo, dzt, wo = dzo(), dzt(), wo()
    spread_out(half, dzo, dzt, wo, do)
    mine_kvq = mine_kvq()
    k, v, q = (mine_kvq.at[i] for i in range(3))
    ks, vs = keys_values(near, two, one)
    p, total = p(), adds()
    tables = tables()
    own = dzo.shape[0]
    width = q.shape[1]
    pairs = width // HEAD // 2
    length = 128
    last = tables.shape[1] - length
    mixed, grad_out = (o_own(), o_oth()), grad_out()
    part = dzo.shape[1] // 2
    for out, where in ((send, 1 - half), (keep, half)):
        cols = at(where * part, part)
        out.ref[...] = (
            grad_out[:, cols] + (tn(mixed[0][...], dzo[:, cols]) + tn(mixed[1][...], dzt[:, cols]))
        ).astype(BF16)
    for c in range(2 * own // length):
        group = idx[3 + c]
        mine = slice(c * length, (c + 1) * length)
        theirs = at(group * own, own)
        dot = do[mine, :].T
        for j in range(4):
            kt[:, j * own : (j + 1) * own] = ks[j][theirs, :].T
        kt[:, 4 * own :] = k[mine, :].T
        for pair in range(pairs):
            feats = slice(pair * 2 * HEAD, (pair + 1) * 2 * HEAD)
            do2 = jnp.concatenate([head_rows(dot, 2 * pair), head_rows(dot, 2 * pair + 1)], axis=1)
            probs = [p[c, pair, j * own : (j + 1) * own, :].astype(F32) for j in range(4)]
            probs.append(p[c, pair, 4 * own :, :].astype(F32))
            terms = [probs[j] * nn(vs[j][theirs, :], do2) for j in range(4)]
            terms.append(probs[4] * nn(v[mine, :], do2))
            centre = sum(jnp.sum(t, axis=0, keepdims=True) for t in terms)
            for j in range(4):
                dst[pair, j * own : (j + 1) * own, :] = (terms[j] - probs[j] * centre).astype(BF16)
            dst[pair, 4 * own :, :] = (terms[4] - probs[4] * centre).astype(BF16)
            both = nn(kt[feats, :], dst[pair]) * (HEAD**-0.5)
            first = pair * 2 * HEAD
            dqt[first : first + HEAD, :] = both[:HEAD, :length]
            dqt[first + HEAD : first + 2 * HEAD, :] = both[HEAD:, length:]
        q2, do2 = (
            [
                jnp.concatenate([head_lanes(t[mine, :], 2 * r), head_lanes(t[mine, :], 2 * r + 1)], axis=0)
                for r in range(pairs)
            ]
            for t in (q, do)
        )
        for j in range(4):
            keys = slice(j * own, (j + 1) * own)
            total[j, 0, theirs, :] += sum(nn(dst[r, keys, :], q2[r]) for r in range(pairs))
            total[j, 1, theirs, :] += sum(nn(p[c, r, keys, :], do2[r]) for r in range(pairs))
        dkf = sum(nn(dst[r, 4 * own :, :], q2[r]) for r in range(pairs))
        dkvq.ref[1, mine, :] = sum(nn(p[c, r, 4 * own :, :], do2[r]) for r in range(pairs)).astype(BF16)
        dkvq.ref[0, mine, :] = turn(dkf, last, tables, -1.0).astype(BF16)
        dkvq.ref[2, mine, :] = turn(dqt[...].T, last, tables, -1.0).astype(BF16)
    for j in range(4):
        for start in range(0, 2 * own, 128):
            r = slice(start, start + 128)
            blocks.ref[j, 0, r, :] = turn(
                total[j, 0, r, :], (ctx ^ j) * own + start % own, tables, -1.0
            ).astype(BF16)
        blocks.ref[j, 1] = total[j, 1].astype(BF16)


def input_kernel(idx, dkvq, w_own, w_oth, send, keep):
    half = idx[1]
    dkvq, weights = dkvq(), (w_own(), w_oth())
    own = keep.ref.shape[0]
    part = keep.ref.shape[1] // 2
    local = dkvq.shape[2]
    for out, rows in ((send, slice(own, 2 * own)), (keep, slice(0, own))):
        for side, w in enumerate(weights):
            cols = at((half if side == 0 else 1 - half) * part, part)
            total = sum(nt(dkvq[i, rows, :], w[:, i * local : (i + 1) * local]) for i in range(3))
            out.ref[:, cols] = total.astype(out.ref.dtype)


def blocks_input_kernel(first, idx, dkv, dq, w_own, w_oth, send_a, send_b, keep):
    half = idx[1]
    dkv, dq, weights = dkv(), dq(), (w_own(), w_oth())
    own = keep.ref.shape[1]
    part = keep.ref.shape[2] // 2
    local = dq.shape[1]
    for i, send in enumerate((send_a, send_b)):
        j = first + i
        for mine, rows in ((False, slice(own, 2 * own)), (True, slice(0, own))):
            for side, w in enumerate(weights):
                cols = at((half if side == 0 else 1 - half) * part, part)
                total = nt(dkv[j, 0, rows, :], w[:, :local]) + nt(dkv[j, 1, rows, :], w[:, local : 2 * local])
                if j == 0:
                    total += nt(dq[rows, :], w[:, 2 * local :])
                if mine:
                    keep.ref[i, :, cols] = total
                else:
                    send.ref[:, cols] = total.astype(BF16)


def blocks_cores_kernel(idx, keep, came_a, came_b, send, mine):
    bit = idx[7]
    keep, came = keep(), (came_a(), came_b())
    piece = send.ref.shape[1]
    for out, where in ((send, 1 - bit), (mine, bit)):
        rows = at(where * piece, piece)
        for i in range(2):
            out.ref[i] = (keep[i, rows, :] + came[i][rows, :].astype(F32)).astype(out.ref.dtype)


def blocks_tp_kernel(idx, mine_a, came_a, mine_b, came_b, three, one, own_two):
    pairs = ((mine_a(), came_a()), (mine_b(), came_b()))

    def total(j):
        mine, came = pairs[j // 2]
        return mine[j % 2] + came[j % 2].astype(F32)

    three.ref[...] = total(3).astype(BF16)
    one.ref[...] = total(1).astype(BF16)
    own_two.ref[0] = total(0)
    own_two.ref[1] = total(2)


def two_kernel(idx, own_two, came, total):
    total.ref[...] = (own_two()[1] + came()[...].astype(F32)).astype(BF16)


def first_prompt_kernel(idx, own_two, one, two, x, gb, dx1, dx, grads):
    own_two, one, two, x, gb, dx1 = own_two(), one(), two(), x(), gb(), dx1()
    back = own_two[0] + one[...].astype(F32) + two[...].astype(F32)
    normed, inverse = norm(x[...].astype(F32))
    grads.ref[0:1, :] = jnp.sum(back * normed, axis=0, keepdims=True)
    grads.ref[1:2, :] = jnp.sum(back, axis=0, keepdims=True)
    dx.ref[...] = (dx1[...] + norm_back(normed, inverse, back, gb[0:1, :])).astype(BF16)


def first_kernel(idx, mine, theirs, x, gb, dx1, dx, grads):
    mine, theirs, x, gb, dx1 = mine(), theirs(), x(), gb(), dx1()
    grads.ref[...] = jnp.zeros_like(grads.ref)

    def one(rows):
        back = mine[rows, :].astype(F32) + theirs[rows, :].astype(F32)
        normed, inverse = norm(x[rows, :].astype(F32))
        grads.ref[0:1, :] += jnp.sum(back * normed, axis=0, keepdims=True)
        grads.ref[1:2, :] += jnp.sum(back, axis=0, keepdims=True)
        dx.ref[rows, :] = (dx1[rows, :] + norm_back(normed, inverse, back, gb[0:1, :])).astype(BF16)

    tiles(mine.shape[0], one)


def cut_right(idx, pairs, send, keep):
    half = idx[1]
    part = send.ref.shape[1]
    for out, where in ((send, 1 - half), (keep, half)):
        cols = at(where * part, part)
        for start in range(0, out.ref.shape[0], 256):
            feats = slice(start, start + 256)
            out.ref[feats, :] = sum(tn(left[rows, feats], right[:, cols]) for left, rows, right in pairs).astype(
                BF16
            )
        out.send()


def grad_down_kernel(idx, act_a, act_b, a0, a1, b0, b1, send, keep):
    pairs = []
    for act, rights in ((act_a(), (a0, a1)), (act_b(), (b0, b1))):
        for i, right in enumerate(rights):
            right = right()
            own = right.shape[0]
            pairs.append((act, slice(i * own, (i + 1) * own), right))
    cut_right(idx, pairs, send, keep)


def grad_up_kernel(idx, a0, a1, b0, b1, du_a, du_b, send, keep):
    half = idx[1]
    lefts = [r() for r in (a0, a1, b0, b1)]
    rights = (du_a(), du_b())
    own = lefts[0].shape[0]
    part = send.ref.shape[0]
    for out, where in ((send, 1 - half), (keep, half)):
        for start in range(0, part, 256):
            feats = at(where * part + start, 256)
            for col in range(0, rights[0].shape[1], 512):
                out.ref[start : start + 256, col : col + 512] = sum(
                    tn(left[:, feats], rights[i // 2][(i % 2) * own : (i % 2 + 1) * own, col : col + 512])
                    for i, left in enumerate(lefts)
                ).astype(BF16)
        out.send()


def grad_qkv_kernel(idx, dkv, dq, dkvq_c, send_out, keep_out, n1p, n1c, n1_two, n1_one, send, keep):
    half = idx[1]
    dkv, dq, dkvq_c, n1p, n1c, n1_two, n1_one = (r() for r in (dkv, dq, dkvq_c, n1p, n1c, n1_two, n1_one))
    part = send.ref.shape[0]
    local = dq.shape[1]
    lefts = (n1p, n1_two.at[0], n1_two.at[1], n1_one.at[0], n1c)
    for out, where in ((send, 1 - half), (keep, half)):
        for start in range(0, part, 256):
            feats = at(where * part + start, 256)
            for i in range(2):
                rights = [*[dkv[j, i] for j in range(4)], dkvq_c[i]]
                out.ref[start : start + 256, i * local : (i + 1) * local] = sum(
                    tn(left[:, feats], right) for left, right in zip(lefts, rights)
                ).astype(BF16)
            out.ref[start : start + 256, 2 * local : 3 * local] = (
                tn(n1p[:, feats], dq[...]) + tn(n1c[:, feats], dkvq_c[2])
            ).astype(BF16)
    for out, proj in ((send, send_out()), (keep, keep_out())):
        few, cols = proj.shape[0] // 4, proj.shape[1] // 2
        for j in range(8):
            out.ref[j * few : (j + 1) * few, 3 * local :] = proj[
                j // 2 * few : (j // 2 + 1) * few, j % 2 * cols : (j % 2 + 1) * cols
            ]


def over_shard_kernel(idx, keep, came, send, mine):
    ctx = idx[2]
    keep, came = keep(), came()
    rows = keep.shape[0] // 4
    for out, order in ((send, (1, 3)), (mine, (0, 2))):
        for place, j in enumerate(order):
            r = at((ctx ^ j) * rows, rows)
            out.ref[place] = (keep[r, :].astype(F32) + came[r, :].astype(F32)).astype(BF16)


def near_kernel(idx, mine, came, send, keep):
    mine, came = mine(), came()
    send.ref[...] = (mine[1].astype(F32) + came[1].astype(F32)).astype(BF16)
    keep.ref[...] = mine[0].astype(F32) + came[0].astype(F32)


def far_kernel(idx, keep, came, total):
    total.ref[...] = (keep()[...] + came()[...].astype(F32)).astype(BF16)


def place_kernel(idx, q0, q1, q2, q3, out):
    ctx = idx[2]
    for j, quarter in enumerate((q0, q1, q2, q3)):
        quarter = quarter()
        out.ref[at((ctx ^ j) * quarter.shape[0], quarter.shape[0]), :] = quarter[...].astype(F32)


def place_two_kernel(idx, q0, q1, q2, q3, key, value, query, proj):
    ctx = idx[2]
    local = key.ref.shape[1]
    few, half = proj.ref.shape[0] // 4, proj.ref.shape[1] // 2
    for j, quarter in enumerate((q0, q1, q2, q3)):
        quarter = quarter()
        rows = at((ctx ^ j) * quarter.shape[0], quarter.shape[0])
        for i, out in enumerate((key, value, query)):
            out.ref[rows, :] = quarter[:, i * local : (i + 1) * local].astype(F32)
        rows = at((ctx ^ j) * few, few)
        proj.ref[rows, :half] = quarter[:few, 3 * local :].astype(F32)
        proj.ref[rows, half:] = quarter[few:, 3 * local :].astype(F32)


def whole_kernel(idx, *refs):
    core = idx[0]
    count = len(refs) // 3
    for i in range(count):
        out = refs[2 * count + i]
        for j, part in enumerate(refs[2 * i : 2 * i + 2]):
            part = part()
            rows = at((core if j == 0 else 1 - core) * part.shape[0], part.shape[0])
            out.ref[rows, :] = part[...]
        out.send()


def whole_quarters_kernel(idx, *refs):
    core, bit = idx[0], idx[7]
    out = refs[-1]
    for place, part in zip((2 * core + bit, 2 * core + 1 - bit, 2 - 2 * core + bit, 3 - 2 * core - bit), refs):
        part = part()
        out.ref[at(place * part.shape[0], part.shape[0]), :] = part[...]


def sum_kernel(idx, keep, came, total):
    keep, came = keep(), came()
    total.ref[...] = (keep[...] + came[...].astype(F32)).astype(BF16)


def small_kernel(idx, first_a, first_b, mid_a, mid_b, last_a, last_b, out):
    first, mid, last = (a()[...] + b()[...] for a, b in ((first_a, first_b), (mid_a, mid_b), (last_a, last_b)))
    out.ref[0:1, :] = first[0:1, :]
    out.ref[1:3, :] = mid[0:2, :]
    out.ref[3:4, :] = last[0:1, :]
    out.ref[4:5, :] = first[1:2, :]
    out.ref[5:7, :] = mid[2:4, :]
    out.ref[7:8, :] = last[1:2, :]


def rope_tables(length):
    freqs = ROPE_BASE ** (-np.arange(HEAD // 2, dtype=np.float32) * np.float32(2.0 / HEAD))
    theta = np.arange(length, dtype=np.float32)[:, None] * freqs.astype(np.float32)[None, :]
    cosine, sine = np.cos(theta), np.sin(theta)
    none = np.zeros_like(sine)
    pairs = ((cosine, cosine), (-sine, none), (none, sine))
    return jnp.asarray(np.stack([np.tile(np.concatenate(pair, axis=1), (1, 2)) for pair in pairs]).astype(np.float32))


def swap(value, axis, bit):
    size = lax.axis_size(axis)
    return lax.ppermute(value, axis, [(i, i ^ bit) for i in range(size)])


class Reduction:
    def __init__(self, line, send, keep, dim, proj=None):
        self.line, self.send, self.keep, self.dim, self.proj = line, send, keep, dim, proj
        self.pair = lax.axis_size("shard") == 2

    def start(self):
        if self.pair:
            self.came = swap(self.line.after(self.send), "shard", 1)

    def arrived(self):
        if self.pair:
            self.came = self.line.after(self.came)

    def summed(self, send, keep, dim):
        full = jnp.concatenate([keep, send], axis=dim)
        part = lax.psum_scatter(full, "shard", scatter_dimension=dim, tiled=True)
        return lax.psum(part, "ctx").astype(F32)

    def over_shard(self):
        if self.pair:
            self.shape = rows, width = self.keep.shape
            send, self.mine = self.line.call(
                over_shard_kernel,
                [self.keep, self.came],
                [((2, rows // 4, width), BF16)] * 2,
                name="over_shard",
            )
            self.moving = swap(send, "ctx", 1)

    def near(self):
        if self.pair:
            shape = self.mine.shape[1:]
            send, self.keep = self.line.call(
                near_kernel, [self.mine, self.moving], [(shape, BF16), (shape, F32)], name="near"
            )
            self.moving = swap(send, "ctx", 2)

    def far(self):
        if self.pair:
            (self.q0,) = self.line.call(
                far_kernel, [self.keep, self.moving], [(self.keep.shape, BF16)], name="far"
            )
            self.q2, self.q1 = swap(self.q0, "ctx", 2), swap(self.q0, "ctx", 1)

    def last(self):
        if self.pair:
            self.q2 = self.line.after(self.q2)
            self.q3 = swap(self.q2, "ctx", 1)

    def settled(self):
        if self.pair:
            self.q1, self.q3 = self.line.after(self.q1, self.q3)

    def placed(self):
        if not self.pair:
            if self.proj is None:
                return [self.summed(self.send, self.keep, self.dim)]
            width = self.keep.shape[1] // 4 * 3
            total = self.summed(self.send[:, :width], self.keep[:, :width], self.dim)
            return [*jnp.split(total, 3, axis=1), self.summed(*self.proj, 1)]
        rows, width = self.shape
        outs, kernel = [((rows, width), F32)], place_kernel
        if self.proj is not None:
            outs = [((rows, width // 4), F32)] * 3 + [(self.proj[1].shape, F32)]
            kernel = place_two_kernel
        return self.line.call(kernel, [self.q0, self.q1, self.q2, self.q3], outs, name="place")


def per_device(
    prompt_x,
    cont_x,
    owner,
    w_query,
    w_key,
    w_value,
    w_out,
    w_up,
    w_down,
    ln_gain,
    ln_bias,
    prompt_grad,
    cont_grad,
):
    shards = lax.axis_size("shard")
    groups, block, width = prompt_x.shape
    conts, cont_len, _ = cont_x.shape
    local = w_query.shape[1]
    hidden = w_up.shape[1]
    rows = groups * block
    own = rows // 2
    piece = own // 2
    part = width // 2
    prompt_len = block * lax.axis_size("ctx")
    core = lax.axis_index("tp") % 2
    bit = lax.axis_index("tp") // 2
    shard = lax.axis_index("shard")
    ctx = lax.axis_index("ctx")
    xs = (prompt_x.reshape(rows, width), cont_x.reshape(rows, width))
    dys = (prompt_grad.reshape(rows, width), cont_grad.reshape(rows, width))

    def both(weight, dim):
        if shards == 2:
            return weight, swap(weight, "shard", 1)
        full = lax.all_gather(weight, "shard", axis=dim, tiled=True)
        return tuple(jnp.split(full, 2, axis=dim))

    half = shard if shards == 2 else jnp.zeros_like(shard)
    which = (owner - shard * groups).reshape(2, conts // 2)
    which = jnp.where(core == 1, which[::-1], which) ^ core
    idx = jnp.concatenate([jnp.stack([core, half, ctx]), which.reshape(conts), jnp.stack([bit])])
    line = Line(idx.astype(jnp.int32))

    small = both(jnp.concatenate([ln_gain, ln_bias], axis=0), 1)
    (gb,) = line.call(gains_kernel, list(small), [((8, width), F32)], name="gains")
    packed = jnp.concatenate([w_key, w_value, w_query], axis=1)
    if shards == 2:
        (packed,) = line.call(
            pack_kernel, [w_key, w_value, w_query], [((part, 3 * local), BF16)], name="pack"
        )
    wqkv = both(packed, 0)
    quarter = lax.dynamic_slice_in_dim(xs[0], core * own + bit * piece, piece, 0)
    far, near = swap(quarter, "ctx", 2), swap(quarter, "ctx", 1)
    tables = rope_tables(prompt_len + cont_len)

    wo = both(line.after(w_out), 1)
    n1p, n1c = (
        line.call(normed_kernel, [x, gb], [((rows, width), BF16)], name="norm_first")[0] for x in xs
    )
    if shards == 2:
        (hidden_packed,) = line.call(
            pack_hidden_kernel, [w_up, w_down], [((2, part, hidden), BF16)], name="pack_hidden"
        )
    wide_rows = (rows, local)
    raw = pltpu.VMEM(wide_rows, F32)
    chunks = []
    for prompt in (True, False):
        chunks += line.call(
            functools.partial(qkv_kernel, prompt),
            [n1p if prompt else n1c, *wqkv, tables],
            [((3, *wide_rows), BF16)],
            [raw],
            name="qkv_prompt" if prompt else "qkv_cont",
        )
        if prompt:
            (normed,) = line.call(norm_pieces_kernel, [near, far, gb], [((own, width), BF16)], name="norm_pieces")
            both_near = [normed, swap(normed, "tp", 2)]
            far, *wo = line.after(far, *wo)
            last_near = swap(far, "ctx", 1)
            if shards == 2:
                hidden_packed = swap(line.after(hidden_packed), "shard", 1)
    kvq_p, kvq_c = chunks
    both_near.append(swap(line.after(normed), "tp", 1))
    (normed,) = line.call(norm_pieces_kernel, [last_near, gb], [((piece, width), BF16)], name="norm_piece")
    one_near = [normed, swap(normed, "tp", 2), swap(normed, "tp", 1)]
    both_near[1] = line.after(both_near[1])
    both_near.append(swap(both_near[1], "tp", 1))
    seen, far_normed = [kvq_p], []

    def far_keys(blocks, parts):
        seen.extend(
            line.call(
                functools.partial(kv_kernel, blocks),
                [*parts, *wqkv, tables],
                [((2 * len(blocks), *wide_rows), BF16), ((len(blocks), rows, width), BF16, "far")],
                [raw],
                name="far_keys",
            )
        )
        far_normed.append(seen.pop())

    far_keys((1, 2), both_near)
    (wo0,) = line.call(stack_kernel, wo, [((2, *wo[0].shape), BF16)], name="stack_out")
    wo0 = line.after(wo0)
    wo2, wo1 = swap(wo0, "tp", 2), swap(wo0, "tp", 1)
    one_near[1] = line.after(one_near[1])
    one_near.append(swap(one_near[1], "tp", 1))
    far_keys((3,), one_near)

    half_o = ((own, local), BF16)
    o_oth_p, o_own_p, probs_p = line.call(
        prompt_kernel,
        seen,
        [half_o, half_o, ((2, local // HEAD, prompt_len, own), BF16, "far")],
        [pltpu.VMEM((local, prompt_len), BF16), pltpu.VMEM((local, own), F32)],
        name="attend_prompt",
    )
    wo1, wo2 = line.after(wo1, wo2)
    wo3 = swap(wo2, "tp", 1)
    pairs = local // HEAD // 2
    mixed = [(o_own_p, o_oth_p)]

    def gathered(o_own, o_oth):
        return o_own, swap(o_oth, "tp", 1), swap(o_own, "tp", 2), swap(o_oth, "tp", 3)

    full_o = [gathered(o_own_p, o_oth_p)]
    all_len = prompt_len + cont_len
    o_oth_c, o_own_c, probs_c = line.call(
        cont_kernel,
        [kvq_c, *seen],
        [half_o, half_o, ((conts, pairs, all_len, 2 * cont_len), BF16, "far")],
        [pltpu.VMEM((local, all_len), BF16), pltpu.VMEM((local, cont_len), F32)],
        name="attend_cont",
    )
    mixed.append((o_own_c, o_oth_c))
    full_o.append(gathered(o_own_c, o_oth_c))

    if shards == 2:
        others = line.call(
            unpack_hidden_kernel, [hidden_packed], [(w_up.shape, BF16), (w_down.shape, BF16)], name="unpack_hidden"
        )
        wu, wd = (w_up, others[0]), (w_down, others[1])
    else:
        wu, wd = both(w_up, 0), both(w_down, 1)

    def mine(value):
        return Part(value, own, lambda idx: idx[0] * own)

    own_rows, own_rows_f = ((own, width), BF16), ((own, width), F32)
    own_pieces = (*own_rows, "cut")

    def swapped(pieces):
        return [swap(piece, "tp", 1) for piece in pieces]

    def summed(keep, send):
        came = swapped(send)
        (total,) = line.call(sum_kernel, [keep, came], [own_rows], name="sum_cores")
        return total, swap(total, "tp", 2)

    stage = []
    for x, os in zip(xs, full_o):
        n3, z, x1 = line.call(
            after_kernel,
            [wo0, os[0], wo1, os[1], wo2, os[2], wo3, os[3], mine(x), gb],
            [own_pieces, own_rows_f, own_rows_f],
            name="after_attention",
        )
        n3t = swapped(n3)
        send, act, slope, keep = line.call(
            up_down_kernel,
            [n3, *wu, n3t, *wd],
            [own_pieces, ((rows, hidden), BF16), ((rows, hidden), BF16), own_rows_f],
            name="up_down",
        )
        stage.append((z, x1, n3, n3t, act, slope, *summed(keep, send)))

    later = []
    for i, dy in enumerate(dys):
        z, x1, n3, n3t, act, slope, total, theirs = stage[i]
        dm, y, grads_last = line.call(
            last_kernel,
            [total, theirs, x1, mine(dy), gb],
            [own_pieces, own_rows, ((2, width), F32)],
            name="last_norm",
        )
        dmt = swapped(dm)
        send, du, keep = line.call(
            down_up_kernel,
            [dm, *wd, slope, dmt, *wu],
            [own_pieces, ((rows, hidden), BF16), own_rows_f],
            name="down_up",
        )
        later.append((y, dm, dmt, du, *summed(keep, send), grads_last))

    middle = []

    def middle_norms(i):
        z, x1 = stage[i][:2]
        total, theirs = later[i][4:6]
        dz, dx1, grads_middle = line.call(
            middle_kernel,
            [total, theirs, x1, mine(dys[i]), gb, z],
            [own_pieces, own_rows_f, ((4, width), F32)],
            name="middle_norms",
        )
        middle.append((dx1, dz, swapped(dz), grads_middle))

    y_p, y_c = later[0][0], later[1][0]

    def assembled(*pairs):
        return line.call(
            whole_kernel,
            [value for pair in pairs for value in pair],
            [((rows, width), BF16)] * len(pairs),
            name="whole",
        )

    middle_norms(0)
    send, keep = line.call(
        grad_down_kernel,
        [stage[0][4], stage[1][4], *later[0][1:3], *later[1][1:3]],
        [((hidden, part), BF16)] * 2,
        name="grad_down",
    )
    down = Reduction(line, send, keep, 1)
    down.start()
    y_p, y_c = line.after(y_p, y_c)
    y_others = [swap(value, "tp", 1) for value in (y_p, y_c)]
    pair_rows = (2, *wide_rows)
    grads, dqp, grad_out = line.call(
        prompt_back_kernel,
        [*middle[0][1:3], *[Far(a) for a in (wo0, *seen, probs_p)], tables, *[Far(o) for o in mixed[0]]],
        [((4, *pair_rows), F32, "far"), (wide_rows, BF16), ((local, width), F32, "far")],
        [
            pltpu.VMEM(wide_rows, BF16),
            pltpu.VMEM((local, prompt_len), BF16),
            pltpu.VMEM((local, own), F32),
            pltpu.VMEM((local // HEAD, prompt_len, own), BF16),
        ],
        name="attend_prompt_back",
    )
    y_others = line.after(*y_others)
    send, keep = line.call(
        grad_up_kernel,
        [*stage[0][2:4], *stage[1][2:4], later[0][3], later[1][3]],
        [((part, hidden), BF16)] * 2,
        name="grad_up",
    )
    middle_norms(1)
    down.over_shard()
    up = Reduction(line, send, keep, 0)
    up.start()
    send_out, keep_out, dkvq_c, dkv_p = line.call(
        cont_back_kernel,
        [*middle[1][1:3], *[Far(a) for a in (wo0, kvq_c, *seen, probs_c, grads)], tables]
        + [*[Far(o) for o in mixed[1]], Far(grad_out)],
        [((local, part), BF16)] * 2 + [((3, *wide_rows), BF16), ((4, *pair_rows), BF16)],
        [
            pltpu.VMEM(wide_rows, BF16),
            pltpu.VMEM((local, all_len), BF16),
            pltpu.VMEM((local, cont_len), F32),
            pltpu.VMEM((pairs, all_len, 2 * cont_len), BF16),
        ],
        name="attend_cont_back",
    )
    down.near()

    def blocks_input(first):
        return line.call(
            functools.partial(blocks_input_kernel, first),
            [dkv_p, Far(dqp), *[Far(w) for w in wqkv]],
            [own_rows] * 2 + [((2, own, width), F32)],
            name="input_blocks",
        )

    def blocks_cores(keep, came):
        send, mine = line.call(
            blocks_cores_kernel,
            [keep, *came],
            [((2, piece, width), BF16), ((2, piece, width), F32)],
            name="blocks_cores",
        )
        return mine, swap(send, "tp", 2)

    *sent, keep_a = blocks_input(0)
    came_a = swapped(sent)
    send, keep = line.call(
        grad_qkv_kernel,
        [dkv_p, Far(dqp), dkvq_c, send_out, keep_out, *[Far(a) for a in (n1p, n1c, *far_normed)]],
        [((part, 4 * local), BF16)] * 2,
        name="grad_qkv",
    )
    qkv = Reduction(line, send, keep, 0, (send_out, keep_out))
    *sent, keep_b = blocks_input(2)
    down.far()
    came_b = swapped(line.after(*sent))
    qkv.start()
    tp_a = blocks_cores(keep_a, came_a)
    up.over_shard()
    tp_b = blocks_cores(keep_b, came_b)
    send_c, keep_c = line.call(
        input_kernel, [dkvq_c, *[Far(w) for w in wqkv]], [own_pieces, own_rows_f], name="input_back"
    )
    yp, yc = assembled((y_p, y_others[0]), (y_c, y_others[1]))
    up.near()
    down.last()
    qkv.over_shard()
    totals_c = summed(keep_c, line.after(*send_c))
    three, one, own_two = line.call(
        blocks_tp_kernel,
        [*tp_a, *tp_b],
        [((piece, width), BF16)] * 2 + [((2, piece, width), F32)],
        name="blocks_tp",
    )
    three, one = swap(three, "ctx", 1), swap(one, "ctx", 1)
    up.far()
    (two,) = line.call(two_kernel, [own_two, three], [((piece, width), BF16)], name="blocks_two")
    two = swap(two, "ctx", 2)
    qkv.near()
    dxc, first_c = line.call(
        first_kernel,
        [*totals_c, mine(xs[1]), gb, Far(middle[1][0])],
        [own_rows, ((2, width), F32)],
        name="first_norm",
    )
    up.last()
    (grad_down,) = down.placed()
    qkv.far()
    dxp, first_p = line.call(
        first_prompt_kernel,
        [
            own_two,
            one,
            two,
            Part(xs[0], piece, lambda idx: idx[0] * own + idx[7] * piece),
            gb,
            Part(middle[0][0], piece, lambda idx: idx[7] * piece),
        ],
        [((piece, width), BF16), ((2, width), F32)],
        name="first_norm_prompt",
    )
    first_other, dxp_across = swap(first_p, "tp", 2), swap(dxp, "tp", 2)
    up.settled()
    first_p = first_p + line.after(first_other)
    (small,) = line.call(
        small_kernel,
        [first_c, first_p, middle[0][3], middle[1][3], later[0][6], later[1][6]],
        [((8, width), F32)],
        name="small",
    )
    small = small + swap(small, "tp", 1)
    qkv.last()
    dxp_across, small = line.after(dxp_across, small)
    dxp_parts = [dxp, dxp_across, swap(dxp, "tp", 1), swap(dxp_across, "tp", 1)]
    if shards == 2:
        small = lax.dynamic_slice_in_dim(small, shard * part, part, 1) + swap(
            lax.dynamic_slice_in_dim(small, (1 - shard) * part, part, 1), "shard", 1
        )
    else:
        small = lax.psum_scatter(small, "shard", scatter_dimension=1, tiled=True)
    dxc = line.after(dxc)
    dxc_other = swap(dxc, "tp", 1)
    (grad_up,) = up.placed()
    (dxc,) = assembled((dxc, dxc_other))
    small = line.after(small)
    small = small + swap(small, "ctx", 1)
    (dxp,) = line.call(whole_quarters_kernel, dxp_parts, [((rows, width), BF16)], name="whole_prompt")
    qkv.settled()
    small = line.after(small)
    small = small + swap(small, "ctx", 2)
    grad_key, grad_value, grad_query, grad_out = qkv.placed()
    return (
        yp.reshape(prompt_x.shape),
        yc.reshape(cont_x.shape),
        dxp.reshape(prompt_x.shape),
        dxc.reshape(cont_x.shape),
        grad_query,
        grad_key,
        grad_value,
        grad_out,
        grad_up,
        grad_down,
        small[:4],
        small[4:],
    )


def solution(mesh):
    placed = (
        P("shard", "ctx", None),
        P(("shard", "ctx"), None, None),
        P(("shard", "ctx")),
        P("shard", "tp"),
        P("shard", "tp"),
        P("shard", "tp"),
        P("tp", "shard"),
        P("shard", "tp"),
        P("tp", "shard"),
        P(None, "shard"),
        P(None, "shard"),
        P("shard", "ctx", None),
        P(("shard", "ctx"), None, None),
    )
    rows = (P("shard", "ctx", None), P(("shard", "ctx"), None, None))
    return jax.shard_map(
        per_device,
        mesh=mesh,
        in_specs=placed,
        out_specs=rows + rows + placed[3:11],
        check_vma=False,
    )
```
